32 devices in a mesh: ctx: 8 (over y, x, core), tp: 4 (over z).
Axes of the slice: x: 2, y: 2, z: 4, core: 2. Of those that a mesh axis runs over, the one named last changes fastest.
Arguments:
- inputs: bfloat16 [512, 2, 2048], P('ctx'), may hold values from -6 to 6
- attn_gain: bfloat16 [2048], P('ctx'), may hold values from 0.5 to 1.5
- w_query: bfloat16 [2048, 2048], P('ctx', 'tp'), may hold values from -0.125 to 0.125
- w_key: bfloat16 [2048, 2048], P('ctx', 'tp'), may hold values from -0.125 to 0.125
- w_value: bfloat16 [2048, 2048], P('ctx', 'tp'), may hold values from -0.125 to 0.125
- query_gain: bfloat16 [128], replicated, may hold values from 0.5 to 1.5
- key_gain: bfloat16 [128], replicated, may hold values from 0.5 to 1.5
- w_out: bfloat16 [2048, 2048], P('tp', 'ctx'), may hold values from -1.75 to 1.75
- ffn_gain: bfloat16 [2048], P('ctx'), may hold values from 0.5 to 1.5
- w_router: bfloat16 [2048, 16], P('ctx'), may hold values from -0.0625 to 0.0625
- w_gate: bfloat16 [16, 2048, 1024], P(None, 'ctx', 'tp'), may hold values from -0.125 to 0.125
- w_up: bfloat16 [16, 2048, 1024], P(None, 'ctx', 'tp'), may hold values from -0.125 to 0.125
- w_down: bfloat16 [16, 1024, 2048], P(None, 'tp', 'ctx'), may hold values from -1 to 1
- routes: int32 [512, 2, 8], P('ctx'), may hold values from 0 to 15, all different within a row; in each aligned block of 128 rows (0 to 127, 128 to 255, ..., all dimensions but the last counted through in order) at most 88 rows name the same one
- cotangent: bfloat16 [512, 2, 2048], P('ctx'), may hold values from -6 to 6
Outputs:
- output: bfloat16 [512, 2, 2048], P('ctx')
- input_grad: float32 [512, 2, 2048], P('ctx')
- attn_gain_grad: float32 [2048], P('ctx')
- query_weight_grad: float32 [2048, 2048], P('ctx', 'tp')
- key_weight_grad: float32 [2048, 2048], P('ctx', 'tp')
- value_weight_grad: float32 [2048, 2048], P('ctx', 'tp')
- query_gain_grad: float32 [128], replicated
- key_gain_grad: float32 [128], replicated
- out_weight_grad: float32 [2048, 2048], P('tp', 'ctx')
- ffn_gain_grad: float32 [2048], P('ctx')
- router_grad: float32 [2048, 16], P('ctx')
- gate_weight_grad: float32 [16, 2048, 1024], P(None, 'ctx', 'tp')
- up_weight_grad: float32 [16, 2048, 1024], P(None, 'ctx', 'tp')
- down_weight_grad: float32 [16, 1024, 2048], P(None, 'tp', 'ctx')
The draws below stay inside these ranges and needn't reach their ends.
Inputs may be any that keep to these rules, and one draw needn't show every extreme that they name: `routes`: each token names 8 different experts. Among the rows of one device (64 positions of all 2 sequences, an aligned block of the rows in order) no expert is named more than 88 times, and in some device's rows some expert is named exactly 88 times.
All inputs are finite; a program needn't handle non-finite values.
Results may differ from the reference program's by a relative error of at most 0.029.
Values may be sent and summed in bfloat16 or wider, within the bound.
No kernel may reach another device: no remote copies, remote signals or barrier semaphores. Data moves between devices by JAX's collectives and lax.ppermute only.
A program may use at most 256 MiB of HBM per device.

```python
import math
from functools import partial
import jax
import jax.numpy as jnp
import numpy as np
from jax import lax

D = 2048
H = 16
HD = 128
FF = 1024
TOP = 8
EXPERTS = 16
SEQS = 2
SEQ_DEV = 64
MOST = 88
LEN = 512
N_CTX = 8


def levels(stream_key, shape, pieces, smallest, largest):
    def one(dim, blocks):
        heights = jax.random.uniform(jax.random.fold_in(jax.random.fold_in(stream_key, 6), dim), (blocks,), jnp.float32, smallest / len(pieces), largest / len(pieces))
        return jnp.repeat(jnp.exp(heights), shape[dim] // blocks).reshape((-1,) + (1,) * (len(shape) - dim - 1))

    loudness = one(*pieces[0])
    for cut in pieces[1:]:
        loudness = loudness * one(*cut)
    return loudness


def shared_out(stream_key, own, number, rows, count, top, bound, lean):
    ranking = jax.random.permutation(stream_key, count)
    heavy_load, ordinary = portions_of(count, rows * top, bound, lean, True), portions_of(count, rows * top, bound, lean, False)
    places = jnp.arange(count)

    def named(sizes, rotation):
        used = int((sizes > 0).sum())
        fixed = max(1, used // 4)
        moved = fixed + (places - fixed + rotation * (used - fixed)) % max(1, count - fixed)
        return jnp.zeros((count,), jnp.int32).at[ranking[jnp.where(places < fixed, places, moved)]].set(jnp.asarray(sizes, jnp.int32))

    sizes = jnp.where(number % 4 == 0, named(heavy_load, number // 4), named(ordinary, number - number // 4 - 1))
    mixed = jax.random.permutation(jax.random.fold_in(own, 3), count)
    donor, taker = mixed[0:count // 2 * 2:2], mixed[1:count // 2 * 2:2]
    room = jnp.minimum(sizes[donor] - 1, bound - sizes[taker]) // 2
    room = jnp.where((donor == ranking[0]) | (taker == ranking[0]) | (sizes[taker] == 0), 0, jnp.maximum(room, 0))
    moved = jax.random.randint(jax.random.fold_in(own, 4), (count // 2,), 0, 1 << 20) % (room + 1)
    sizes = sizes.at[donor].add(-moved).at[taker].add(moved)
    items = jnp.searchsorted(jnp.cumsum(sizes), jnp.arange(rows * top), side="right").astype(jnp.int32)
    table = items.reshape(top, rows).T
    table = table[jax.random.permutation(jax.random.fold_in(own, 1), rows)]
    rotation = jax.random.randint(jax.random.fold_in(own, 2), (rows, 1), 0, top)
    return jnp.take_along_axis(table, (jnp.arange(top)[None, :] + rotation) % top, axis=1)


def portions_of(count, total, bound, lean, full):
    loads = [(1 << 20) // math.isqrt(standing ** lean) + 1 for standing in range(1, count + 1)]
    largest = bound if full else min(bound, max(-(-total // count), total * loads[0] // sum(loads)))
    least = 1 if total - largest >= count - 1 else 0
    given, spare = [largest] + [least] * (count - 1), total - largest - least * (count - 1)
    while spare > 0:
        free = [i for i in range(1, count) if given[i] < largest] or [i for i in range(1, count) if given[i] < bound]
        mass, budget = sum([loads[i] for i in free]), spare
        for i in free:
            addition = min(bound - given[i], max(1, budget * loads[i] // mass), spare)
            given[i] = given[i] + addition
            spare = spare - addition
    return np.array(given)


def centred(rng, shape, spread, bound, shards=(), held_as=jnp.bfloat16):
    values = jax.random.normal(rng, shape, jnp.float32) * spread
    if len(shards) > 0:
        values = levels(rng, shape, shards, -0.22, 0.18) * values
    return jnp.clip(values, min=-bound, max=bound).astype(held_as)


def setup_inputs(seed: int = 0) -> dict:
    arg_keys = jax.random.split(jax.random.key(seed), 16)
    inputs = centred(arg_keys[0], (LEN, SEQS, D), 1.0, 6.0, ((0, 8),))
    attn_gain = jnp.clip(1.0 + 0.1 * jax.random.normal(arg_keys[1], (D,), jnp.float32), 0.5, 1.5).astype(jnp.bfloat16)
    w_query = centred(arg_keys[2], (D, H * HD), D ** -0.5, 0.125, ((0, 8), (1, 4)))
    w_key = centred(arg_keys[3], (D, H * HD), D ** -0.5, 0.125, ((0, 8), (1, 4)))
    w_value = centred(arg_keys[4], (D, H * HD), D ** -0.5, 0.125, ((0, 8), (1, 4)))
    query_gain = jnp.clip(1.0 + 0.1 * jax.random.normal(arg_keys[5], (HD,), jnp.float32), 0.5, 1.5).astype(jnp.bfloat16)
    key_gain = jnp.clip(1.0 + 0.1 * jax.random.normal(arg_keys[6], (HD,), jnp.float32), 0.5, 1.5).astype(jnp.bfloat16)
    w_out = centred(arg_keys[7], (H * HD, D), (max(3 * H * HD // LEN, 1)) ** -0.5, 1.75, ((0, 4), (1, 8)))
    ffn_gain = jnp.clip(1.0 + 0.1 * jax.random.normal(arg_keys[8], (D,), jnp.float32), 0.5, 1.5).astype(jnp.bfloat16)
    w_router = centred(arg_keys[9], (D, EXPERTS), (4 * D) ** -0.5, 0.0625, ((0, 8),))
    w_gate = centred(arg_keys[10], (EXPERTS, D, FF), D ** -0.5, 0.125, ((1, 8), (2, 4)))
    w_up = centred(arg_keys[11], (EXPERTS, D, FF), D ** -0.5, 0.125, ((1, 8), (2, 4)))
    w_down = centred(arg_keys[12], (EXPERTS, FF, D), (max(FF // 32, 1)) ** -0.5, 1.0, ((1, 4), (2, 8)))
    routes_keys = jax.random.split(jax.random.fold_in(arg_keys[13], 1), LEN * SEQS // (SEQ_DEV * SEQS))
    routes_turns = jax.random.permutation(jax.random.fold_in(arg_keys[13], 3), LEN * SEQS // (SEQ_DEV * SEQS))
    routes = jax.vmap(lambda own, number: shared_out(jax.random.fold_in(arg_keys[13], 2), own, number, SEQ_DEV * SEQS, EXPERTS, TOP, MOST, 1))(routes_keys, routes_turns).reshape((LEN, SEQS, TOP))
    cotangent = centred(arg_keys[14], (LEN, SEQS, D), 1.0, 6.0, ((0, 8),))
    return dict(inputs=inputs, attn_gain=attn_gain, w_query=w_query, w_key=w_key, w_value=w_value, query_gain=query_gain, key_gain=key_gain, w_out=w_out, ffn_gain=ffn_gain, w_router=w_router, w_gate=w_gate, w_up=w_up, w_down=w_down, routes=routes, cotangent=cotangent)


EPSILON = 1e-06
THETA = 50000.0
PRECISE = lax.Precision.HIGHEST

@jax.custom_vjp
def low(v):
    return lax.optimization_barrier(v.astype(jnp.bfloat16)).astype(jnp.float32)

@jax.custom_vjp
def low_back(v):
    return v

def low_keep(v):
    return (low(v), None)

def low_pass(kept, grad):
    return (grad,)

def back_keep(v):
    return (v, None)

def back_low(kept, grad):
    return (low(grad),)
low.defvjp(low_keep, low_pass)
low_back.defvjp(back_keep, back_low)

def normalize(values, gain_values):
    return values * lax.rsqrt(lax.optimization_barrier(jnp.mean(values * values, -1, keepdims=True)) + EPSILON) * gain_values

def rotate(values, positions):
    half_width = values.shape[-1] // 2
    frequency = THETA ** (-(jnp.arange(half_width, dtype=jnp.float32) * 2.0) / values.shape[-1])
    angles = positions[:, None] * frequency[None, :]
    cosine = jnp.cos(angles)[:, None, None, :]
    sine_part = jnp.sin(angles)[:, None, None, :]
    first_half = values[..., :half_width]
    second_half = values[..., half_width:]
    return jnp.concatenate([first_half * cosine - second_half * sine_part, second_half * cosine + first_half * sine_part], -1)

def head_prep(projected, gain_values, positions):
    row_count, seq_count, columns = projected.shape
    head_dim = gain_values.shape[0]
    shaped = projected.reshape(row_count, seq_count, columns // head_dim, head_dim)
    return rotate(normalize(shaped, gain_values), positions)

def head_attention(queries, keys_all, values_all):
    scores = low_back(jnp.dot(queries, keys_all.T, precision=PRECISE) / math.sqrt(queries.shape[-1]))
    top_score = lax.optimization_barrier(jnp.max(scores, -1, keepdims=True))
    weights = jnp.exp(scores - top_score)
    weights = low(weights / lax.optimization_barrier(jnp.sum(weights, -1, keepdims=True)))
    return jnp.dot(weights, values_all, precision=PRECISE)

def attend_group(triple):
    return head_attention(triple[0], triple[1], triple[2])

def layer(slot_table, entry_index, hot_float, inputs, attn_gain, w_query, w_key, w_value, query_gain, key_gain, w_out, ffn_gain, w_router, w_gate, w_up, w_down):
    length = inputs.shape[0]
    seq_count = inputs.shape[1]
    positions = jnp.arange(length, dtype=jnp.float32)
    normed = low(normalize(inputs, attn_gain))
    queries = low(head_prep(low_back(jnp.dot(normed, w_query, precision=PRECISE)), query_gain, positions))
    keys_all = low(head_prep(low_back(jnp.dot(normed, w_key, precision=PRECISE)), key_gain, positions))
    values_all = low(low_back(jnp.dot(normed, w_value, precision=PRECISE))).reshape(length, seq_count, H, HD)
    grouped = tuple((member.transpose(1, 2, 0, 3).reshape(seq_count * H, length, HD) for member in (queries, keys_all, values_all)))
    mixed_heads = lax.map(jax.checkpoint(attend_group), grouped)
    mixed_heads = mixed_heads.reshape(seq_count, H, length, HD).transpose(2, 0, 1, 3).reshape(length, seq_count, H * HD)
    mixed_heads = low(low_back(mixed_heads))
    hidden_one = inputs + low_back(jnp.dot(mixed_heads, w_out, precision=PRECISE))
    normed_two = low(normalize(hidden_one, ffn_gain))
    flat_normed = normed_two.reshape(length * seq_count, D)
    logits = jnp.dot(flat_normed, w_router, precision=PRECISE)
    router_probs = jax.nn.softmax(logits, -1)
    gate_values = lax.optimization_barrier(jnp.sum(hot_float * router_probs[:, None, :], -1))
    dispatched = flat_normed[slot_table].reshape(EXPERTS, N_CTX * MOST, D)
    act_gate = low_back(jnp.einsum('ecd,edf->ecf', dispatched, w_gate, precision=PRECISE))
    act_up = low_back(jnp.einsum('ecd,edf->ecf', dispatched, w_up, precision=PRECISE))
    inner_act = low(jax.nn.silu(act_gate) * act_up)
    expert_out = low_back(jnp.einsum('ecf,efd->ecd', inner_act, w_down, precision=PRECISE))
    picked = expert_out.reshape(EXPERTS * N_CTX * MOST, D)[entry_index].reshape(length * seq_count, TOP, D)
    combined = lax.optimization_barrier(jnp.sum(gate_values[:, :, None] * picked, 1))
    return hidden_one + combined.reshape(length, seq_count, D)

def reference(inputs, attn_gain, w_query, w_key, w_value, query_gain, key_gain, w_out, ffn_gain, w_router, w_gate, w_up, w_down, routes, cotangent):
    token_count = LEN * SEQS
    flat_routes = routes.reshape(token_count * TOP).astype(jnp.int32)
    route_hot = (flat_routes[:, None] == jnp.arange(EXPERTS, dtype=jnp.int32)[None, :]).astype(jnp.int32)
    slot_number = lax.optimization_barrier(jnp.sum((jnp.cumsum(route_hot, 0, dtype=jnp.int32) - 1) * route_hot, 1, dtype=jnp.int32))
    entry_index = (flat_routes * (N_CTX * MOST) + slot_number).astype(jnp.int32)
    slot_table = jnp.zeros((EXPERTS * N_CTX * MOST,), jnp.int32).at[entry_index].set(jnp.arange(token_count * TOP, dtype=jnp.int32) // TOP)
    hot_float = route_hot.reshape(token_count, TOP, EXPERTS).astype(jnp.float32)
    floats = jax.tree.map(lambda member: member.astype(jnp.float32), (inputs, attn_gain, w_query, w_key, w_value, query_gain, key_gain, w_out, ffn_gain, w_router, w_gate, w_up, w_down))
    output, pullback = jax.vjp(partial(layer, slot_table, entry_index, hot_float), *floats)
    gradients = pullback(cotangent.astype(jnp.float32))
    return (output.astype(jnp.bfloat16), gradients[0], gradients[1], gradients[2], gradients[3], gradients[4], gradients[5], gradients[6], gradients[7], gradients[8], gradients[9], gradients[10], gradients[11], gradients[12])
```

```python
import functools
import math

import jax
import jax.numpy as jnp
from jax import lax
from jax.experimental import pallas as pl
from jax.experimental.pallas import tpu as pltpu
from jax.sharding import PartitionSpec as P

EPSILON = 1e-06
THETA = 50000.0
PRECISE = lax.Precision.HIGHEST
LOW = jnp.bfloat16
WIDE = jnp.float32
LANES = 128


def mul(equation, left, right):
    return jnp.einsum(equation, left, right, preferred_element_type=WIDE)


def dot(left, right, over):
    return lax.dot_general(left, right, (over, ((), ())), preferred_element_type=WIDE)


def inverse_rms(values):
    return lax.rsqrt(jnp.mean(values * values, -1, keepdims=True) + EPSILON)


def normalize(values, gain_values):
    return values * inverse_rms(values) * gain_values


def rotate(values, cosine, sine):
    half = values.shape[-1] // 2
    first, second = values[..., :half], values[..., half:]
    return jnp.concatenate([first * cosine - second * sine, second * cosine + first * sine], -1)


def tie(*values):
    return lax.optimization_barrier(values)


def trade(values, axis):
    return lax.all_to_all(values, axis, 0, 0, tiled=True)


def swap(values, axis, count, turn):
    return lax.ppermute(values, axis, [(i, i ^ turn) for i in range(count)])


def block_at(values, number, size, dim=0):
    return lax.dynamic_slice_in_dim(values, number * size, size, dim)


def sum_over_tp(values, count, rider=None):
    rows = values.shape[0] // count
    place = lax.axis_index("tp")
    values = values.astype(LOW)
    total = block_at(values, place, rows).astype(WIDE)
    for turn in range(1, count):
        total += swap(block_at(values, place ^ turn, rows), "tp", count, turn).astype(WIDE)
    total = total.astype(LOW)
    if rider is None:
        return lax.all_gather(total, "tp", axis=0, tiled=True)
    width = values.shape[1]
    rider_rows = -(-rider.size // (16 * width)) * 16
    rider = jnp.pad(rider.astype(LOW), (0, rider_rows * width - rider.size))
    both = jnp.concatenate([total, rider.reshape(rider_rows, width)], 0)
    both = lax.all_gather(both, "tp", axis=0)
    return both[:, :rows].reshape(count * rows, width), both[:, rows:].reshape(count, -1)


def attend(queries, keys, values, scale):
    scores = mul("xqd,xkd->xqk", queries, keys) * scale
    weights = jnp.exp(scores - jnp.max(scores, -1, keepdims=True))
    probs = weights / jnp.sum(weights, -1, keepdims=True)
    mixed = mul("xqk,xkd->xqd", probs.astype(LOW), values).astype(LOW)
    return probs, mixed


def attend_back(probs, mixed_grad, queries, keys, values, scale):
    values_grad = mul("xqk,xqd->xkd", probs.astype(LOW), mixed_grad)
    prob_grad = mul("xqd,xkd->xqk", mixed_grad, values)
    row_delta = jnp.sum(probs * prob_grad, -1, keepdims=True)
    score_grad = (probs * (prob_grad - row_delta)).astype(LOW)
    queries_grad = mul("xqk,xkd->xqd", score_grad, keys) * scale
    keys_grad = mul("xqk,xqd->xkd", score_grad, queries) * scale
    return queries_grad, keys_grad, values_grad


def pack_kernel(own_experts, place, *refs):
    weights, (*pieces, held, in_sems, out_sems) = refs[:3], refs[3:]
    arriving, leaving = [], []
    for turn, piece in enumerate(pieces):
        start = (place[0] ^ turn) * own_experts
        for kind, weight in enumerate(weights):
            source = weight.at[pl.ds(start, own_experts)]
            target = held.at[turn, pl.ds(kind * own_experts, own_experts)]
            arriving.append(pltpu.make_async_copy(source, target, in_sems.at[3 * turn + kind]))
        leaving.append(pltpu.make_async_copy(held.at[turn], piece, out_sems.at[turn]))
    for copy in arriving:
        copy.start()
    for turn, copy in enumerate(leaving):
        for part in arriving[3 * turn : 3 * turn + 3]:
            part.wait()
        copy.start()
    for copy in leaving:
        copy.wait()


def pack_experts(here, weights, count):
    experts, deep, wide = weights[0].shape
    own_experts = experts // count
    shape = (3 * own_experts, deep, wide)
    anywhere = pl.BlockSpec(memory_space=pl.ANY)
    return pl.pallas_call(
        functools.partial(pack_kernel, own_experts),
        grid_spec=pltpu.PrefetchScalarGridSpec(
            num_scalar_prefetch=1,
            grid=(1,),
            in_specs=[anywhere] * 3,
            out_specs=[anywhere] * count,
            scratch_shapes=[
                pltpu.VMEM((count,) + shape, LOW),
                pltpu.SemaphoreType.DMA((3 * count,)),
                pltpu.SemaphoreType.DMA((count,)),
            ],
        ),
        out_shape=[jax.ShapeDtypeStruct(shape, LOW)] * count,
        compiler_params=pltpu.CompilerParams(vmem_limit_bytes=24 * 2**20),
        cost_estimate=pl.CostEstimate(
            flops=0, bytes_accessed=2 * 2 * 3 * experts * deep * wide, transcendentals=0
        ),
    )(here.reshape(1), *weights)


def unpack_kernel(own_experts, turns, place, *refs):
    count = len(turns)
    pieces, (*outs, held, wide, in_sems, out_sems) = refs[:count], refs[-7:]
    arriving = [
        pltpu.make_async_copy(piece, held.at[i], in_sems.at[i]) for i, piece in enumerate(pieces)
    ]
    leaving = []
    for i, turn in enumerate(turns):
        target = pl.ds((place[0] ^ turn) * own_experts, own_experts)
        for kind, out in enumerate(outs):
            part = pl.ds(kind * own_experts, own_experts)
            leaving.append(
                pltpu.make_async_copy(
                    wide.at[i % 2, part], out.at[target], out_sems.at[3 * i + kind]
                )
            )
    for copy in arriving:
        copy.start()
    for i in range(count):
        arriving[i].wait()
        if i >= 2:
            for copy in leaving[3 * i - 6 : 3 * i - 3]:
                copy.wait()
        wide[i % 2] = held[i].astype(WIDE)
        for copy in leaving[3 * i : 3 * i + 3]:
            copy.start()
    for copy in leaving[-6:] if count > 1 else leaving:
        copy.wait()


def unpack_experts(here, pieces, turns, count, kept):
    blocks, deep, wide = pieces[0].shape
    own_experts = blocks // 3
    anywhere = pl.BlockSpec(memory_space=pl.ANY)
    aliases = {1 + len(turns) + i: i for i in range(3)} if kept else {}
    return pl.pallas_call(
        functools.partial(unpack_kernel, own_experts, turns),
        grid_spec=pltpu.PrefetchScalarGridSpec(
            num_scalar_prefetch=1,
            grid=(1,),
            in_specs=[anywhere] * (len(turns) + len(kept)),
            out_specs=[anywhere] * 3,
            scratch_shapes=[
                pltpu.VMEM((len(turns), blocks, deep, wide), LOW),
                pltpu.VMEM((2, blocks, deep, wide), WIDE),
                pltpu.SemaphoreType.DMA((len(turns),)),
                pltpu.SemaphoreType.DMA((3 * len(turns),)),
            ],
        ),
        out_shape=[jax.ShapeDtypeStruct((count * own_experts, deep, wide), WIDE)] * 3,
        input_output_aliases=aliases,
        compiler_params=pltpu.CompilerParams(vmem_limit_bytes=24 * 2**20),
        cost_estimate=pl.CostEstimate(
            flops=0, bytes_accessed=6 * len(turns) * blocks * deep * wide, transcendentals=0
        ),
    )(here.reshape(1), *pieces, *kept)


def expert_kernel(own_experts, count, sources, place, *refs):
    tokens, grads, refs = refs[:count], refs[count : 2 * count], refs[2 * count :]
    router, pieces = refs[0], refs[1 : 1 + sources]
    gated_out, act_out, *backs, probs_out, rise, fall, token, grad, sems = refs[1 + sources :]
    rows, width = tokens[0].shape
    width_here, hidden_here = pieces[0].shape[1:]
    own_hidden = own_experts * hidden_here
    here = place[0]
    rise_copies, fall_copies = [], []
    for source, piece in enumerate(pieces):
        start = pl.multiple_of((here ^ source) * width_here, width_here)
        deep = pl.ds(start, width_here)
        for own in range(own_experts):
            near = pl.ds(own * hidden_here, hidden_here)
            far = pl.ds(own_hidden + own * hidden_here, hidden_here)
            targets = (rise.at[deep, near], rise.at[deep, far], fall.at[near, deep])
            for kind, target in enumerate(targets):
                block = kind * own_experts + own
                sem = sems.at[3 * own_experts * source + block]
                copy = pltpu.make_async_copy(piece.at[block], target, sem)
                (fall_copies if kind == 2 else rise_copies).append(copy)
    for copy in rise_copies + fall_copies:
        copy.start()
    for i in range(count):
        part = pl.ds(i * rows, rows)
        token[part] = tokens[i][...]
        grad[part] = grads[i][...].reshape(rows, width + LANES)
    lane = lax.broadcasted_iota(jnp.int32, (2 * rows, LANES), 1)
    experts = sources * own_experts
    step = min(512, width)
    for pair in range(count // 2):
        part = pl.ds(2 * pair * rows, 2 * rows)
        logits = dot(token[part], router[...], ((1,), (1,)))
        logits = jnp.where(lane < experts, logits, -1e30)
        exp_logits = jnp.exp(logits - jnp.max(logits, -1, keepdims=True))
        probs = exp_logits / jnp.sum(exp_logits, -1, keepdims=True)
        if pair == 0:
            probs_out[...] = probs
        hot = grad[part, width : width + LANES].astype(WIDE)
        routed = probs * hot
        if pair == 0:
            for copy in rise_copies:
                copy.wait()
        placed = jnp.zeros((2 * rows, LANES), WIDE)
        for own in range(own_experts):
            near = pl.ds(own * hidden_here, hidden_here)
            far = pl.ds(own_hidden + own * hidden_here, hidden_here)
            mine = lane == here * own_experts + own
            gates = jnp.sum(jnp.where(mine, routed, 0.0), -1, keepdims=True)
            act_gate = dot(token[part], rise[:, near], ((1,), (0,)))
            act_up = dot(token[part], rise[:, far], ((1,), (0,)))
            if pair == 0 and own == 0:
                for copy in fall_copies:
                    copy.wait()
            pulled = dot(grad[part, :width], fall[near, :], ((1,), (1,)))
            sigmoid_gate = jax.nn.sigmoid(act_gate)
            silu = act_gate * sigmoid_gate
            inner = (silu * act_up).astype(LOW).astype(WIDE)
            gate_grads = jnp.sum(inner * pulled, -1, keepdims=True)
            placed = jnp.where(mine, gate_grads * hot, placed)
            gated_out[part, near] = (inner * gates).astype(LOW)
            inner_grad = pulled * gates
            gate_side = inner_grad * act_up * sigmoid_gate * (1.0 + act_gate * (1.0 - sigmoid_gate))
            act_out[part, near] = gate_side.astype(LOW)
            act_out[part, far] = (inner_grad * silu).astype(LOW)
        for start in range(0, width, step):
            columns = pl.ds(start, step)
            back = dot(act_out[part], rise[columns, :], ((1,), (1,))).astype(LOW)
            backs[2 * pair][:, columns] = back[:rows]
            backs[2 * pair + 1][:, columns] = back[rows:]
        backs[2 * pair][:, width:] = placed[:rows].astype(LOW)
        backs[2 * pair + 1][:, width:] = placed[rows:].astype(LOW)


def run_experts(turns, here, tokens, grad_hot, router, pieces):
    count = len(turns)
    rows, width = tokens[0].shape
    sources, own_experts = len(pieces), pieces[0].shape[0] // 3
    own_hidden = own_experts * pieces[0].shape[2]
    slices, _, slice_rows, _ = grad_hot.shape

    def whole(shape):
        return pl.BlockSpec(shape, lambda i, p: (0,) * len(shape))

    def grad_spec(turn):
        shape = (slices, 1, slice_rows, width + LANES)
        return pl.BlockSpec(shape, lambda i, p: (0, p[0] ^ turn, 0, 0))

    in_specs = [whole((rows, width))] * count
    in_specs += [grad_spec(turn) for turn in turns]
    in_specs += [whole((LANES, width))] + [pl.BlockSpec(memory_space=pl.ANY)] * sources
    shapes = [
        jax.ShapeDtypeStruct((count * rows, own_hidden), LOW),
        jax.ShapeDtypeStruct((count * rows, 2 * own_hidden), LOW),
        *[jax.ShapeDtypeStruct((rows, width + LANES), LOW)] * count,
        jax.ShapeDtypeStruct((2 * rows, LANES), WIDE),
    ]
    return pl.pallas_call(
        functools.partial(expert_kernel, own_experts, count, sources),
        grid_spec=pltpu.PrefetchScalarGridSpec(
            num_scalar_prefetch=1,
            grid=(1,),
            in_specs=in_specs,
            out_specs=[whole(shape.shape) for shape in shapes],
            scratch_shapes=[
                pltpu.VMEM((width, 2 * own_hidden), LOW),
                pltpu.VMEM((own_hidden, width), LOW),
                pltpu.VMEM((count * rows, width), LOW),
                pltpu.VMEM((count * rows, width + LANES), LOW),
                pltpu.SemaphoreType.DMA((3 * own_experts * sources,)),
            ],
        ),
        out_shape=shapes,
        compiler_params=pltpu.CompilerParams(vmem_limit_bytes=56 * 2**20),
        cost_estimate=pl.CostEstimate(
            flops=2 * count * rows * width * own_hidden * 5,
            bytes_accessed=2 * (3 * own_hidden * width + count * rows * width * 4),
            transcendentals=0,
        ),
    )(here.reshape(1), *tokens, *[grad_hot] * count, router, *pieces)


def mix_kernel(own_experts, sources, place, *refs):
    gated_near, gated_far, pieces = refs[0], refs[1], refs[2 : 2 + sources]
    out, fall, sems = refs[2 + sources :]
    width_here, hidden_here = pieces[0].shape[1:]
    rows = gated_near.shape[0] // 2
    step, here = pl.program_id(0), place[0]

    @pl.when(step == 0)
    def _():
        copies = []
        for source, piece in enumerate(pieces):
            start = pl.multiple_of((here ^ source) * width_here, width_here)
            for own in range(own_experts):
                target = fall.at[pl.ds(own * hidden_here, hidden_here), pl.ds(start, width_here)]
                sem = sems.at[own_experts * source + own]
                block = piece.at[2 * own_experts + own]
                copies.append(pltpu.make_async_copy(block, target, sem))
        for copy in copies:
            copy.start()
        for copy in copies:
            copy.wait()

    gated = jnp.where(step == 0, gated_near[...], gated_far[...])
    swapped = lax.rem(here, 2)
    first = pl.ds(pl.multiple_of(swapped * rows, rows), rows)
    second = pl.ds(pl.multiple_of((1 - swapped) * rows, rows), rows)
    mix = dot(gated, fall[...], ((1,), (0,))).astype(LOW)
    out[first] = mix[:rows]
    out[second] = mix[rows:]


def mix_experts(here, gated_parts, pieces):
    sources, own_experts = len(pieces), pieces[0].shape[0] // 3
    pair_rows, own_hidden = gated_parts[0].shape
    total = pair_rows * sources // 2
    width = sources * pieces[0].shape[1]
    return pl.pallas_call(
        functools.partial(mix_kernel, own_experts, sources),
        grid_spec=pltpu.PrefetchScalarGridSpec(
            num_scalar_prefetch=1,
            grid=(sources // 2,),
            in_specs=[
                pl.BlockSpec((pair_rows, own_hidden), lambda t, p: (0, 0)),
                pl.BlockSpec((pair_rows, own_hidden), lambda t, p: (jnp.maximum(t - 1, 0), 0)),
            ]
            + [pl.BlockSpec(memory_space=pl.ANY)] * sources,
            out_specs=pl.BlockSpec((pair_rows, width), lambda t, p: ((p[0] ^ (2 * t)) // 2, 0)),
            scratch_shapes=[
                pltpu.VMEM((own_hidden, width), LOW),
                pltpu.SemaphoreType.DMA((own_experts * sources,)),
            ],
        ),
        out_shape=jax.ShapeDtypeStruct((total, width), LOW),
        compiler_params=pltpu.CompilerParams(vmem_limit_bytes=56 * 2**20),
        cost_estimate=pl.CostEstimate(
            flops=2 * total * width * own_hidden,
            bytes_accessed=2 * (own_hidden * width + total * width),
            transcendentals=0,
        ),
    )(here.reshape(1), *gated_parts, *pieces)


def project_kernel(first_column, mixed, blocks, out_all, attended, sems):
    count, rows, _ = blocks.shape
    columns, width = out_all.shape
    width_here = width // count
    copies = []
    for source in range(count):
        for i in range(columns // rows):
            block = blocks.at[source, :, pl.ds(first_column + i * width_here, width_here)]
            target = out_all.at[pl.ds(i * rows, rows), pl.ds(source * width_here, width_here)]
            sem = sems.at[source * (columns // rows) + i]
            copies.append(pltpu.make_async_copy(block, target, sem))
    for copy in copies:
        copy.start()
    for copy in copies:
        copy.wait()
    attended[...] = dot(mixed[...], out_all[...], ((1,), (0,))).astype(LOW)


def project(mixed, blocks, first_column, width):
    rows, columns = mixed.shape
    count = blocks.shape[0]
    return pl.pallas_call(
        functools.partial(project_kernel, first_column),
        in_specs=[pl.BlockSpec(memory_space=pltpu.VMEM), pl.BlockSpec(memory_space=pl.ANY)],
        out_specs=[pl.BlockSpec(memory_space=pltpu.VMEM)] * 2,
        scratch_shapes=[pltpu.SemaphoreType.DMA((count * (columns // rows),))],
        out_shape=[
            jax.ShapeDtypeStruct((columns, width), LOW),
            jax.ShapeDtypeStruct((rows, width), LOW),
        ],
        compiler_params=pltpu.CompilerParams(vmem_limit_bytes=32 * 2**20),
        cost_estimate=pl.CostEstimate(
            flops=2 * rows * columns * width,
            bytes_accessed=2 * 2 * columns * width,
            transcendentals=0,
        ),
    )(mixed, blocks)


def join_kernel(seqs, heads, head_dim, moved, *outs):
    for i, out in enumerate(outs):
        part = slice(i * head_dim, (i + 1) * head_dim)
        for head in range(heads):
            total = moved[head, :, part].astype(WIDE)
            for seq in range(1, seqs):
                total += moved[seq * heads + head, :, part].astype(WIDE)
            out[:, head * head_dim : (head + 1) * head_dim] = total


def join_projections(moved, seqs, heads, head_dim):
    rows = moved.shape[1]
    shape = jax.ShapeDtypeStruct((rows, heads * head_dim), WIDE)
    return pl.pallas_call(
        functools.partial(join_kernel, seqs, heads, head_dim),
        out_shape=[shape] * 3,
        compiler_params=pltpu.CompilerParams(vmem_limit_bytes=32 * 2**20),
        cost_estimate=pl.CostEstimate(
            flops=0, bytes_accessed=2 * moved.size + 12 * rows * heads * head_dim, transcendentals=0
        ),
    )(moved)


def weight_grad_kernel(own_experts, count, place, *refs):
    tokens, grads = refs[:count], refs[count : 2 * count]
    act_parts, gated_parts = refs[2 * count : 2 * count + 2], refs[2 * count + 2 : 2 * count + 4]
    pieces, (token, grad, act, gated) = refs[2 * count + 4 : -4], refs[-4:]
    rows = tokens[0].shape[0]
    hidden_here = pieces[0].shape[2]
    split = 2 * rows

    @pl.when(pl.program_id(0) == 0)
    def _():
        for part, source in ((slice(0, split), 0), (slice(split, None), 1)):
            act[part] = act_parts[source][...]
            gated[:, part] = gated_parts[source][...].T

    for turn in range(count):
        part = pl.ds(turn * rows, rows)
        token[part] = tokens[turn][...]
        grad[part] = grads[turn][...].reshape(rows, grad.shape[1])
    rise = dot(token[...], act[...], ((0,), (0,))).astype(LOW)
    fall = dot(gated[...], grad[...], ((1,), (0,))).astype(LOW)
    for turn, piece in enumerate(pieces):

        @pl.when(pl.program_id(0) == turn)
        def _():
            for i in range(2 * own_experts):
                piece[i] = rise[:, i * hidden_here : (i + 1) * hidden_here]
            for i in range(own_experts):
                piece[2 * own_experts + i] = fall[i * hidden_here : (i + 1) * hidden_here]


def weight_grads(here, tokens, grad_hot, act_parts, gated_parts):
    count = len(tokens)
    rows, width = tokens[0].shape
    width_here = width // count
    own_hidden = gated_parts[0].shape[1]
    own_experts = own_hidden // width_here
    hidden_here = own_hidden // own_experts
    total = count * rows
    slices, _, slice_rows, _ = grad_hot.shape

    def grad_spec(turn):
        shape = (slices, 1, slice_rows, width_here)
        return pl.BlockSpec(shape, lambda t, p: (0, p[0] ^ turn, 0, p[0] ^ t))

    def whole(shape):
        return pl.BlockSpec(shape, lambda t, p: (0,) * len(shape))

    shape = (3 * own_experts, width_here, hidden_here)
    return pl.pallas_call(
        functools.partial(weight_grad_kernel, own_experts, count),
        grid_spec=pltpu.PrefetchScalarGridSpec(
            num_scalar_prefetch=1,
            grid=(count,),
            in_specs=[pl.BlockSpec((rows, width_here), lambda t, p: (0, p[0] ^ t))] * count
            + [grad_spec(turn) for turn in range(count)]
            + [whole(part.shape) for part in (*act_parts, *gated_parts)],
            out_specs=[whole(shape)] * count,
            scratch_shapes=[
                pltpu.VMEM((total, width_here), LOW),
                pltpu.VMEM((total, width_here), LOW),
                pltpu.VMEM((total, 2 * own_hidden), LOW),
                pltpu.VMEM((own_hidden, total), LOW),
            ],
        ),
        out_shape=[jax.ShapeDtypeStruct(shape, LOW)] * count,
        compiler_params=pltpu.CompilerParams(vmem_limit_bytes=56 * 2**20),
        cost_estimate=pl.CostEstimate(
            flops=2 * total * width * own_hidden * 3,
            bytes_accessed=2 * (3 * own_hidden * width + 2 * total * width),
            transcendentals=0,
        ),
    )(here.reshape(1), *tokens, *([grad_hot] * count), *act_parts, *gated_parts)


def per_device(
    inputs,
    attn_gain,
    w_query,
    w_key,
    w_value,
    query_gain,
    key_gain,
    w_out,
    ffn_gain,
    w_router,
    w_gate,
    w_up,
    w_down,
    routes,
    cotangent,
):
    here = lax.axis_index("ctx")
    shard_len, seqs, width = inputs.shape
    width_here = attn_gain.shape[0]
    ctx_count = width // width_here
    head_dim = query_gain.shape[0]
    columns = w_query.shape[1]
    heads = columns // head_dim
    experts, _, hidden_here = w_gate.shape
    own_experts = experts // ctx_count
    tp_count = lax.axis_size("tp")
    rows = seqs * shard_len
    units = seqs * heads
    length = ctx_count * shard_len
    scale = 1.0 / math.sqrt(head_dim)

    def by_sequence(values):
        return jnp.swapaxes(values, 0, 1).reshape((rows,) + values.shape[2:])

    def by_position(values):
        return jnp.swapaxes(values.reshape((seqs, shard_len) + values.shape[1:]), 0, 1)

    extra = jnp.concatenate([w_router.T, attn_gain[None, :], ffn_gain[None, :]], 0)
    extra = jnp.pad(extra, ((0, 32 - extra.shape[0]), (0, 0)))

    residual_in = by_sequence(inputs).astype(WIDE)
    grad_low = by_sequence(cotangent)
    frequency = THETA ** (-(jnp.arange(head_dim // 2, dtype=WIDE) * 2.0) / head_dim)
    query_scale, key_scale = query_gain.astype(WIDE), key_gain.astype(WIDE)

    def turned(positions):
        angles = positions.astype(WIDE)[:, None] * frequency
        cosine, sine = jnp.cos(angles), jnp.sin(angles)

        def prepare(values, gain_values):
            return rotate(normalize(values, gain_values), cosine, sine)

        return prepare

    def to_units(member):
        member = member.reshape(seqs, shard_len, heads, head_dim).transpose(0, 2, 1, 3)
        return trade(member.reshape(units, shard_len, head_dim), "ctx").reshape(length, head_dim)

    def from_units(member):
        moved = trade(member.reshape(ctx_count, shard_len, head_dim), "ctx")
        moved = moved.reshape(seqs, heads, shard_len, head_dim).transpose(0, 2, 1, 3)
        return moved.reshape(rows, columns)

    def attention_by_units(sent_pieces):
        sent = jnp.broadcast_to(
            jnp.swapaxes(inputs, 0, 1)[:, None], (seqs, heads, shard_len, width)
        )
        rider = extra.reshape(1, -1, width)
        rider_rows = rider.shape[1]
        rider = jnp.pad(rider, ((0, 0), (0, 8 - rider_rows), (0, 0)))
        rider = jnp.broadcast_to(rider, (units, 8, width))
        sent = jnp.concatenate([sent.reshape(units, shard_len, width), rider], 1)
        arrived = trade(sent, "ctx")
        cuts = [w.reshape(width_here, heads, head_dim) for w in (w_query, w_key, w_value)]
        sent = jnp.stack(cuts, 2).reshape(width_here, heads, 3 * head_dim)
        sent = jnp.broadcast_to(
            jnp.swapaxes(sent, 0, 1), (seqs, heads, width_here, 3 * head_dim)
        )
        *sent_pieces, grad_hot = sent_pieces
        sent, arrived, grad_hot, *sent_pieces = tie(
            sent.reshape(units, width_here, 3 * head_dim), arrived, grad_hot, *sent_pieces
        )
        unit_in = arrived[:, :shard_len].reshape(length, width)
        extra_all = arrived[:, shard_len : shard_len + rider_rows]
        extra_all = extra_all.reshape(ctx_count, 32, width_here)
        extra_all = jnp.swapaxes(extra_all, 0, 1).reshape(32, width)
        first_gain = extra_all[experts].astype(WIDE)
        unit_weights = trade(sent, "ctx")
        unit_weights = unit_weights.reshape(width, 3 * head_dim)
        unit_normed = normalize(unit_in.astype(WIDE), first_gain).astype(LOW)
        unit_normed, *sent_pieces = tie(unit_normed, *sent_pieces)
        sent_pieces.append(grad_hot)
        projected = jnp.dot(unit_normed, unit_weights, preferred_element_type=WIDE)
        prepare = turned(jnp.arange(length, dtype=jnp.int32))
        queries, query_pull = jax.vjp(prepare, projected[:, :head_dim], query_scale)
        keys, key_pull = jax.vjp(prepare, projected[:, head_dim : 2 * head_dim], key_scale)
        parts = [m.astype(LOW)[None] for m in (queries, keys, projected[:, 2 * head_dim :])]
        probs, unit_mixed = attend(*parts, scale)

        def back(mixed_grad, mix_part, grad_pieces):
            unit_grad = to_units(mixed_grad)[None]
            grads = attend_back(probs, unit_grad, *parts, scale)
            query_grad, query_gain_grad = query_pull(grads[0][0])
            key_grad, key_gain_grad = key_pull(grads[1][0])
            proj_grad = jnp.concatenate([query_grad, key_grad, grads[2][0]], 1).astype(LOW)
            part = dot(proj_grad, unit_weights, ((1,), (1,))).astype(LOW)
            part, mix_low = tie(part, mix_part)
            part = trade(part.reshape(ctx_count, shard_len, width), "ctx")
            mix_sum = sum_over_tp(mix_low, tp_count)
            part, mix_sum, grad_pieces[3], grad_pieces[5] = tie(
                part, mix_sum, grad_pieces[3], grad_pieces[5]
            )
            part = jnp.sum(part.reshape(seqs, heads, shard_len, width).astype(WIDE), 1)
            weight_grad = dot(unit_normed, proj_grad, ((0,), (0,))).astype(LOW)

            def owned(weight_grad):
                moved = trade(weight_grad.reshape(ctx_count, width_here, 3 * head_dim), "ctx")
                return moved

            part = part.reshape(rows, width)
            return part, mix_sum, (weight_grad, owned), query_gain_grad, key_gain_grad

        return unit_mixed[0], from_units, back, extra_all, sent_pieces

    def attention_by_tokens(sent_pieces):
        extra_all = jnp.swapaxes(lax.all_gather(extra, "ctx", axis=0), 0, 1).reshape(32, width)
        first_gain = extra_all[experts].astype(WIDE)
        packed = jnp.concatenate([w_query, w_key, w_value], 1)
        packed = lax.all_gather(packed, "ctx", axis=0, tiled=True)
        normed = normalize(residual_in, first_gain).astype(LOW)
        projected = jnp.dot(normed, packed, preferred_element_type=WIDE)
        positions = here * shard_len + jnp.arange(shard_len, dtype=jnp.int32)

        def heads_first(member):
            member = member.reshape(seqs, shard_len, heads, head_dim)
            return member.transpose(0, 2, 1, 3).reshape(units, shard_len, head_dim)

        def tokens_first(member):
            member = member.reshape(seqs, heads, shard_len, head_dim)
            return member.transpose(0, 2, 1, 3).reshape(rows, columns)

        prepare = turned(positions)
        cuts = [heads_first(projected[:, i * columns : (i + 1) * columns]) for i in range(3)]
        queries, query_pull = jax.vjp(prepare, cuts[0], query_scale)
        keys, key_pull = jax.vjp(prepare, cuts[1], key_scale)
        queries = queries.astype(LOW)
        pairs = jnp.concatenate([keys, cuts[2]], -1).astype(LOW)
        pairs = lax.all_gather(pairs, "ctx", axis=1, tiled=True)
        parts = [queries, pairs[..., :head_dim], pairs[..., head_dim:]]
        probs, mixed = attend(*parts, scale)

        def back(mixed_grad, mix_part, grad_pieces):
            grads = attend_back(probs, heads_first(mixed_grad), *parts, scale)
            moved = jnp.concatenate(grads[1:], -1).astype(LOW)
            moved = lax.psum_scatter(moved, "ctx", scatter_dimension=1, tiled=True).astype(WIDE)
            query_grad, query_gain_grad = query_pull(grads[0])
            key_grad, key_gain_grad = key_pull(moved[..., :head_dim])
            proj_grad = [tokens_first(g) for g in (query_grad, key_grad, moved[..., head_dim:])]
            proj_grad = jnp.concatenate(proj_grad, 1).astype(LOW)
            part = dot(proj_grad, packed, ((1,), (1,)))
            weight_grad = dot(normed, proj_grad, ((0,), (0,))).astype(LOW)

            def owned(weight_grad):
                moved = lax.psum_scatter(weight_grad, "ctx", scatter_dimension=0, tiled=True)
                return moved

            mix_sum = sum_over_tp(mix_part, tp_count)
            return part, mix_sum, (weight_grad, owned), query_gain_grad, key_gain_grad

        return mixed, tokens_first, back, extra_all, sent_pieces

    by_units = units == ctx_count
    expert_ids = jnp.arange(LANES, dtype=jnp.int32)
    hot = jnp.sum((by_sequence(routes)[:, :, None] == expert_ids).astype(WIDE), 1).astype(LOW)
    grad_hot = jnp.concatenate([grad_low, hot], 1)
    sent = pack_experts(here, (w_gate, w_up, w_down), ctx_count)
    local_mixed, to_tokens, attention_back, extra_all, (*sent, grad_hot) = (
        attention_by_units([*sent, grad_hot])
        if by_units
        else attention_by_tokens([*sent, grad_hot])
    )
    first_gain = extra_all[experts].astype(WIDE)
    second_gain = extra_all[experts + 1].astype(WIDE)
    router_rows = jnp.pad(extra_all[:experts], ((0, LANES - experts), (0, 0)))
    stack = columns // rows
    out_cut = jnp.swapaxes(w_out.reshape(stack, rows, width_here), 0, 1)
    out_cut = out_cut.reshape(rows, stack * width_here)
    out_blocks = lax.all_gather(out_cut, "ctx", axis=0)
    grad_hot = lax.all_gather(grad_hot, "ctx", axis=0)[None]

    pieces = [sent[0]] + [swap(sent[t], "ctx", ctx_count, t) for t in range(1, ctx_count)]
    local_mixed, pieces[1], pieces[2], pieces[4] = tie(
        local_mixed, pieces[1], pieces[2], pieces[4]
    )
    mixed = to_tokens(local_mixed)
    mixed, pieces[3], pieces[5] = tie(mixed, pieces[3], pieces[5])

    out_all, attended = project(mixed, out_blocks, 0, width)
    attended = sum_over_tp(attended, tp_count)
    attended, *pieces[6:] = tie(attended, *pieces[6:])
    hidden_one = residual_in + attended.astype(WIDE)
    normed_two = normalize(hidden_one, second_gain).astype(LOW)

    token_blocks = [normed_two, swap(normed_two, "ctx", ctx_count, 1)]
    token_blocks += [None] * (ctx_count - 2)
    for turn in range(2, ctx_count, 2):
        token_blocks[turn] = swap(normed_two, "ctx", ctx_count, turn)
    back_parts, gated_parts, act_parts = [], [], []
    for turns in (range(2), range(2, ctx_count)):
        blocks = [token_blocks[turn] for turn in turns]
        gated, act_grad, *backs, probs = run_experts(
            turns, here, blocks, grad_hot, router_rows, pieces
        )
        gated_parts.append(gated)
        act_parts.append(act_grad)
        if turns[0] == 0:
            probs, *token_blocks[2::2] = tie(probs, *token_blocks[2::2])
            for turn in range(2, ctx_count, 2):
                token_blocks[turn + 1] = swap(token_blocks[turn], "ctx", ctx_count, 1)
            router_probs = probs[:rows, :experts]
        for i in range(0, len(turns), 2):
            moved = swap(backs[i + 1], "ctx", ctx_count, 1)
            back_sum = backs[i].astype(WIDE) + moved.astype(WIDE)
            if turns[i] == 0:
                back_parts.append(back_sum)
                continue
            back_sum = back_sum.astype(LOW)
            if turns[i] == ctx_count - 2:
                back_sum, act_parts[1], gated_parts[1] = tie(back_sum, act_parts[1], gated_parts[1])
            back_parts.append(swap(back_sum, "ctx", ctx_count, turns[i]))
    grad_pieces = list(weight_grads(here, token_blocks, grad_hot, act_parts, gated_parts))
    back_parts[-1], grad_pieces[0], gated_parts[0] = tie(
        back_parts[-1], grad_pieces[0], gated_parts[0]
    )
    mix_part = mix_experts(here, gated_parts, pieces)
    back_total = sum(part.astype(WIDE) for part in back_parts)
    mix_part = lax.psum_scatter(mix_part, "ctx", scatter_dimension=0, tiled=True)
    for turn in range(1, ctx_count):
        grad_pieces[turn] = swap(grad_pieces[turn], "ctx", ctx_count, turn)
    back_sum = sum_over_tp(back_total, tp_count).astype(WIDE)
    back_sum, grad_pieces[1], grad_pieces[2], grad_pieces[4] = tie(
        back_sum, grad_pieces[1], grad_pieces[2], grad_pieces[4]
    )

    normed_two_grad, prob_grads = back_sum[:, :width], back_sum[:, width : width + experts]
    logit_grads = router_probs * (
        prob_grads - jnp.sum(router_probs * prob_grads, -1, keepdims=True)
    )
    router_grad = jnp.dot(logit_grads.T, normed_two.astype(WIDE), precision=PRECISE)
    normed_two_grad = normed_two_grad + jnp.dot(
        logit_grads, extra_all[:experts].astype(WIDE), precision=PRECISE
    )
    inverse = inverse_rms(hidden_one)
    unit_hidden = hidden_one * inverse
    ffn_gain_grad = jnp.sum(normed_two_grad * unit_hidden, 0)
    scaled = normed_two_grad * second_gain
    hidden_grad = grad_low.astype(WIDE) + inverse * (
        scaled - unit_hidden * jnp.mean(scaled * unit_hidden, -1, keepdims=True)
    )
    attended_grad = hidden_grad.astype(LOW)
    mixed_grad = dot(attended_grad, out_all, ((1,), (1,))).astype(LOW)
    out_grad = dot(mixed, attended_grad, ((0,), (0,))).astype(LOW)
    out_w_low = lax.psum_scatter(out_grad, "ctx", scatter_dimension=1, tiled=True)

    normed_part, mix_sum, (weight_grad, owned), *head_gain_grads = attention_back(
        mixed_grad, mix_part, grad_pieces
    )
    some = (0, 1, 2, 3, 4, 5) if ctx_count > 6 else tuple(range(ctx_count))
    rest = tuple(range(len(some), ctx_count))
    unpacked = list(
        unpack_experts(here, [grad_pieces[t] for t in some], some, ctx_count, [])
    )
    inverse = inverse_rms(residual_in)
    unit_input = residual_in * inverse
    attn_gain_grad = jnp.sum(normed_part * unit_input, 0).reshape(ctx_count, width_here)
    head_gain_grad = jnp.concatenate(head_gain_grads)
    head_gain_grad = jnp.broadcast_to(head_gain_grad, (ctx_count, 2 * head_dim))
    second_grads = jnp.concatenate([ffn_gain_grad[None, :], router_grad], 0)
    second_grads = second_grads.reshape(1 + experts, ctx_count, width_here).swapaxes(0, 1)
    second_grads = second_grads.reshape(ctx_count, -1)
    gain_parts = trade(jnp.concatenate([attn_gain_grad, head_gain_grad, second_grads], 1), "ctx")
    weight_grad, gain_parts = tie(weight_grad, gain_parts)
    gain_part = jnp.sum(gain_parts, 0)
    second_sums = gain_part[width_here + 2 * head_dim :].reshape(1 + experts, width_here)
    gain_part = gain_part[: width_here + 2 * head_dim]
    proj_weight_grad = owned(weight_grad)
    normed_grad, gain_sum = sum_over_tp(normed_part, tp_count, gain_part)
    normed_grad, mix_sum, out_w_low, proj_weight_grad, unpacked[0], *grad_pieces[6:] = tie(
        normed_grad, mix_sum, out_w_low, proj_weight_grad, unpacked[0], *grad_pieces[6:]
    )
    if rest:
        unpacked = unpack_experts(here, [grad_pieces[t] for t in rest], rest, ctx_count, unpacked)
    normed_grad, mix_sum = normed_grad.astype(WIDE), mix_sum.astype(WIDE)
    gain_sum = jnp.sum(gain_sum.astype(WIDE), 0)
    scaled = normed_grad * first_gain
    input_grad = hidden_grad + inverse * (
        scaled - unit_input * jnp.mean(scaled * unit_input, -1, keepdims=True)
    )
    output = (hidden_one + mix_sum).astype(LOW)
    gate_out, up_out, down_out = unpacked
    if by_units:
        proj_weight_grad = join_projections(proj_weight_grad, seqs, heads, head_dim)
    else:
        proj_weight_grad = proj_weight_grad.astype(WIDE).reshape(width_here, 3, columns)
        proj_weight_grad = jnp.swapaxes(proj_weight_grad, 0, 1)
    return (
        by_position(output),
        by_position(input_grad),
        gain_sum[:width_here],
        proj_weight_grad[0],
        proj_weight_grad[1],
        proj_weight_grad[2],
        gain_sum[width_here : width_here + head_dim],
        gain_sum[width_here + head_dim : width_here + 2 * head_dim],
        out_w_low.astype(WIDE),
        second_sums[0],
        second_sums[1:].T,
        gate_out,
        up_out,
        down_out,
    )


def solution(mesh):
    token = P("ctx", None, None)
    placed = (
        token,
        P("ctx"),
        P("ctx", "tp"),
        P("ctx", "tp"),
        P("ctx", "tp"),
        P(),
        P(),
        P("tp", "ctx"),
        P("ctx"),
        P("ctx", None),
        P(None, "ctx", "tp"),
        P(None, "ctx", "tp"),
        P(None, "tp", "ctx"),
        token,
        token,
    )
    given = (
        token,
        token,
        P("ctx"),
        P("ctx", "tp"),
        P("ctx", "tp"),
        P("ctx", "tp"),
        P(),
        P(),
        P("tp", "ctx"),
        P("ctx"),
        P("ctx", None),
        P(None, "ctx", "tp"),
        P(None, "ctx", "tp"),
        P(None, "tp", "ctx"),
    )
    return jax.shard_map(
        per_device, mesh=mesh, in_specs=placed, out_specs=given, check_vma=False
    )
```

```python
import functools
import math

import jax
import jax.numpy as jnp
from jax import lax
from jax.experimental import pallas as pl
from jax.experimental.pallas import tpu as pltpu
from jax.sharding import PartitionSpec as P

EPSILON = 1e-06
THETA = 50000.0
PRECISE = lax.Precision.HIGHEST
LOW = jnp.bfloat16
WIDE = jnp.float32
LANES = 128


def mul(equation, left, right):
    return jnp.einsum(equation, left, right, preferred_element_type=WIDE)


def dot(left, right, over):
    return lax.dot_general(left, right, (over, ((), ())), preferred_element_type=WIDE)


def inverse_rms(values):
    return lax.rsqrt(jnp.mean(values * values, -1, keepdims=True) + EPSILON)


def normalize(values, gain_values):
    return values * inverse_rms(values) * gain_values


def rotate(values, cosine, sine):
    half = values.shape[-1] // 2
    first, second = values[..., :half], values[..., half:]
    return jnp.concatenate([first * cosine - second * sine, second * cosine + first * sine], -1)


def tie(*values):
    return lax.optimization_barrier(values)


def trade(values, axis):
    return lax.all_to_all(values, axis, 0, 0, tiled=True)


def swap(values, axis, count, turn):
    return lax.ppermute(values, axis, [(i, i ^ turn) for i in range(count)])


def block_at(values, number, size, dim=0):
    return lax.dynamic_slice_in_dim(values, number * size, size, dim)


def rows_over_tp(values, count):
    rows = values.shape[0] // count
    place = lax.axis_index("tp")
    values = values.astype(LOW)
    total = block_at(values, place, rows).astype(WIDE)
    for turn in range(1, count):
        total += swap(block_at(values, place ^ turn, rows), "tp", count, turn).astype(WIDE)
    return total


def spread_over_tp(total, count):
    return [total] + [swap(total, "tp", count, turn) for turn in range(1, count)]


def sum_over_tp(values, count):
    total = rows_over_tp(values, count).astype(LOW)
    return lax.all_gather(total, "tp", axis=0, tiled=True)


def attend(queries, keys, values, scale):
    scores = mul("xqd,xkd->xqk", queries, keys) * scale
    weights = jnp.exp(scores - jnp.max(scores, -1, keepdims=True))
    probs = weights / jnp.sum(weights, -1, keepdims=True)
    mixed = mul("xqk,xkd->xqd", probs.astype(LOW), values).astype(LOW)
    return probs, mixed


def attend_back(probs, mixed_grad, queries, keys, values, scale):
    values_grad = mul("xqk,xqd->xkd", probs.astype(LOW), mixed_grad)
    prob_grad = mul("xqd,xkd->xqk", mixed_grad, values)
    row_delta = jnp.sum(probs * prob_grad, -1, keepdims=True)
    score_grad = (probs * (prob_grad - row_delta)).astype(LOW)
    queries_grad = mul("xqk,xkd->xqd", score_grad, keys) * scale
    keys_grad = mul("xqk,xqd->xkd", score_grad, queries) * scale
    return queries_grad, keys_grad, values_grad


def pack_kernel(own_experts, place, *refs):
    weights, (*pieces, held, in_sems, out_sems) = refs[:3], refs[3:]
    arriving, leaving = [], []
    for turn, piece in enumerate(pieces):
        start = (place[0] ^ turn) * own_experts
        for kind, weight in enumerate(weights):
            source = weight.at[pl.ds(start, own_experts)]
            target = held.at[turn, pl.ds(kind * own_experts, own_experts)]
            arriving.append(pltpu.make_async_copy(source, target, in_sems.at[3 * turn + kind]))
        leaving.append(pltpu.make_async_copy(held.at[turn], piece, out_sems.at[turn]))
    for copy in arriving:
        copy.start()
    for turn, copy in enumerate(leaving):
        for part in arriving[3 * turn : 3 * turn + 3]:
            part.wait()
        copy.start()
    for copy in leaving:
        copy.wait()


def pack_experts(here, weights, count):
    experts, deep, wide = weights[0].shape
    own_experts = experts // count
    shape = (3 * own_experts, deep, wide)
    anywhere = pl.BlockSpec(memory_space=pl.ANY)
    return pl.pallas_call(
        functools.partial(pack_kernel, own_experts),
        grid_spec=pltpu.PrefetchScalarGridSpec(
            num_scalar_prefetch=1,
            grid=(1,),
            in_specs=[anywhere] * 3,
            out_specs=[anywhere] * count,
            scratch_shapes=[
                pltpu.VMEM((count,) + shape, LOW),
                pltpu.SemaphoreType.DMA((3 * count,)),
                pltpu.SemaphoreType.DMA((count,)),
            ],
        ),
        out_shape=[jax.ShapeDtypeStruct(shape, LOW)] * count,
        compiler_params=pltpu.CompilerParams(vmem_limit_bytes=24 * 2**20),
        cost_estimate=pl.CostEstimate(
            flops=0, bytes_accessed=2 * 2 * 3 * experts * deep * wide, transcendentals=0
        ),
    )(here.reshape(1), *weights)


def unpack_kernel(own_experts, turns, place, *refs):
    count = len(turns)
    pieces, (*outs, held, wide, in_sems, out_sems) = refs[:count], refs[-7:]
    arriving = [
        pltpu.make_async_copy(piece, held.at[i], in_sems.at[i]) for i, piece in enumerate(pieces)
    ]
    leaving = []
    for i, turn in enumerate(turns):
        target = pl.ds((place[0] ^ turn) * own_experts, own_experts)
        for kind, out in enumerate(outs):
            part = pl.ds(kind * own_experts, own_experts)
            leaving.append(
                pltpu.make_async_copy(
                    wide.at[i % 2, part], out.at[target], out_sems.at[3 * i + kind]
                )
            )
    for copy in arriving:
        copy.start()
    for i in range(count):
        arriving[i].wait()
        if i >= 2:
            for copy in leaving[3 * i - 6 : 3 * i - 3]:
                copy.wait()
        wide[i % 2] = held[i].astype(WIDE)
        for copy in leaving[3 * i : 3 * i + 3]:
            copy.start()
    for copy in leaving[-6:] if count > 1 else leaving:
        copy.wait()


def unpack_experts(here, pieces, turns, count, kept):
    blocks, deep, wide = pieces[0].shape
    own_experts = blocks // 3
    anywhere = pl.BlockSpec(memory_space=pl.ANY)
    aliases = {1 + len(turns) + i: i for i in range(3)} if kept else {}
    return pl.pallas_call(
        functools.partial(unpack_kernel, own_experts, turns),
        grid_spec=pltpu.PrefetchScalarGridSpec(
            num_scalar_prefetch=1,
            grid=(1,),
            in_specs=[anywhere] * (len(turns) + len(kept)),
            out_specs=[anywhere] * 3,
            scratch_shapes=[
                pltpu.VMEM((len(turns), blocks, deep, wide), LOW),
                pltpu.VMEM((2, blocks, deep, wide), WIDE),
                pltpu.SemaphoreType.DMA((len(turns),)),
                pltpu.SemaphoreType.DMA((3 * len(turns),)),
            ],
        ),
        out_shape=[jax.ShapeDtypeStruct((count * own_experts, deep, wide), WIDE)] * 3,
        input_output_aliases=aliases,
        compiler_params=pltpu.CompilerParams(vmem_limit_bytes=24 * 2**20),
        cost_estimate=pl.CostEstimate(
            flops=0, bytes_accessed=6 * len(turns) * blocks * deep * wide, transcendentals=0
        ),
    )(here.reshape(1), *pieces, *kept)


def expert_kernel(own_experts, turns, place, *refs):
    count = len(turns)
    tokens, (grad_hot, router, *refs) = refs[:count], refs[count:]
    scratch = refs[-9:]
    rise, fall, token, grad, gated, act, back, in_sems, out_sems = scratch
    sources = len(refs) - 9 - 3 - count
    pieces, (gated_out, act_out, *backs, probs_out) = refs[:sources], refs[sources:-9]
    rows, width = tokens[0].shape
    slices, _, slice_rows, _ = grad_hot.shape
    width_here, hidden_here = pieces[0].shape[1:]
    own_hidden = own_experts * hidden_here
    here = place[0]
    started = []

    def start(source, target):
        copy = pltpu.make_async_copy(source, target, in_sems.at[len(started)])
        copy.start()
        started.append(copy)
        return copy

    def start_tokens(pair):
        return [
            start(tokens[i], token.at[pl.ds(i * rows, rows)]) for i in (2 * pair, 2 * pair + 1)
        ]

    def start_grads(pair):
        return [
            start(
                grad_hot.at[j, here ^ turns[i], :, pl.ds(0, width + LANES)],
                grad.at[pl.ds(i * rows + j * slice_rows, slice_rows)],
            )
            for i in (2 * pair, 2 * pair + 1)
            for j in range(slices)
        ]

    def start_weights(kinds):
        copies = []
        for source, piece in enumerate(pieces):
            deep = pl.ds(pl.multiple_of((here ^ source) * width_here, width_here), width_here)
            for own in range(own_experts):
                near = pl.ds(own * hidden_here, hidden_here)
                far = pl.ds(own_hidden + own * hidden_here, hidden_here)
                targets = (rise.at[deep, near], rise.at[deep, far], fall.at[near, deep])
                for kind in kinds:
                    block = piece.at[kind * own_experts + own]
                    copies.append(start(block, targets[kind]))
        return copies

    token_copies = [start_tokens(0)]
    rise_copies = start_weights((0, 1))
    grad_copies = [start_grads(0)]
    fall_copies = start_weights((2,))
    for pair in range(1, count // 2):
        token_copies.append(start_tokens(pair))
        grad_copies.append(start_grads(pair))
    left = []

    def leave(source, target):
        copy = pltpu.make_async_copy(source, target, out_sems.at[len(left)])
        copy.start()
        left.append(copy)

    lane = lax.broadcasted_iota(jnp.int32, (2 * rows, LANES), 1)
    experts = sources * own_experts
    step = min(512, width)
    for pair in range(count // 2):
        part = pl.ds(2 * pair * rows, 2 * rows)
        for copy in token_copies[pair]:
            copy.wait()
        logits = dot(token[part], router[...], ((1,), (1,)))
        logits = jnp.where(lane < experts, logits, -1e30)
        exp_logits = jnp.exp(logits - jnp.max(logits, -1, keepdims=True))
        probs = exp_logits / jnp.sum(exp_logits, -1, keepdims=True)
        if pair == 0:
            probs_out[...] = probs
            for copy in rise_copies:
                copy.wait()
        acts = []
        for own in range(own_experts):
            near = pl.ds(own * hidden_here, hidden_here)
            far = pl.ds(own_hidden + own * hidden_here, hidden_here)
            acts.append(
                (
                    dot(token[part], rise[:, near], ((1,), (0,))),
                    dot(token[part], rise[:, far], ((1,), (0,))),
                )
            )
        for copy in grad_copies[pair]:
            copy.wait()
        if pair == 0:
            for copy in fall_copies:
                copy.wait()
        hot = grad[part, width : width + LANES].astype(WIDE)
        routed = probs * hot
        placed = jnp.zeros((2 * rows, LANES), WIDE)
        for own, (act_gate, act_up) in enumerate(acts):
            near = pl.ds(own * hidden_here, hidden_here)
            far = pl.ds(own_hidden + own * hidden_here, hidden_here)
            mine = lane == here * own_experts + own
            gates = jnp.sum(jnp.where(mine, routed, 0.0), -1, keepdims=True)
            pulled = dot(grad[part, :width], fall[near, :], ((1,), (1,)))
            sigmoid_gate = jax.nn.sigmoid(act_gate)
            silu = act_gate * sigmoid_gate
            inner = (silu * act_up).astype(LOW).astype(WIDE)
            gate_grads = jnp.sum(inner * pulled, -1, keepdims=True)
            placed = jnp.where(mine, gate_grads * hot, placed)
            gated[part, near] = (inner * gates).astype(LOW)
            inner_grad = pulled * gates
            gate_side = inner_grad * act_up * sigmoid_gate * (1.0 + act_gate * (1.0 - sigmoid_gate))
            act[part, near] = gate_side.astype(LOW)
            act[part, far] = (inner_grad * silu).astype(LOW)
        for first in range(0, width, step):
            columns = pl.ds(first, step)
            back[part, columns] = dot(act[part], rise[columns, :], ((1,), (1,))).astype(LOW)
        back[part, width:] = placed.astype(LOW)
        for i in (2 * pair, 2 * pair + 1):
            leave(back.at[pl.ds(i * rows, rows)], backs[i])
        leave(gated.at[part], gated_out.at[part])
        leave(act.at[part], act_out.at[part])
    for copy in left:
        copy.wait()


def run_experts(turns, here, tokens, grad_hot, router, pieces):
    count = len(turns)
    rows, width = tokens[0].shape
    sources, own_experts = len(pieces), pieces[0].shape[0] // 3
    own_hidden = own_experts * pieces[0].shape[2]
    anywhere = pl.BlockSpec(memory_space=pl.ANY)
    router_spec = pl.BlockSpec((LANES, width), lambda i, p: (0, 0))
    probs_spec = pl.BlockSpec((2 * rows, LANES), lambda i, p: (0, 0))
    shapes = [
        jax.ShapeDtypeStruct((count * rows, own_hidden), LOW),
        jax.ShapeDtypeStruct((count * rows, 2 * own_hidden), LOW),
        *[jax.ShapeDtypeStruct((rows, width + LANES), LOW)] * count,
        jax.ShapeDtypeStruct((2 * rows, LANES), WIDE),
    ]
    copies_in = count * (1 + grad_hot.shape[0]) + 3 * own_experts * sources
    return pl.pallas_call(
        functools.partial(expert_kernel, own_experts, tuple(turns)),
        grid_spec=pltpu.PrefetchScalarGridSpec(
            num_scalar_prefetch=1,
            grid=(1,),
            in_specs=[anywhere] * (count + 1) + [router_spec] + [anywhere] * sources,
            out_specs=[anywhere] * (2 + count) + [probs_spec],
            scratch_shapes=[
                pltpu.VMEM((width, 2 * own_hidden), LOW),
                pltpu.VMEM((own_hidden, width), LOW),
                pltpu.VMEM((count * rows, width), LOW),
                pltpu.VMEM((count * rows, width + LANES), LOW),
                pltpu.VMEM((count * rows, own_hidden), LOW),
                pltpu.VMEM((count * rows, 2 * own_hidden), LOW),
                pltpu.VMEM((count * rows, width + LANES), LOW),
                pltpu.SemaphoreType.DMA((copies_in,)),
                pltpu.SemaphoreType.DMA((2 * count,)),
            ],
        ),
        out_shape=shapes,
        compiler_params=pltpu.CompilerParams(vmem_limit_bytes=40 * 2**20),
        cost_estimate=pl.CostEstimate(
            flops=2 * count * rows * width * own_hidden * 5,
            bytes_accessed=2 * (3 * own_hidden * width + count * rows * width * 4),
            transcendentals=0,
        ),
    )(here.reshape(1), *tokens, grad_hot, router, *pieces)


def mix_kernel(own_experts, sources, place, *refs):
    gated_near, gated_far, pieces = refs[0], refs[1], refs[2 : 2 + sources]
    out, fall, sems = refs[2 + sources :]
    width_here, hidden_here = pieces[0].shape[1:]
    rows = gated_near.shape[0] // 2
    step, here = pl.program_id(0), place[0]

    @pl.when(step == 0)
    def _():
        copies = []
        for source, piece in enumerate(pieces):
            start = pl.multiple_of((here ^ source) * width_here, width_here)
            for own in range(own_experts):
                target = fall.at[pl.ds(own * hidden_here, hidden_here), pl.ds(start, width_here)]
                sem = sems.at[own_experts * source + own]
                block = piece.at[2 * own_experts + own]
                copies.append(pltpu.make_async_copy(block, target, sem))
        for copy in copies:
            copy.start()
        for copy in copies:
            copy.wait()

    gated = jnp.where(step == 0, gated_near[...], gated_far[...])
    swapped = lax.rem(here, 2)
    first = pl.ds(pl.multiple_of(swapped * rows, rows), rows)
    second = pl.ds(pl.multiple_of((1 - swapped) * rows, rows), rows)
    mix = dot(gated, fall[...], ((1,), (0,))).astype(LOW)
    out[first] = mix[:rows]
    out[second] = mix[rows:]


def mix_experts(here, gated_parts, pieces):
    sources, own_experts = len(pieces), pieces[0].shape[0] // 3
    pair_rows, own_hidden = gated_parts[0].shape
    total = pair_rows * sources // 2
    width = sources * pieces[0].shape[1]
    return pl.pallas_call(
        functools.partial(mix_kernel, own_experts, sources),
        grid_spec=pltpu.PrefetchScalarGridSpec(
            num_scalar_prefetch=1,
            grid=(sources // 2,),
            in_specs=[
                pl.BlockSpec((pair_rows, own_hidden), lambda t, p: (0, 0)),
                pl.BlockSpec((pair_rows, own_hidden), lambda t, p: (jnp.maximum(t - 1, 0), 0)),
            ]
            + [pl.BlockSpec(memory_space=pl.ANY)] * sources,
            out_specs=pl.BlockSpec((pair_rows, width), lambda t, p: ((p[0] ^ (2 * t)) // 2, 0)),
            scratch_shapes=[
                pltpu.VMEM((own_hidden, width), LOW),
                pltpu.SemaphoreType.DMA((own_experts * sources,)),
            ],
        ),
        out_shape=jax.ShapeDtypeStruct((total, width), LOW),
        compiler_params=pltpu.CompilerParams(vmem_limit_bytes=56 * 2**20),
        cost_estimate=pl.CostEstimate(
            flops=0, bytes_accessed=own_hidden * width,
            transcendentals=0,
        ),
    )(here.reshape(1), *gated_parts, *pieces)


def project_kernel(first_column, mixed, blocks, out_all, attended, sems):
    count, rows, _ = blocks.shape
    columns, width = out_all.shape
    width_here = width // count
    copies = []
    for source in range(count):
        for i in range(columns // rows):
            block = blocks.at[source, :, pl.ds(first_column + i * width_here, width_here)]
            target = out_all.at[pl.ds(i * rows, rows), pl.ds(source * width_here, width_here)]
            sem = sems.at[source * (columns // rows) + i]
            copies.append(pltpu.make_async_copy(block, target, sem))
    for copy in copies:
        copy.start()
    for copy in copies:
        copy.wait()
    attended[...] = dot(mixed[...], out_all[...], ((1,), (0,))).astype(LOW)


def project(mixed, blocks, first_column, width):
    rows, columns = mixed.shape
    count = blocks.shape[0]
    return pl.pallas_call(
        functools.partial(project_kernel, first_column),
        in_specs=[pl.BlockSpec(memory_space=pltpu.VMEM), pl.BlockSpec(memory_space=pl.ANY)],
        out_specs=[pl.BlockSpec(memory_space=pltpu.VMEM)] * 2,
        scratch_shapes=[pltpu.SemaphoreType.DMA((count * (columns // rows),))],
        out_shape=[
            jax.ShapeDtypeStruct((columns, width), LOW),
            jax.ShapeDtypeStruct((rows, width), LOW),
        ],
        compiler_params=pltpu.CompilerParams(vmem_limit_bytes=32 * 2**20),
        cost_estimate=pl.CostEstimate(
            flops=2 * rows * columns * width,
            bytes_accessed=2 * 2 * columns * width,
            transcendentals=0,
        ),
    )(mixed, blocks)


def join_kernel(seqs, heads, head_dim, moved, *outs):
    for i, out in enumerate(outs):
        part = slice(i * head_dim, (i + 1) * head_dim)
        for head in range(heads):
            units = [2 * seqs * (head // 2) + 2 * seq + head % 2 for seq in range(seqs)]
            total = sum(moved[unit, : out.shape[0], part].astype(WIDE) for unit in units)
            out[:, head * head_dim : (head + 1) * head_dim] = total


def join_projections(moved, rows, seqs, heads, head_dim):
    shape = jax.ShapeDtypeStruct((rows, heads * head_dim), WIDE)
    return pl.pallas_call(
        functools.partial(join_kernel, seqs, heads, head_dim),
        out_shape=[shape] * 3,
        compiler_params=pltpu.CompilerParams(vmem_limit_bytes=32 * 2**20),
        cost_estimate=pl.CostEstimate(
            flops=0, bytes_accessed=2 * moved.size + 12 * rows * heads * head_dim, transcendentals=0
        ),
    )(moved)


def finish_kernel(count, place, *refs):
    normed, refs = refs[:count], refs[count:]
    hidden, mix, inputs, hidden_grad, gain, output, input_grad, grad_all = refs
    rows = normed[0].shape[0]
    for turn in range(count):
        part = pl.ds(pl.multiple_of((place[0] ^ turn) * rows, rows), rows)
        grad_all[part] = normed[turn][...]
    shard_len, seqs, _ = output.shape
    for seq in range(seqs):
        part = slice(seq * shard_len, (seq + 1) * shard_len)
        values = inputs[part]
        inverse = lax.rsqrt(jnp.mean(values * values, -1, keepdims=True) + EPSILON)
        unit = values * inverse
        scaled = grad_all[part].astype(WIDE) * gain[...]
        mean = jnp.mean(scaled * unit, -1, keepdims=True)
        input_grad[:, seq, :] = hidden_grad[part] + inverse * (scaled - unit * mean)
        output[:, seq, :] = (hidden[part] + mix[part].astype(WIDE)).astype(LOW)


def finish(place, normed, hidden, mix, inputs, hidden_grad, gain, seqs):
    count = len(normed)
    rows, width = inputs.shape
    shard_len = rows // seqs
    vmem = pl.BlockSpec(memory_space=pltpu.VMEM)
    smem = pl.BlockSpec(memory_space=pltpu.SMEM)
    return pl.pallas_call(
        functools.partial(finish_kernel, count),
        in_specs=[smem] + [vmem] * (count + 5),
        out_specs=[vmem] * 2,
        scratch_shapes=[pltpu.VMEM((rows, width), LOW)],
        out_shape=[
            jax.ShapeDtypeStruct((shard_len, seqs, width), LOW),
            jax.ShapeDtypeStruct((shard_len, seqs, width), WIDE),
        ],
        compiler_params=pltpu.CompilerParams(vmem_limit_bytes=32 * 2**20),
        cost_estimate=pl.CostEstimate(
            flops=10 * rows * width, bytes_accessed=16 * rows * width, transcendentals=0
        ),
    )(place.reshape(1), *normed, hidden, mix, inputs, hidden_grad, gain)


def pack_heads_kernel(head_dim, *refs):
    weights, (sent, held, in_sems, out_sems) = refs[:3], refs[3:]
    arriving = [pltpu.make_async_copy(w, held.at[i], in_sems.at[i]) for i, w in enumerate(weights)]
    for copy in arriving:
        copy.start()
    leaving = []
    for kind, copy in enumerate(arriving):
        copy.wait()
        for unit in range(sent.shape[0]):
            head = 2 * (unit // 4) + unit % 2
            source = held.at[kind, :, pl.ds(head * head_dim, head_dim)]
            target = sent.at[unit, :, pl.ds(kind * head_dim, head_dim)]
            leaving.append(pltpu.make_async_copy(source, target, out_sems.at[len(leaving)]))
            leaving[-1].start()
    for copy in leaving:
        copy.wait()


def pack_heads(weights, units, head_dim):
    rows, columns = weights[0].shape
    anywhere = pl.BlockSpec(memory_space=pl.ANY)
    return pl.pallas_call(
        functools.partial(pack_heads_kernel, head_dim),
        in_specs=[anywhere] * 3,
        out_specs=anywhere,
        scratch_shapes=[
            pltpu.VMEM((3, rows, columns), LOW),
            pltpu.SemaphoreType.DMA((3,)),
            pltpu.SemaphoreType.DMA((3 * units,)),
        ],
        out_shape=jax.ShapeDtypeStruct((units, rows, 3 * head_dim), LOW),
        compiler_params=pltpu.CompilerParams(vmem_limit_bytes=24 * 2**20),
        cost_estimate=pl.CostEstimate(flops=0, bytes_accessed=rows * columns, transcendentals=0),
    )(*weights)


def unit_norm_kernel(shard_len, width_here, gain_at, place, near, far, unit_in, normed, gain):
    core = lax.rem(place[0], 2)
    chips, _, width = near.shape
    row, lane = shard_len + gain_at // width, gain_at % width
    for other, part in enumerate((near, far)):
        for chip in range(chips):
            start = pl.multiple_of((2 * chip + (core ^ other)) * width_here, width_here)
            piece = part[chip, row : row + 1, lane : lane + width_here]
            gain[:, pl.ds(start, width_here)] = piece.astype(WIDE)
    for other, part in enumerate((near, far)):
        for chip in range(chips):
            rows = pl.ds((other * chips + chip) * shard_len, shard_len)
            low = part[chip, :shard_len]
            values = low.astype(WIDE)
            inverse = lax.rsqrt(jnp.mean(values * values, -1, keepdims=True) + EPSILON)
            unit_in[rows] = low
            normed[rows] = (values * inverse * gain[...]).astype(LOW)


def unit_norm(here, near, far, shard_len, width_here, gain_at):
    chips, _, width = near.shape
    vmem = pl.BlockSpec(memory_space=pltpu.VMEM)
    smem = pl.BlockSpec(memory_space=pltpu.SMEM)
    shape = jax.ShapeDtypeStruct((2 * chips * shard_len, width), LOW)
    return pl.pallas_call(
        functools.partial(unit_norm_kernel, shard_len, width_here, gain_at),
        in_specs=[smem, vmem, vmem],
        out_specs=[vmem] * 2,
        scratch_shapes=[pltpu.VMEM((1, width), WIDE)],
        out_shape=[shape] * 2,
        compiler_params=pltpu.CompilerParams(vmem_limit_bytes=32 * 2**20),
        cost_estimate=pl.CostEstimate(flops=0, bytes_accessed=0, transcendentals=0),
    )(here.reshape(1), near, far)


def weight_grad_kernel(own_experts, count, place, *refs):
    tokens, grads = refs[:count], refs[count : 2 * count]
    act_parts, gated_parts = refs[2 * count : 2 * count + 2], refs[2 * count + 2 : 2 * count + 4]
    pieces, (token, grad, act, gated) = refs[2 * count + 4 : -4], refs[-4:]
    rows = tokens[0].shape[0]
    hidden_here = pieces[0].shape[2]
    split = 2 * rows

    @pl.when(pl.program_id(0) == 0)
    def _():
        for part, source in ((slice(0, split), 0), (slice(split, None), 1)):
            act[part] = act_parts[source][...]
            gated[:, part] = gated_parts[source][...].T

    for turn in range(count):
        part = pl.ds(turn * rows, rows)
        token[part] = tokens[turn][...]
        grad[part] = grads[turn][...].reshape(rows, grad.shape[1])
    rise = dot(token[...], act[...], ((0,), (0,))).astype(LOW)
    fall = dot(gated[...], grad[...], ((1,), (0,))).astype(LOW)
    for turn, piece in enumerate(pieces):

        @pl.when(pl.program_id(0) == turn)
        def _():
            for i in range(2 * own_experts):
                piece[i] = rise[:, i * hidden_here : (i + 1) * hidden_here]
            for i in range(own_experts):
                piece[2 * own_experts + i] = fall[i * hidden_here : (i + 1) * hidden_here]


def weight_grads(here, tokens, grad_hot, act_parts, gated_parts):
    count = len(tokens)
    rows, width = tokens[0].shape
    width_here = width // count
    own_hidden = gated_parts[0].shape[1]
    own_experts = own_hidden // width_here
    hidden_here = own_hidden // own_experts
    total = count * rows
    slices, _, slice_rows, _ = grad_hot.shape

    def grad_spec(turn):
        shape = (slices, 1, slice_rows, width_here)
        return pl.BlockSpec(shape, lambda t, p: (0, p[0] ^ turn, 0, p[0] ^ t))

    def whole(shape):
        return pl.BlockSpec(shape, lambda t, p: (0,) * len(shape))

    shape = (3 * own_experts, width_here, hidden_here)
    return pl.pallas_call(
        functools.partial(weight_grad_kernel, own_experts, count),
        grid_spec=pltpu.PrefetchScalarGridSpec(
            num_scalar_prefetch=1,
            grid=(count,),
            in_specs=[pl.BlockSpec((rows, width_here), lambda t, p: (0, p[0] ^ t))] * count
            + [grad_spec(turn) for turn in range(count)]
            + [whole(part.shape) for part in (*act_parts, *gated_parts)],
            out_specs=[whole(shape)] * count,
            scratch_shapes=[
                pltpu.VMEM((total, width_here), LOW),
                pltpu.VMEM((total, width_here), LOW),
                pltpu.VMEM((total, 2 * own_hidden), LOW),
                pltpu.VMEM((own_hidden, total), LOW),
            ],
        ),
        out_shape=[jax.ShapeDtypeStruct(shape, LOW)] * count,
        compiler_params=pltpu.CompilerParams(vmem_limit_bytes=56 * 2**20),
        cost_estimate=pl.CostEstimate(
            flops=0, bytes_accessed=2 * own_hidden * width,
            transcendentals=0,
        ),
    )(here.reshape(1), *tokens, *([grad_hot] * count), *act_parts, *gated_parts)


def per_device(
    inputs,
    attn_gain,
    w_query,
    w_key,
    w_value,
    query_gain,
    key_gain,
    w_out,
    ffn_gain,
    w_router,
    w_gate,
    w_up,
    w_down,
    routes,
    cotangent,
):
    here = lax.axis_index("ctx")
    shard_len, seqs, width = inputs.shape
    width_here = attn_gain.shape[0]
    ctx_count = width // width_here
    head_dim = query_gain.shape[0]
    columns = w_query.shape[1]
    heads = columns // head_dim
    experts, _, hidden_here = w_gate.shape
    own_experts = experts // ctx_count
    tp_count = lax.axis_size("tp")
    rows = seqs * shard_len
    units = seqs * heads
    length = ctx_count * shard_len
    scale = 1.0 / math.sqrt(head_dim)

    def by_sequence(values):
        return jnp.swapaxes(values, 0, 1).reshape((rows,) + values.shape[2:])

    extra = jnp.concatenate([w_router.T, attn_gain[None, :], ffn_gain[None, :]], 0)
    extra = jnp.pad(extra, ((0, 32 - extra.shape[0]), (0, 0)))

    residual_in = by_sequence(inputs).astype(WIDE)
    grad_low = by_sequence(cotangent)
    frequency = THETA ** (-(jnp.arange(head_dim // 2, dtype=WIDE) * 2.0) / head_dim)
    query_scale, key_scale = query_gain.astype(WIDE), key_gain.astype(WIDE)

    def turned(positions):
        angles = positions.astype(WIDE)[:, None] * frequency
        cosine, sine = jnp.cos(angles), jnp.sin(angles)

        def prepare(values, gain_values):
            return rotate(normalize(values, gain_values), cosine, sine)

        return prepare

    core = here % 2

    def own_core_first(blocks):
        pairs = jnp.swapaxes(blocks.reshape((ctx_count // 2, 2) + blocks.shape[1:]), 0, 1)
        return jnp.where(core == 0, pairs, pairs[::-1])

    def by_ctx(pairs):
        pairs = jnp.where(core == 0, pairs, pairs[::-1])
        return jnp.swapaxes(pairs, 0, 1).reshape((ctx_count,) + pairs.shape[2:])

    def to_units(member):
        member = member.reshape(seqs, shard_len, heads // 2, 2, head_dim)
        member = member.transpose(2, 0, 3, 1, 4).reshape(units, shard_len, head_dim)
        return own_core_first(trade(member, "ctx")).reshape(length, head_dim)

    def from_units(member):
        member = by_ctx(member.reshape(2, ctx_count // 2, shard_len, head_dim))
        moved = trade(member, "ctx").reshape(heads // 2, seqs, 2, shard_len, head_dim)
        return moved.transpose(1, 3, 0, 2, 4).reshape(rows, columns)

    def trade_same_core(values):
        groups = [list(range(i, ctx_count, 2)) for i in range(2)]
        return lax.all_to_all(values, "ctx", 0, 0, tiled=True, axis_index_groups=groups)

    def attention_by_units(sent_pieces):
        chips = ctx_count // 2
        sent = jnp.swapaxes(inputs, 0, 1)
        sent = jnp.broadcast_to(sent[None], (chips // seqs, seqs, shard_len, width))
        rider = extra.reshape(1, -1, width)
        rider_rows = rider.shape[1]
        rider = jnp.pad(rider, ((0, 0), (0, 8 - rider_rows), (0, 0)))
        rider = jnp.broadcast_to(rider, (chips, 8, width))
        sent = jnp.concatenate([sent.reshape(chips, shard_len, width), rider], 1)
        near = trade_same_core(sent)
        sent = pack_heads((w_query, w_key, w_value), units, head_dim)
        sent, near, *sent_pieces = tie(sent, near, *sent_pieces)
        far = swap(near, "ctx", ctx_count, 1)
        unit_weights = trade(sent, "ctx").reshape(width, 3 * head_dim)
        far, *sent_pieces = tie(far, *sent_pieces)
        unit_in, unit_normed = unit_norm(
            here, near, far, shard_len, width_here, experts * width_here
        )
        riders = jnp.stack([part[:, shard_len : shard_len + rider_rows] for part in (near, far)])
        extra_all = by_ctx(riders).reshape(ctx_count, 32, width_here)
        extra_all = jnp.swapaxes(extra_all, 0, 1).reshape(32, width)
        first_gain = extra_all[experts].astype(WIDE)
        projected = jnp.dot(unit_normed, unit_weights, preferred_element_type=WIDE)
        owners = jnp.arange(2)[:, None] ^ core
        owners = (2 * jnp.arange(chips)[None, :] + owners).reshape(ctx_count, 1)
        prepare = turned((owners * shard_len + jnp.arange(shard_len)).reshape(length))
        queries, query_pull = jax.vjp(prepare, projected[:, :head_dim], query_scale)
        keys, key_pull = jax.vjp(prepare, projected[:, head_dim : 2 * head_dim], key_scale)
        parts = [m.astype(LOW)[None] for m in (queries, keys, projected[:, 2 * head_dim :])]
        probs, unit_mixed = attend(*parts, scale)

        def back(mixed_grad, grad_pieces):
            unit_grad = to_units(mixed_grad)[None]
            grads = attend_back(probs, unit_grad, *parts, scale)
            query_grad, query_gain_grad = query_pull(grads[0][0])
            key_grad, key_gain_grad = key_pull(grads[1][0])
            proj_grad = jnp.concatenate([query_grad, key_grad, grads[2][0]], 1).astype(LOW)
            part = dot(proj_grad, unit_weights, ((1,), (1,)))
            unit_input = unit_in.astype(WIDE)
            attn_gain_grad = jnp.sum(part * unit_input * inverse_rms(unit_input), 0)
            part = part.astype(LOW)
            part = part.reshape(2, chips, shard_len, width)
            moved = swap(part[1], "ctx", ctx_count, 1).astype(WIDE)
            part = (part[0].astype(WIDE) + moved).astype(LOW)
            part = trade_same_core(part)
            part, grad_pieces[3], grad_pieces[5] = tie(part, grad_pieces[3], grad_pieces[5])
            part = part.reshape(chips // seqs, seqs, shard_len, width).astype(WIDE)
            part = jnp.sum(part, 0)
            weight_grad = dot(unit_normed, proj_grad, ((0,), (0,))).astype(LOW)

            def owned(weight_grad, gains):
                deep = 3 * head_dim
                rider_rows = -(-gains.shape[1] // (16 * deep)) * 16
                pad = rider_rows * deep - gains.shape[1]
                rider = jnp.pad(gains.astype(LOW), ((0, 0), (0, pad)))
                rider = rider.reshape(ctx_count, rider_rows, deep)
                weight_grad = weight_grad.reshape(ctx_count, width_here, deep)
                moved = trade(jnp.concatenate([weight_grad, rider], 1), "ctx")
                gains_in = moved[:, width_here:].reshape(ctx_count, -1)[:, : gains.shape[1]]
                return moved, gains_in

            part = part.reshape(rows, width)
            gain_grads = attn_gain_grad, query_gain_grad, key_gain_grad
            return part, (weight_grad, owned), gain_grads

        return unit_mixed[0], from_units, back, extra_all, sent_pieces

    def attention_by_tokens(sent_pieces):
        extra_all = jnp.swapaxes(lax.all_gather(extra, "ctx", axis=0), 0, 1).reshape(32, width)
        first_gain = extra_all[experts].astype(WIDE)
        packed = jnp.concatenate([w_query, w_key, w_value], 1)
        packed = lax.all_gather(packed, "ctx", axis=0, tiled=True)
        normed = normalize(residual_in, first_gain).astype(LOW)
        projected = jnp.dot(normed, packed, preferred_element_type=WIDE)
        positions = here * shard_len + jnp.arange(shard_len, dtype=jnp.int32)

        def heads_first(member):
            member = member.reshape(seqs, shard_len, heads, head_dim)
            return member.transpose(0, 2, 1, 3).reshape(units, shard_len, head_dim)

        def tokens_first(member):
            member = member.reshape(seqs, heads, shard_len, head_dim)
            return member.transpose(0, 2, 1, 3).reshape(rows, columns)

        prepare = turned(positions)
        cuts = [heads_first(projected[:, i * columns : (i + 1) * columns]) for i in range(3)]
        queries, query_pull = jax.vjp(prepare, cuts[0], query_scale)
        keys, key_pull = jax.vjp(prepare, cuts[1], key_scale)
        queries = queries.astype(LOW)
        pairs = jnp.concatenate([keys, cuts[2]], -1).astype(LOW)
        pairs = lax.all_gather(pairs, "ctx", axis=1, tiled=True)
        parts = [queries, pairs[..., :head_dim], pairs[..., head_dim:]]
        probs, mixed = attend(*parts, scale)

        def back(mixed_grad, grad_pieces):
            grads = attend_back(probs, heads_first(mixed_grad), *parts, scale)
            moved = jnp.concatenate(grads[1:], -1).astype(LOW)
            moved = lax.psum_scatter(moved, "ctx", scatter_dimension=1, tiled=True).astype(WIDE)
            query_grad, query_gain_grad = query_pull(grads[0])
            key_grad, key_gain_grad = key_pull(moved[..., :head_dim])
            proj_grad = [tokens_first(g) for g in (query_grad, key_grad, moved[..., head_dim:])]
            proj_grad = jnp.concatenate(proj_grad, 1).astype(LOW)
            part = dot(proj_grad, packed, ((1,), (1,)))
            weight_grad = dot(normed, proj_grad, ((0,), (0,))).astype(LOW)

            def owned(weight_grad, gains):
                moved = lax.psum_scatter(weight_grad, "ctx", scatter_dimension=0, tiled=True)
                return moved, trade(gains.astype(LOW), "ctx")

            attn_gain_grad = jnp.sum(part * residual_in * inverse_rms(residual_in), 0)
            gain_grads = attn_gain_grad, query_gain_grad, key_gain_grad
            return part, (weight_grad, owned), gain_grads

        return mixed, tokens_first, back, extra_all, sent_pieces

    by_units = (ctx_count, seqs, heads) == (8, 2, 4)
    expert_ids = jnp.arange(LANES, dtype=jnp.int32)
    hot = jnp.sum((by_sequence(routes)[:, :, None] == expert_ids).astype(WIDE), 1).astype(LOW)
    grad_hot = jnp.concatenate([grad_low, hot], 1)
    sent = pack_experts(here, (w_gate, w_up, w_down), ctx_count)
    local_mixed, to_tokens, attention_back, extra_all, (*sent, grad_hot) = (
        attention_by_units([*sent, grad_hot])
        if by_units
        else attention_by_tokens([*sent, grad_hot])
    )
    first_gain = extra_all[experts].astype(WIDE)
    second_gain = extra_all[experts + 1].astype(WIDE)
    router_rows = jnp.pad(extra_all[:experts], ((0, LANES - experts), (0, 0)))
    stack = columns // rows
    out_cut = jnp.swapaxes(w_out.reshape(stack, rows, width_here), 0, 1)
    out_cut = out_cut.reshape(rows, stack * width_here)
    out_blocks = lax.all_gather(out_cut, "ctx", axis=0)
    grad_hot = lax.all_gather(grad_hot, "ctx", axis=0)[None]

    pieces = list(sent)
    for turn in (1, 2, 4):
        pieces[turn] = swap(sent[turn], "ctx", ctx_count, turn)
    mixed = to_tokens(local_mixed)
    mixed, *pieces = tie(mixed, *pieces)
    for turn in (3, *range(5, ctx_count)):
        pieces[turn] = swap(pieces[turn], "ctx", ctx_count, turn)

    out_all, attended = project(mixed, out_blocks, 0, width)
    attended = sum_over_tp(attended, tp_count)
    attended, pieces[3], *pieces[5:] = tie(attended, pieces[3], *pieces[5:])
    hidden_one = residual_in + attended.astype(WIDE)
    normed_two = normalize(hidden_one, second_gain).astype(LOW)

    token_blocks = [normed_two, swap(normed_two, "ctx", ctx_count, 1)]
    token_blocks += [None] * (ctx_count - 2)
    for turn in range(2, ctx_count, 2):
        token_blocks[turn] = swap(normed_two, "ctx", ctx_count, turn)
    back_parts, gated_parts, act_parts = [], [], []
    for turns in (range(2), range(2, ctx_count)):
        blocks = [token_blocks[turn] for turn in turns]
        gated, act_grad, *backs, probs = run_experts(
            turns, here, blocks, grad_hot, router_rows, pieces
        )
        gated_parts.append(gated)
        act_parts.append(act_grad)
        if turns[0] == 0:
            probs, *token_blocks[2::2] = tie(probs, *token_blocks[2::2])
            for turn in range(2, ctx_count, 2):
                token_blocks[turn + 1] = swap(token_blocks[turn], "ctx", ctx_count, 1)
            router_probs = probs[:rows, :experts]
        for i in range(0, len(turns), 2):
            moved = swap(backs[i + 1], "ctx", ctx_count, 1)
            back_sum = backs[i].astype(WIDE) + moved.astype(WIDE)
            if turns[i] == 0:
                back_parts.append(back_sum)
                continue
            back_parts.append(back_sum.astype(LOW))
    *back_parts, act_parts[1], gated_parts[1] = tie(*back_parts, act_parts[1], gated_parts[1])
    for i in range(1, len(back_parts)):
        back_parts[i] = swap(back_parts[i], "ctx", ctx_count, 2 * i)
    grad_pieces = list(weight_grads(here, token_blocks, grad_hot, act_parts, gated_parts))
    mix_part = mix_experts(here, gated_parts, pieces)
    *back_parts, grad_pieces[0], mix_part = tie(*back_parts, grad_pieces[0], mix_part)
    back_total = sum(part.astype(WIDE) for part in back_parts)
    mix_part = lax.psum_scatter(mix_part, "ctx", scatter_dimension=0, tiled=True)
    mix_sum = lax.psum(mix_part, "tp")
    for turn in range(1, ctx_count):
        grad_pieces[turn] = swap(grad_pieces[turn], "ctx", ctx_count, turn)
    back_sum = sum_over_tp(back_total, tp_count).astype(WIDE)
    back_sum, grad_pieces[1], grad_pieces[2], grad_pieces[4] = tie(
        back_sum, grad_pieces[1], grad_pieces[2], grad_pieces[4]
    )

    normed_two_grad, prob_grads = back_sum[:, :width], back_sum[:, width : width + experts]
    logit_grads = router_probs * (
        prob_grads - jnp.sum(router_probs * prob_grads, -1, keepdims=True)
    )
    router_grad = jnp.dot(logit_grads.T, normed_two.astype(WIDE), precision=PRECISE)
    normed_two_grad = normed_two_grad + jnp.dot(
        logit_grads, extra_all[:experts].astype(WIDE), precision=PRECISE
    )
    inverse = inverse_rms(hidden_one)
    unit_hidden = hidden_one * inverse
    ffn_gain_grad = jnp.sum(normed_two_grad * unit_hidden, 0)
    scaled = normed_two_grad * second_gain
    hidden_grad = grad_low.astype(WIDE) + inverse * (
        scaled - unit_hidden * jnp.mean(scaled * unit_hidden, -1, keepdims=True)
    )
    attended_grad = hidden_grad.astype(LOW)
    mixed_grad = dot(attended_grad, out_all, ((1,), (1,))).astype(LOW)
    out_grad = dot(mixed, attended_grad, ((0,), (0,))).astype(LOW)

    normed_part, (weight_grad, owned), gain_grads = attention_back(mixed_grad, grad_pieces)
    normed_part, out_grad = tie(normed_part, out_grad)
    out_w_low = lax.psum_scatter(out_grad, "ctx", scatter_dimension=1, tiled=True)
    some = (0, 1, 2, 3, 4, 5) if ctx_count > 6 else tuple(range(ctx_count))
    rest = tuple(range(len(some), ctx_count))
    unpacked = list(
        unpack_experts(here, [grad_pieces[t] for t in some], some, ctx_count, [])
    )
    attn_gain_grad = gain_grads[0].reshape(ctx_count, width_here)
    head_gain_grad = jnp.concatenate(gain_grads[1:])
    head_gain_grad = jnp.broadcast_to(head_gain_grad, (ctx_count, 2 * head_dim))
    second_grads = jnp.concatenate([ffn_gain_grad[None, :], router_grad], 0)
    second_grads = second_grads.reshape(1 + experts, ctx_count, width_here).swapaxes(0, 1)
    second_grads = second_grads.reshape(ctx_count, -1)
    gain_parts = jnp.concatenate([attn_gain_grad, head_gain_grad, second_grads], 1)
    weight_grad, normed_part = tie(weight_grad, normed_part)
    proj_weight_grad, gain_parts = owned(weight_grad, gain_parts)
    gain_part = jnp.sum(gain_parts.astype(WIDE), 0)
    second_sums = gain_part[width_here + 2 * head_dim :].reshape(1 + experts, width_here)
    gain_part = gain_part[: width_here + 2 * head_dim]
    place = lax.axis_index("tp")
    normed_rows = rows_over_tp(normed_part, tp_count).astype(LOW)
    normed_rows, unpacked[0] = tie(normed_rows, unpacked[0])
    normed_rows = spread_over_tp(normed_rows, tp_count)
    gain_sum = sum(spread_over_tp(gain_part, tp_count))
    output, input_grad = finish(
        place, normed_rows, hidden_one, mix_sum, residual_in, hidden_grad, first_gain[None, :], seqs
    )
    input_grad, out_w_low, *grad_pieces[6:] = tie(input_grad, out_w_low, *grad_pieces[6:])
    router_out, ffn_gain_out = second_sums[1:].T, second_sums[0]
    if rest:
        unpacked = unpack_experts(here, [grad_pieces[t] for t in rest], rest, ctx_count, unpacked)
    gate_out, up_out, down_out = unpacked
    if by_units:
        proj_weight_grad = join_projections(proj_weight_grad, width_here, seqs, heads, head_dim)
    else:
        proj_weight_grad = proj_weight_grad.astype(WIDE).reshape(width_here, 3, columns)
        proj_weight_grad = jnp.swapaxes(proj_weight_grad, 0, 1)
    return (
        output,
        input_grad,
        gain_sum[:width_here],
        proj_weight_grad[0],
        proj_weight_grad[1],
        proj_weight_grad[2],
        gain_sum[width_here : width_here + head_dim],
        gain_sum[width_here + head_dim : width_here + 2 * head_dim],
        out_w_low.astype(WIDE),
        ffn_gain_out,
        router_out,
        gate_out,
        up_out,
        down_out,
    )


def solution(mesh):
    token = P("ctx", None, None)
    placed = (
        token,
        P("ctx"),
        P("ctx", "tp"),
        P("ctx", "tp"),
        P("ctx", "tp"),
        P(),
        P(),
        P("tp", "ctx"),
        P("ctx"),
        P("ctx", None),
        P(None, "ctx", "tp"),
        P(None, "ctx", "tp"),
        P(None, "tp", "ctx"),
        token,
        token,
    )
    given = (
        token,
        token,
        P("ctx"),
        P("ctx", "tp"),
        P("ctx", "tp"),
        P("ctx", "tp"),
        P(),
        P(),
        P("tp", "ctx"),
        P("ctx"),
        P("ctx", None),
        P(None, "ctx", "tp"),
        P(None, "ctx", "tp"),
        P(None, "tp", "ctx"),
    )
    return jax.shard_map(
        per_device, mesh=mesh, in_specs=placed, out_specs=given, check_vma=False
    )
```

```python
import functools
import math

import jax
import jax.numpy as jnp
from jax import lax
from jax.experimental import pallas as pl
from jax.experimental.pallas import tpu as pltpu
from jax.sharding import PartitionSpec as P

EPSILON = 1e-06
THETA = 50000.0
PRECISE = lax.Precision.HIGHEST
LOW = jnp.bfloat16
WIDE = jnp.float32
LANES = 128


def mul(equation, left, right):
    return jnp.einsum(equation, left, right, preferred_element_type=WIDE)


def dot(left, right, over):
    return lax.dot_general(left, right, (over, ((), ())), preferred_element_type=WIDE)


def inverse_rms(values):
    return lax.rsqrt(jnp.mean(values * values, -1, keepdims=True) + EPSILON)


def normalize(values, gain_values):
    return values * inverse_rms(values) * gain_values


def rotate(values, cosine, sine):
    half = values.shape[-1] // 2
    first, second = values[..., :half], values[..., half:]
    return jnp.concatenate([first * cosine - second * sine, second * cosine + first * sine], -1)


def tie(*values):
    return lax.optimization_barrier(values)


def trade(values, axis):
    return lax.all_to_all(values, axis, 0, 0, tiled=True)


def swap(values, axis, count, turn):
    return lax.ppermute(values, axis, [(i, i ^ turn) for i in range(count)])


def block_at(values, number, size, dim=0):
    return lax.dynamic_slice_in_dim(values, number * size, size, dim)


def rows_over_tp(values, count):
    rows = values.shape[0] // count
    place = lax.axis_index("tp")
    values = values.astype(LOW)
    total = block_at(values, place, rows).astype(WIDE)
    for turn in range(1, count):
        total += swap(block_at(values, place ^ turn, rows), "tp", count, turn).astype(WIDE)
    return total


def spread_over_tp(total, count):
    return [total] + [swap(total, "tp", count, turn) for turn in range(1, count)]


def sum_over_tp(values, count):
    total = rows_over_tp(values, count).astype(LOW)
    return lax.all_gather(total, "tp", axis=0, tiled=True)


def attend(queries, keys, values, scale):
    scores = mul("xqd,xkd->xqk", queries, keys) * scale
    weights = jnp.exp(scores - jnp.max(scores, -1, keepdims=True))
    probs = weights / jnp.sum(weights, -1, keepdims=True)
    mixed = mul("xqk,xkd->xqd", probs.astype(LOW), values).astype(LOW)
    return probs, mixed


def attend_back(probs, mixed_grad, queries, keys, values, scale):
    values_grad = mul("xqk,xqd->xkd", probs.astype(LOW), mixed_grad)
    prob_grad = mul("xqd,xkd->xqk", mixed_grad, values)
    row_delta = jnp.sum(probs * prob_grad, -1, keepdims=True)
    score_grad = (probs * (prob_grad - row_delta)).astype(LOW)
    queries_grad = mul("xqk,xkd->xqd", score_grad, keys) * scale
    keys_grad = mul("xqk,xqd->xkd", score_grad, queries) * scale
    return queries_grad, keys_grad, values_grad


def pack_kernel(own_experts, place, *refs):
    weights, (*pieces, held, in_sems, out_sems) = refs[:3], refs[3:]
    arriving, leaving = [], []
    for turn, piece in enumerate(pieces):
        start = (place[0] ^ turn) * own_experts
        for kind, weight in enumerate(weights):
            source = weight.at[pl.ds(start, own_experts)]
            target = held.at[turn, pl.ds(kind * own_experts, own_experts)]
            arriving.append(pltpu.make_async_copy(source, target, in_sems.at[3 * turn + kind]))
        leaving.append(pltpu.make_async_copy(held.at[turn], piece, out_sems.at[turn]))
    for copy in arriving:
        copy.start()
    for turn, copy in enumerate(leaving):
        for part in arriving[3 * turn : 3 * turn + 3]:
            part.wait()
        copy.start()
    for copy in leaving:
        copy.wait()


def pack_experts(here, weights, count):
    experts, deep, wide = weights[0].shape
    own_experts = experts // count
    shape = (3 * own_experts, deep, wide)
    anywhere = pl.BlockSpec(memory_space=pl.ANY)
    return pl.pallas_call(
        functools.partial(pack_kernel, own_experts),
        grid_spec=pltpu.PrefetchScalarGridSpec(
            num_scalar_prefetch=1,
            grid=(1,),
            in_specs=[anywhere] * 3,
            out_specs=[anywhere] * count,
            scratch_shapes=[
                pltpu.VMEM((count,) + shape, LOW),
                pltpu.SemaphoreType.DMA((3 * count,)),
                pltpu.SemaphoreType.DMA((count,)),
            ],
        ),
        out_shape=[jax.ShapeDtypeStruct(shape, LOW)] * count,
        compiler_params=pltpu.CompilerParams(vmem_limit_bytes=24 * 2**20),
        cost_estimate=pl.CostEstimate(
            flops=0, bytes_accessed=2 * 2 * 3 * experts * deep * wide, transcendentals=0
        ),
    )(here.reshape(1), *weights)


def unpack_kernel(own_experts, turns, place, *refs):
    count = len(turns)
    pieces, (*outs, held, wide, in_sems, out_sems) = refs[:count], refs[-7:]
    arriving = [
        pltpu.make_async_copy(piece, held.at[i], in_sems.at[i]) for i, piece in enumerate(pieces)
    ]
    leaving = []
    for i, turn in enumerate(turns):
        target = pl.ds((place[0] ^ turn) * own_experts, own_experts)
        for kind, out in enumerate(outs):
            part = pl.ds(kind * own_experts, own_experts)
            leaving.append(
                pltpu.make_async_copy(
                    wide.at[i % 2, part], out.at[target], out_sems.at[3 * i + kind]
                )
            )
    for copy in arriving:
        copy.start()
    for i in range(count):
        arriving[i].wait()
        if i >= 2:
            for copy in leaving[3 * i - 6 : 3 * i - 3]:
                copy.wait()
        wide[i % 2] = held[i].astype(WIDE)
        for copy in leaving[3 * i : 3 * i + 3]:
            copy.start()
    for copy in leaving[-6:] if count > 1 else leaving:
        copy.wait()


def unpack_experts(here, pieces, turns, count, kept):
    blocks, deep, wide = pieces[0].shape
    own_experts = blocks // 3
    anywhere = pl.BlockSpec(memory_space=pl.ANY)
    aliases = {1 + len(turns) + i: i for i in range(3)} if kept else {}
    return pl.pallas_call(
        functools.partial(unpack_kernel, own_experts, turns),
        grid_spec=pltpu.PrefetchScalarGridSpec(
            num_scalar_prefetch=1,
            grid=(1,),
            in_specs=[anywhere] * (len(turns) + len(kept)),
            out_specs=[anywhere] * 3,
            scratch_shapes=[
                pltpu.VMEM((len(turns), blocks, deep, wide), LOW),
                pltpu.VMEM((2, blocks, deep, wide), WIDE),
                pltpu.SemaphoreType.DMA((len(turns),)),
                pltpu.SemaphoreType.DMA((3 * len(turns),)),
            ],
        ),
        out_shape=[jax.ShapeDtypeStruct((count * own_experts, deep, wide), WIDE)] * 3,
        input_output_aliases=aliases,
        compiler_params=pltpu.CompilerParams(vmem_limit_bytes=24 * 2**20),
        cost_estimate=pl.CostEstimate(
            flops=0, bytes_accessed=6 * len(turns) * blocks * deep * wide, transcendentals=0
        ),
    )(here.reshape(1), *pieces, *kept)


def expert_kernel(own_experts, turns, place, *refs):
    count = len(turns)
    tokens, (grad_hot, router, *refs) = refs[:count], refs[count:]
    scratch = refs[-9:]
    rise, fall, token, grad, gated, act, back, in_sems, out_sems = scratch
    sources = len(refs) - 9 - 3 - count
    pieces, (gated_out, act_out, *backs, probs_out) = refs[:sources], refs[sources:-9]
    rows, width = tokens[0].shape
    slices, _, slice_rows, _ = grad_hot.shape
    width_here, hidden_here = pieces[0].shape[1:]
    own_hidden = own_experts * hidden_here
    here = place[0]
    started = []

    def start(source, target):
        copy = pltpu.make_async_copy(source, target, in_sems.at[len(started)])
        copy.start()
        started.append(copy)
        return copy

    def start_tokens(pair):
        return [
            start(tokens[i], token.at[pl.ds(i * rows, rows)]) for i in (2 * pair, 2 * pair + 1)
        ]

    def start_grads(pair):
        return [
            start(
                grad_hot.at[j, here ^ turns[i], :, pl.ds(0, width + LANES)],
                grad.at[pl.ds(i * rows + j * slice_rows, slice_rows)],
            )
            for i in (2 * pair, 2 * pair + 1)
            for j in range(slices)
        ]

    def start_weights(kinds):
        copies = []
        for source, piece in enumerate(pieces):
            deep = pl.ds(pl.multiple_of((here ^ source) * width_here, width_here), width_here)
            for own in range(own_experts):
                near = pl.ds(own * hidden_here, hidden_here)
                far = pl.ds(own_hidden + own * hidden_here, hidden_here)
                targets = (rise.at[deep, near], rise.at[deep, far], fall.at[near, deep])
                for kind in kinds:
                    block = piece.at[kind * own_experts + own]
                    copies.append(start(block, targets[kind]))
        return copies

    token_copies = [start_tokens(0)]
    rise_copies = start_weights((0, 1))
    grad_copies = [start_grads(0)]
    fall_copies = start_weights((2,))
    for pair in range(1, count // 2):
        token_copies.append(start_tokens(pair))
        grad_copies.append(start_grads(pair))
    left = []

    def leave(source, target):
        copy = pltpu.make_async_copy(source, target, out_sems.at[len(left)])
        copy.start()
        left.append(copy)

    lane = lax.broadcasted_iota(jnp.int32, (2 * rows, LANES), 1)
    experts = sources * own_experts
    step = min(512, width)
    for pair in range(count // 2):
        part = pl.ds(2 * pair * rows, 2 * rows)
        for copy in token_copies[pair]:
            copy.wait()
        logits = dot(token[part], router[...], ((1,), (1,)))
        logits = jnp.where(lane < experts, logits, -1e30)
        exp_logits = jnp.exp(logits - jnp.max(logits, -1, keepdims=True))
        probs = exp_logits / jnp.sum(exp_logits, -1, keepdims=True)
        if pair == 0:
            probs_out[...] = probs
            for copy in rise_copies:
                copy.wait()
        acts = []
        for own in range(own_experts):
            near = pl.ds(own * hidden_here, hidden_here)
            far = pl.ds(own_hidden + own * hidden_here, hidden_here)
            acts.append(
                (
                    dot(token[part], rise[:, near], ((1,), (0,))),
                    dot(token[part], rise[:, far], ((1,), (0,))),
                )
            )
        for copy in grad_copies[pair]:
            copy.wait()
        if pair == 0:
            for copy in fall_copies:
                copy.wait()
        hot = grad[part, width : width + LANES].astype(WIDE)
        routed = probs * hot
        placed = jnp.zeros((2 * rows, LANES), WIDE)
        for own, (act_gate, act_up) in enumerate(acts):
            near = pl.ds(own * hidden_here, hidden_here)
            far = pl.ds(own_hidden + own * hidden_here, hidden_here)
            mine = lane == here * own_experts + own
            gates = jnp.sum(jnp.where(mine, routed, 0.0), -1, keepdims=True)
            pulled = dot(grad[part, :width], fall[near, :], ((1,), (1,)))
            sigmoid_gate = jax.nn.sigmoid(act_gate)
            silu = act_gate * sigmoid_gate
            inner = (silu * act_up).astype(LOW).astype(WIDE)
            gate_grads = jnp.sum(inner * pulled, -1, keepdims=True)
            placed = jnp.where(mine, gate_grads * hot, placed)
            gated[part, near] = (inner * gates).astype(LOW)
            inner_grad = pulled * gates
            gate_side = inner_grad * act_up * sigmoid_gate * (1.0 + act_gate * (1.0 - sigmoid_gate))
            act[part, near] = gate_side.astype(LOW)
            act[part, far] = (inner_grad * silu).astype(LOW)
        for first in range(0, width, step):
            columns = pl.ds(first, step)
            back[part, columns] = dot(act[part], rise[columns, :], ((1,), (1,))).astype(LOW)
        back[part, width:] = placed.astype(LOW)
        for i in (2 * pair, 2 * pair + 1):
            leave(back.at[pl.ds(i * rows, rows)], backs[i])
        leave(gated.at[part], gated_out.at[part])
        leave(act.at[part], act_out.at[part])
    for copy in left:
        copy.wait()


def run_experts(turns, here, tokens, grad_hot, router, pieces):
    count = len(turns)
    rows, width = tokens[0].shape
    sources, own_experts = len(pieces), pieces[0].shape[0] // 3
    own_hidden = own_experts * pieces[0].shape[2]
    anywhere = pl.BlockSpec(memory_space=pl.ANY)
    router_spec = pl.BlockSpec((LANES, width), lambda i, p: (0, 0))
    probs_spec = pl.BlockSpec((2 * rows, LANES), lambda i, p: (0, 0))
    shapes = [
        jax.ShapeDtypeStruct((count * rows, own_hidden), LOW),
        jax.ShapeDtypeStruct((count * rows, 2 * own_hidden), LOW),
        *[jax.ShapeDtypeStruct((rows, width + LANES), LOW)] * count,
        jax.ShapeDtypeStruct((2 * rows, LANES), WIDE),
    ]
    copies_in = count * (1 + grad_hot.shape[0]) + 3 * own_experts * sources
    return pl.pallas_call(
        functools.partial(expert_kernel, own_experts, tuple(turns)),
        grid_spec=pltpu.PrefetchScalarGridSpec(
            num_scalar_prefetch=1,
            grid=(1,),
            in_specs=[anywhere] * (count + 1) + [router_spec] + [anywhere] * sources,
            out_specs=[anywhere] * (2 + count) + [probs_spec],
            scratch_shapes=[
                pltpu.VMEM((width, 2 * own_hidden), LOW),
                pltpu.VMEM((own_hidden, width), LOW),
                pltpu.VMEM((count * rows, width), LOW),
                pltpu.VMEM((count * rows, width + LANES), LOW),
                pltpu.VMEM((count * rows, own_hidden), LOW),
                pltpu.VMEM((count * rows, 2 * own_hidden), LOW),
                pltpu.VMEM((count * rows, width + LANES), LOW),
                pltpu.SemaphoreType.DMA((copies_in,)),
                pltpu.SemaphoreType.DMA((2 * count,)),
            ],
        ),
        out_shape=shapes,
        compiler_params=pltpu.CompilerParams(vmem_limit_bytes=40 * 2**20),
        cost_estimate=pl.CostEstimate(
            flops=2 * count * rows * width * own_hidden * 5,
            bytes_accessed=2 * (3 * own_hidden * width + count * rows * width * 4),
            transcendentals=0,
        ),
    )(here.reshape(1), *tokens, grad_hot, router, *pieces)


def mix_kernel(own_experts, sources, place, *refs):
    gated_near, gated_far, pieces = refs[0], refs[1], refs[2 : 2 + sources]
    out, fall, sems = refs[2 + sources :]
    width_here, hidden_here = pieces[0].shape[1:]
    rows = gated_near.shape[0] // 2
    step, here = pl.program_id(0), place[0]

    @pl.when(step == 0)
    def _():
        copies = []
        for source, piece in enumerate(pieces):
            start = pl.multiple_of((here ^ source) * width_here, width_here)
            for own in range(own_experts):
                target = fall.at[pl.ds(own * hidden_here, hidden_here), pl.ds(start, width_here)]
                sem = sems.at[own_experts * source + own]
                block = piece.at[2 * own_experts + own]
                copies.append(pltpu.make_async_copy(block, target, sem))
        for copy in copies:
            copy.start()
        for copy in copies:
            copy.wait()

    gated = jnp.where(step == 0, gated_near[...], gated_far[...])
    swapped = lax.rem(here, 2)
    first = pl.ds(pl.multiple_of(swapped * rows, rows), rows)
    second = pl.ds(pl.multiple_of((1 - swapped) * rows, rows), rows)
    mix = dot(gated, fall[...], ((1,), (0,))).astype(LOW)
    out[first] = mix[:rows]
    out[second] = mix[rows:]


def mix_experts(here, gated_parts, pieces):
    sources, own_experts = len(pieces), pieces[0].shape[0] // 3
    pair_rows, own_hidden = gated_parts[0].shape
    total = pair_rows * sources // 2
    width = sources * pieces[0].shape[1]
    return pl.pallas_call(
        functools.partial(mix_kernel, own_experts, sources),
        grid_spec=pltpu.PrefetchScalarGridSpec(
            num_scalar_prefetch=1,
            grid=(sources // 2,),
            in_specs=[
                pl.BlockSpec((pair_rows, own_hidden), lambda t, p: (0, 0)),
                pl.BlockSpec((pair_rows, own_hidden), lambda t, p: (jnp.maximum(t - 1, 0), 0)),
            ]
            + [pl.BlockSpec(memory_space=pl.ANY)] * sources,
            out_specs=pl.BlockSpec((pair_rows, width), lambda t, p: ((p[0] ^ (2 * t)) // 2, 0)),
            scratch_shapes=[
                pltpu.VMEM((own_hidden, width), LOW),
                pltpu.SemaphoreType.DMA((own_experts * sources,)),
            ],
        ),
        out_shape=jax.ShapeDtypeStruct((total, width), LOW),
        compiler_params=pltpu.CompilerParams(vmem_limit_bytes=56 * 2**20),
        cost_estimate=pl.CostEstimate(
            flops=0, bytes_accessed=own_hidden * width,
            transcendentals=0,
        ),
    )(here.reshape(1), *gated_parts, *pieces)


def project_kernel(first_column, mixed, blocks, out_all, attended, sems):
    count, rows, _ = blocks.shape
    columns, width = out_all.shape
    width_here = width // count
    copies = []
    for source in range(count):
        for i in range(columns // rows):
            block = blocks.at[source, :, pl.ds(first_column + i * width_here, width_here)]
            target = out_all.at[pl.ds(i * rows, rows), pl.ds(source * width_here, width_here)]
            sem = sems.at[source * (columns // rows) + i]
            copies.append(pltpu.make_async_copy(block, target, sem))
    for copy in copies:
        copy.start()
    for copy in copies:
        copy.wait()
    attended[...] = dot(mixed[...], out_all[...], ((1,), (0,))).astype(LOW)


def project(mixed, blocks, first_column, width):
    rows, columns = mixed.shape
    count = blocks.shape[0]
    return pl.pallas_call(
        functools.partial(project_kernel, first_column),
        in_specs=[pl.BlockSpec(memory_space=pltpu.VMEM), pl.BlockSpec(memory_space=pl.ANY)],
        out_specs=[pl.BlockSpec(memory_space=pltpu.VMEM)] * 2,
        scratch_shapes=[pltpu.SemaphoreType.DMA((count * (columns // rows),))],
        out_shape=[
            jax.ShapeDtypeStruct((columns, width), LOW),
            jax.ShapeDtypeStruct((rows, width), LOW),
        ],
        compiler_params=pltpu.CompilerParams(vmem_limit_bytes=32 * 2**20),
        cost_estimate=pl.CostEstimate(
            flops=2 * rows * columns * width,
            bytes_accessed=2 * 2 * columns * width,
            transcendentals=0,
        ),
    )(mixed, blocks)


def join_kernel(seqs, heads, head_dim, moved, *outs):
    for i, out in enumerate(outs):
        part = slice(i * head_dim, (i + 1) * head_dim)
        for head in range(heads):
            units = [2 * seqs * (head // 2) + 2 * seq + head % 2 for seq in range(seqs)]
            total = sum(moved[unit, : out.shape[0], part].astype(WIDE) for unit in units)
            out[:, head * head_dim : (head + 1) * head_dim] = total


def join_projections(moved, rows, seqs, heads, head_dim):
    shape = jax.ShapeDtypeStruct((rows, heads * head_dim), WIDE)
    return pl.pallas_call(
        functools.partial(join_kernel, seqs, heads, head_dim),
        out_shape=[shape] * 3,
        compiler_params=pltpu.CompilerParams(vmem_limit_bytes=32 * 2**20),
        cost_estimate=pl.CostEstimate(
            flops=0, bytes_accessed=2 * moved.size + 12 * rows * heads * head_dim, transcendentals=0
        ),
    )(moved)


def finish_kernel(count, place, *refs):
    normed, refs = refs[:count], refs[count:]
    hidden, mix, inputs, hidden_grad, gain, output, input_grad, grad_all = refs
    rows = normed[0].shape[0]
    for turn in range(count):
        part = pl.ds(pl.multiple_of((place[0] ^ turn) * rows, rows), rows)
        grad_all[part] = normed[turn][...]
    shard_len, seqs, _ = output.shape
    for seq in range(seqs):
        part = slice(seq * shard_len, (seq + 1) * shard_len)
        values = inputs[part]
        inverse = lax.rsqrt(jnp.mean(values * values, -1, keepdims=True) + EPSILON)
        unit = values * inverse
        scaled = grad_all[part].astype(WIDE) * gain[...]
        mean = jnp.mean(scaled * unit, -1, keepdims=True)
        input_grad[:, seq, :] = hidden_grad[part] + inverse * (scaled - unit * mean)
        output[:, seq, :] = (hidden[part] + mix[part].astype(WIDE)).astype(LOW)


def finish(place, normed, hidden, mix, inputs, hidden_grad, gain, seqs):
    count = len(normed)
    rows, width = inputs.shape
    shard_len = rows // seqs
    vmem = pl.BlockSpec(memory_space=pltpu.VMEM)
    smem = pl.BlockSpec(memory_space=pltpu.SMEM)
    return pl.pallas_call(
        functools.partial(finish_kernel, count),
        in_specs=[smem] + [vmem] * (count + 5),
        out_specs=[vmem] * 2,
        scratch_shapes=[pltpu.VMEM((rows, width), LOW)],
        out_shape=[
            jax.ShapeDtypeStruct((shard_len, seqs, width), LOW),
            jax.ShapeDtypeStruct((shard_len, seqs, width), WIDE),
        ],
        compiler_params=pltpu.CompilerParams(vmem_limit_bytes=32 * 2**20),
        cost_estimate=pl.CostEstimate(
            flops=10 * rows * width, bytes_accessed=16 * rows * width, transcendentals=0
        ),
    )(place.reshape(1), *normed, hidden, mix, inputs, hidden_grad, gain)


def second_back_kernel(units, *refs):
    back, hidden, cotangent, gain, router, probs_in, out_all = refs[:7]
    hidden_grad, low_grad, gain_grad, logit_grads, mixed_grad = refs[7:]
    rows, width = hidden.shape
    probs = probs_in[...]
    prob_grads = back[:, width:].astype(WIDE)
    logits = probs * (prob_grads - jnp.sum(probs * prob_grads, -1, keepdims=True))
    logit_grads[...] = logits
    high = logits.astype(LOW)
    rest = (logits - high.astype(WIDE)).astype(LOW)
    normed_grad = back[:, :width].astype(WIDE)
    normed_grad += dot(high, router[...], ((1,), (0,)))
    normed_grad += dot(rest, router[...], ((1,), (0,)))
    values = hidden[...]
    inverse = lax.rsqrt(jnp.mean(values * values, -1, keepdims=True) + EPSILON)
    unit = values * inverse
    gain_grad[...] = jnp.sum(normed_grad * unit, 0, keepdims=True)
    scaled = normed_grad * gain[...]
    mean = jnp.mean(scaled * unit, -1, keepdims=True)
    total = cotangent[...].astype(WIDE) + inverse * (scaled - unit * mean)
    hidden_grad[...] = total
    low_grad[...] = total.astype(LOW)
    mixed = dot(low_grad[...], out_all[...], ((1,), (1,))).astype(LOW)
    if not units:
        mixed_grad[...] = mixed
        return
    _, shard_len, head_dim = mixed_grad.shape
    for unit_number in range(units):
        head, seq = 2 * (unit_number // 4) + unit_number % 2, unit_number // 2 % 2
        part = mixed[seq * shard_len : (seq + 1) * shard_len]
        mixed_grad[unit_number] = part[:, head * head_dim : (head + 1) * head_dim]


def second_back(back, hidden, cotangent, gain, router, probs, out_all, units, head_dim):
    rows, width = hidden.shape
    columns = out_all.shape[0]
    mixed = (units, rows * columns // (units * head_dim), head_dim) if units else (rows, columns)
    vmem = pl.BlockSpec(memory_space=pltpu.VMEM)
    return pl.pallas_call(
        functools.partial(second_back_kernel, units),
        in_specs=[vmem] * 7,
        out_specs=[vmem] * 5,
        out_shape=[
            jax.ShapeDtypeStruct((rows, width), WIDE),
            jax.ShapeDtypeStruct((rows, width), LOW),
            jax.ShapeDtypeStruct((1, width), WIDE),
            jax.ShapeDtypeStruct((rows, LANES), WIDE),
            jax.ShapeDtypeStruct(mixed, LOW),
        ],
        compiler_params=pltpu.CompilerParams(vmem_limit_bytes=24 * 2**20),
        cost_estimate=pl.CostEstimate(
            flops=2 * rows * width * columns, bytes_accessed=4 * rows * width, transcendentals=0
        ),
    )(back, hidden, cotangent, gain, router, probs, out_all)


def pack_heads_kernel(head_dim, *refs):
    weights, (sent, held, in_sems, out_sems) = refs[:3], refs[3:]
    arriving = [pltpu.make_async_copy(w, held.at[i], in_sems.at[i]) for i, w in enumerate(weights)]
    for copy in arriving:
        copy.start()
    leaving = []
    for kind, copy in enumerate(arriving):
        copy.wait()
        for unit in range(sent.shape[0]):
            head = 2 * (unit // 4) + unit % 2
            source = held.at[kind, :, pl.ds(head * head_dim, head_dim)]
            target = sent.at[unit, :, pl.ds(kind * head_dim, head_dim)]
            leaving.append(pltpu.make_async_copy(source, target, out_sems.at[len(leaving)]))
            leaving[-1].start()
    for copy in leaving:
        copy.wait()


def pack_heads(weights, units, head_dim):
    rows, columns = weights[0].shape
    anywhere = pl.BlockSpec(memory_space=pl.ANY)
    return pl.pallas_call(
        functools.partial(pack_heads_kernel, head_dim),
        in_specs=[anywhere] * 3,
        out_specs=anywhere,
        scratch_shapes=[
            pltpu.VMEM((3, rows, columns), LOW),
            pltpu.SemaphoreType.DMA((3,)),
            pltpu.SemaphoreType.DMA((3 * units,)),
        ],
        out_shape=jax.ShapeDtypeStruct((units, rows, 3 * head_dim), LOW),
        compiler_params=pltpu.CompilerParams(vmem_limit_bytes=24 * 2**20),
        cost_estimate=pl.CostEstimate(flops=0, bytes_accessed=rows * columns, transcendentals=0),
    )(*weights)


def unit_norm_kernel(shard_len, width_here, gain_at, place, near, far, unit_in, normed, gain):
    core = lax.rem(place[0], 2)
    chips, _, width = near.shape
    row, lane = shard_len + gain_at // width, gain_at % width
    for other, part in enumerate((near, far)):
        for chip in range(chips):
            start = pl.multiple_of((2 * chip + (core ^ other)) * width_here, width_here)
            piece = part[chip, row : row + 1, lane : lane + width_here]
            gain[:, pl.ds(start, width_here)] = piece.astype(WIDE)
    for other, part in enumerate((near, far)):
        for chip in range(chips):
            rows = pl.ds((other * chips + chip) * shard_len, shard_len)
            low = part[chip, :shard_len]
            values = low.astype(WIDE)
            inverse = lax.rsqrt(jnp.mean(values * values, -1, keepdims=True) + EPSILON)
            unit_in[rows] = low
            normed[rows] = (values * inverse * gain[...]).astype(LOW)


def unit_norm(here, near, far, shard_len, width_here, gain_at):
    chips, _, width = near.shape
    vmem = pl.BlockSpec(memory_space=pltpu.VMEM)
    smem = pl.BlockSpec(memory_space=pltpu.SMEM)
    shape = jax.ShapeDtypeStruct((2 * chips * shard_len, width), LOW)
    return pl.pallas_call(
        functools.partial(unit_norm_kernel, shard_len, width_here, gain_at),
        in_specs=[smem, vmem, vmem],
        out_specs=[vmem] * 2,
        scratch_shapes=[pltpu.VMEM((1, width), WIDE)],
        out_shape=[shape] * 2,
        compiler_params=pltpu.CompilerParams(vmem_limit_bytes=32 * 2**20),
        cost_estimate=pl.CostEstimate(flops=0, bytes_accessed=0, transcendentals=0),
    )(here.reshape(1), near, far)


def weight_grad_kernel(own_experts, count, place, *refs):
    tokens, grads = refs[:count], refs[count : 2 * count]
    act_parts, gated_parts = refs[2 * count : 2 * count + 2], refs[2 * count + 2 : 2 * count + 4]
    pieces, (token, grad, act, gated) = refs[2 * count + 4 : -4], refs[-4:]
    rows = tokens[0].shape[0]
    hidden_here = pieces[0].shape[2]
    split = 2 * rows

    @pl.when(pl.program_id(0) == 0)
    def _():
        for part, source in ((slice(0, split), 0), (slice(split, None), 1)):
            act[part] = act_parts[source][...]
            gated[:, part] = gated_parts[source][...].T

    for turn in range(count):
        part = pl.ds(turn * rows, rows)
        token[part] = tokens[turn][...]
        grad[part] = grads[turn][...].reshape(rows, grad.shape[1])
    rise = dot(token[...], act[...], ((0,), (0,))).astype(LOW)
    fall = dot(gated[...], grad[...], ((1,), (0,))).astype(LOW)
    for turn, piece in enumerate(pieces):

        @pl.when(pl.program_id(0) == turn)
        def _():
            for i in range(2 * own_experts):
                piece[i] = rise[:, i * hidden_here : (i + 1) * hidden_here]
            for i in range(own_experts):
                piece[2 * own_experts + i] = fall[i * hidden_here : (i + 1) * hidden_here]


def weight_grads(here, tokens, grad_hot, act_parts, gated_parts):
    count = len(tokens)
    rows, width = tokens[0].shape
    width_here = width // count
    own_hidden = gated_parts[0].shape[1]
    own_experts = own_hidden // width_here
    hidden_here = own_hidden // own_experts
    total = count * rows
    slices, _, slice_rows, _ = grad_hot.shape

    def grad_spec(turn):
        shape = (slices, 1, slice_rows, width_here)
        return pl.BlockSpec(shape, lambda t, p: (0, p[0] ^ turn, 0, p[0] ^ t))

    def whole(shape):
        return pl.BlockSpec(shape, lambda t, p: (0,) * len(shape))

    shape = (3 * own_experts, width_here, hidden_here)
    return pl.pallas_call(
        functools.partial(weight_grad_kernel, own_experts, count),
        grid_spec=pltpu.PrefetchScalarGridSpec(
            num_scalar_prefetch=1,
            grid=(count,),
            in_specs=[pl.BlockSpec((rows, width_here), lambda t, p: (0, p[0] ^ t))] * count
            + [grad_spec(turn) for turn in range(count)]
            + [whole(part.shape) for part in (*act_parts, *gated_parts)],
            out_specs=[whole(shape)] * count,
            scratch_shapes=[
                pltpu.VMEM((total, width_here), LOW),
                pltpu.VMEM((total, width_here), LOW),
                pltpu.VMEM((total, 2 * own_hidden), LOW),
                pltpu.VMEM((own_hidden, total), LOW),
            ],
        ),
        out_shape=[jax.ShapeDtypeStruct(shape, LOW)] * count,
        compiler_params=pltpu.CompilerParams(vmem_limit_bytes=56 * 2**20),
        cost_estimate=pl.CostEstimate(
            flops=0, bytes_accessed=2 * own_hidden * width,
            transcendentals=0,
        ),
    )(here.reshape(1), *tokens, *([grad_hot] * count), *act_parts, *gated_parts)


def per_device(
    inputs,
    attn_gain,
    w_query,
    w_key,
    w_value,
    query_gain,
    key_gain,
    w_out,
    ffn_gain,
    w_router,
    w_gate,
    w_up,
    w_down,
    routes,
    cotangent,
):
    here = lax.axis_index("ctx")
    shard_len, seqs, width = inputs.shape
    width_here = attn_gain.shape[0]
    ctx_count = width // width_here
    head_dim = query_gain.shape[0]
    columns = w_query.shape[1]
    heads = columns // head_dim
    experts, _, hidden_here = w_gate.shape
    own_experts = experts // ctx_count
    tp_count = lax.axis_size("tp")
    rows = seqs * shard_len
    units = seqs * heads
    length = ctx_count * shard_len
    scale = 1.0 / math.sqrt(head_dim)

    def by_sequence(values):
        return jnp.swapaxes(values, 0, 1).reshape((rows,) + values.shape[2:])

    extra = jnp.concatenate([w_router.T, attn_gain[None, :], ffn_gain[None, :]], 0)
    extra = jnp.pad(extra, ((0, 32 - extra.shape[0]), (0, 0)))

    residual_in = by_sequence(inputs).astype(WIDE)
    grad_low = by_sequence(cotangent)
    frequency = THETA ** (-(jnp.arange(head_dim // 2, dtype=WIDE) * 2.0) / head_dim)
    query_scale, key_scale = query_gain.astype(WIDE), key_gain.astype(WIDE)

    def turned(positions):
        angles = positions.astype(WIDE)[:, None] * frequency
        cosine, sine = jnp.cos(angles), jnp.sin(angles)

        def prepare(values, gain_values):
            return rotate(normalize(values, gain_values), cosine, sine)

        return prepare

    core = here % 2

    def own_core_first(blocks):
        pairs = jnp.swapaxes(blocks.reshape((ctx_count // 2, 2) + blocks.shape[1:]), 0, 1)
        return jnp.where(core == 0, pairs, pairs[::-1])

    def by_ctx(pairs):
        pairs = jnp.where(core == 0, pairs, pairs[::-1])
        return jnp.swapaxes(pairs, 0, 1).reshape((ctx_count,) + pairs.shape[2:])

    def to_units(blocks):
        return own_core_first(trade(blocks, "ctx")).reshape(length, head_dim)

    def from_units(member):
        member = by_ctx(member.reshape(2, ctx_count // 2, shard_len, head_dim))
        moved = trade(member, "ctx").reshape(heads // 2, seqs, 2, shard_len, head_dim)
        return moved.transpose(1, 3, 0, 2, 4).reshape(rows, columns)

    def trade_same_core(values):
        groups = [list(range(i, ctx_count, 2)) for i in range(2)]
        return lax.all_to_all(values, "ctx", 0, 0, tiled=True, axis_index_groups=groups)

    def attention_by_units(sent_pieces):
        chips = ctx_count // 2
        sent = jnp.swapaxes(inputs, 0, 1)
        sent = jnp.broadcast_to(sent[None], (chips // seqs, seqs, shard_len, width))
        rider = extra.reshape(1, -1, width)
        rider_rows = rider.shape[1]
        rider = jnp.pad(rider, ((0, 0), (0, 8 - rider_rows), (0, 0)))
        rider = jnp.broadcast_to(rider, (chips, 8, width))
        sent = jnp.concatenate([sent.reshape(chips, shard_len, width), rider], 1)
        near = trade_same_core(sent)
        sent = pack_heads((w_query, w_key, w_value), units, head_dim)
        sent, near, *sent_pieces = tie(sent, near, *sent_pieces)
        far = swap(near, "ctx", ctx_count, 1)
        unit_weights = trade(sent, "ctx").reshape(width, 3 * head_dim)
        far, *sent_pieces = tie(far, *sent_pieces)
        unit_in, unit_normed = unit_norm(
            here, near, far, shard_len, width_here, experts * width_here
        )
        riders = jnp.stack([part[:, shard_len : shard_len + rider_rows] for part in (near, far)])
        extra_all = by_ctx(riders).reshape(ctx_count, 32, width_here)
        extra_all = jnp.swapaxes(extra_all, 0, 1).reshape(32, width)
        first_gain = extra_all[experts].astype(WIDE)
        projected = jnp.dot(unit_normed, unit_weights, preferred_element_type=WIDE)
        owners = jnp.arange(2)[:, None] ^ core
        owners = (2 * jnp.arange(chips)[None, :] + owners).reshape(ctx_count, 1)
        prepare = turned((owners * shard_len + jnp.arange(shard_len)).reshape(length))
        queries, query_pull = jax.vjp(prepare, projected[:, :head_dim], query_scale)
        keys, key_pull = jax.vjp(prepare, projected[:, head_dim : 2 * head_dim], key_scale)
        parts = [m.astype(LOW)[None] for m in (queries, keys, projected[:, 2 * head_dim :])]
        probs, unit_mixed = attend(*parts, scale)

        def back(mixed_grad, grad_pieces):
            unit_grad = to_units(mixed_grad)[None]
            grads = attend_back(probs, unit_grad, *parts, scale)
            query_grad, query_gain_grad = query_pull(grads[0][0])
            key_grad, key_gain_grad = key_pull(grads[1][0])
            proj_grad = jnp.concatenate([query_grad, key_grad, grads[2][0]], 1).astype(LOW)
            part = dot(proj_grad, unit_weights, ((1,), (1,)))
            unit_input = unit_in.astype(WIDE)
            attn_gain_grad = jnp.sum(part * unit_input * inverse_rms(unit_input), 0)
            part = part.astype(LOW)
            part = part.reshape(2, chips, shard_len, width)
            moved = swap(part[1], "ctx", ctx_count, 1).astype(WIDE)
            part = (part[0].astype(WIDE) + moved).astype(LOW)
            part = trade_same_core(part)
            part, grad_pieces[3], grad_pieces[5] = tie(part, grad_pieces[3], grad_pieces[5])
            part = part.reshape(chips // seqs, seqs, shard_len, width).astype(WIDE)
            part = jnp.sum(part, 0)
            weight_grad = dot(unit_normed, proj_grad, ((0,), (0,))).astype(LOW)

            def owned(weight_grad, gains):
                deep = 3 * head_dim
                rider_rows = -(-gains.shape[1] // (16 * deep)) * 16
                pad = rider_rows * deep - gains.shape[1]
                rider = jnp.pad(gains.astype(LOW), ((0, 0), (0, pad)))
                rider = rider.reshape(ctx_count, rider_rows, deep)
                weight_grad = weight_grad.reshape(ctx_count, width_here, deep)
                moved = trade(jnp.concatenate([weight_grad, rider], 1), "ctx")
                gains_in = moved[:, width_here:].reshape(ctx_count, -1)[:, : gains.shape[1]]
                return moved, gains_in

            part = part.reshape(rows, width)
            gain_grads = attn_gain_grad, query_gain_grad, key_gain_grad
            return part, (weight_grad, owned), gain_grads

        return unit_mixed[0], from_units, back, extra_all, sent_pieces

    def attention_by_tokens(sent_pieces):
        extra_all = jnp.swapaxes(lax.all_gather(extra, "ctx", axis=0), 0, 1).reshape(32, width)
        first_gain = extra_all[experts].astype(WIDE)
        packed = jnp.concatenate([w_query, w_key, w_value], 1)
        packed = lax.all_gather(packed, "ctx", axis=0, tiled=True)
        normed = normalize(residual_in, first_gain).astype(LOW)
        projected = jnp.dot(normed, packed, preferred_element_type=WIDE)
        positions = here * shard_len + jnp.arange(shard_len, dtype=jnp.int32)

        def heads_first(member):
            member = member.reshape(seqs, shard_len, heads, head_dim)
            return member.transpose(0, 2, 1, 3).reshape(units, shard_len, head_dim)

        def tokens_first(member):
            member = member.reshape(seqs, heads, shard_len, head_dim)
            return member.transpose(0, 2, 1, 3).reshape(rows, columns)

        prepare = turned(positions)
        cuts = [heads_first(projected[:, i * columns : (i + 1) * columns]) for i in range(3)]
        queries, query_pull = jax.vjp(prepare, cuts[0], query_scale)
        keys, key_pull = jax.vjp(prepare, cuts[1], key_scale)
        queries = queries.astype(LOW)
        pairs = jnp.concatenate([keys, cuts[2]], -1).astype(LOW)
        pairs = lax.all_gather(pairs, "ctx", axis=1, tiled=True)
        parts = [queries, pairs[..., :head_dim], pairs[..., head_dim:]]
        probs, mixed = attend(*parts, scale)

        def back(mixed_grad, grad_pieces):
            grads = attend_back(probs, heads_first(mixed_grad), *parts, scale)
            moved = jnp.concatenate(grads[1:], -1).astype(LOW)
            moved = lax.psum_scatter(moved, "ctx", scatter_dimension=1, tiled=True).astype(WIDE)
            query_grad, query_gain_grad = query_pull(grads[0])
            key_grad, key_gain_grad = key_pull(moved[..., :head_dim])
            proj_grad = [tokens_first(g) for g in (query_grad, key_grad, moved[..., head_dim:])]
            proj_grad = jnp.concatenate(proj_grad, 1).astype(LOW)
            part = dot(proj_grad, packed, ((1,), (1,)))
            weight_grad = dot(normed, proj_grad, ((0,), (0,))).astype(LOW)

            def owned(weight_grad, gains):
                moved = lax.psum_scatter(weight_grad, "ctx", scatter_dimension=0, tiled=True)
                return moved, trade(gains.astype(LOW), "ctx")

            attn_gain_grad = jnp.sum(part * residual_in * inverse_rms(residual_in), 0)
            gain_grads = attn_gain_grad, query_gain_grad, key_gain_grad
            return part, (weight_grad, owned), gain_grads

        return mixed, tokens_first, back, extra_all, sent_pieces

    by_units = (ctx_count, seqs, heads) == (8, 2, 4)
    expert_ids = jnp.arange(LANES, dtype=jnp.int32)
    hot = jnp.sum((by_sequence(routes)[:, :, None] == expert_ids).astype(WIDE), 1).astype(LOW)
    grad_hot = jnp.concatenate([grad_low, hot], 1)
    sent = pack_experts(here, (w_gate, w_up, w_down), ctx_count)
    local_mixed, to_tokens, attention_back, extra_all, (*sent, grad_hot) = (
        attention_by_units([*sent, grad_hot])
        if by_units
        else attention_by_tokens([*sent, grad_hot])
    )
    first_gain = extra_all[experts].astype(WIDE)
    second_gain = extra_all[experts + 1].astype(WIDE)
    router_rows = jnp.pad(extra_all[:experts], ((0, LANES - experts), (0, 0)))
    stack = columns // rows
    out_cut = jnp.swapaxes(w_out.reshape(stack, rows, width_here), 0, 1)
    out_cut = out_cut.reshape(rows, stack * width_here)
    out_blocks = lax.all_gather(out_cut, "ctx", axis=0)
    grad_hot = lax.all_gather(grad_hot, "ctx", axis=0)[None]

    pieces = list(sent)
    for turn in (1, 2, 4):
        pieces[turn] = swap(sent[turn], "ctx", ctx_count, turn)
    mixed = to_tokens(local_mixed)
    mixed, *pieces = tie(mixed, *pieces)
    for turn in (3, *range(5, ctx_count)):
        pieces[turn] = swap(pieces[turn], "ctx", ctx_count, turn)

    out_all, attended = project(mixed, out_blocks, 0, width)
    attended = sum_over_tp(attended, tp_count)
    attended, pieces[3], *pieces[5:] = tie(attended, pieces[3], *pieces[5:])
    hidden_one = residual_in + attended.astype(WIDE)
    normed_two = normalize(hidden_one, second_gain).astype(LOW)

    token_blocks = [normed_two, swap(normed_two, "ctx", ctx_count, 1)]
    token_blocks += [None] * (ctx_count - 2)
    for turn in range(2, ctx_count, 2):
        token_blocks[turn] = swap(normed_two, "ctx", ctx_count, turn)
    back_parts, gated_parts, act_parts = [], [], []
    for turns in (range(2), range(2, ctx_count)):
        blocks = [token_blocks[turn] for turn in turns]
        gated, act_grad, *backs, probs = run_experts(
            turns, here, blocks, grad_hot, router_rows, pieces
        )
        gated_parts.append(gated)
        act_parts.append(act_grad)
        if turns[0] == 0:
            probs, *token_blocks[2::2] = tie(probs, *token_blocks[2::2])
            for turn in range(2, ctx_count, 2):
                token_blocks[turn + 1] = swap(token_blocks[turn], "ctx", ctx_count, 1)
            router_probs = probs[:rows]
        for i in range(0, len(turns), 2):
            moved = swap(backs[i + 1], "ctx", ctx_count, 1)
            back_sum = backs[i].astype(WIDE) + moved.astype(WIDE)
            if turns[i] == 0:
                back_parts.append(back_sum)
                continue
            back_parts.append(back_sum.astype(LOW))
    *back_parts, act_parts[1], gated_parts[1] = tie(*back_parts, act_parts[1], gated_parts[1])
    for i in range(1, len(back_parts)):
        back_parts[i] = swap(back_parts[i], "ctx", ctx_count, 2 * i)
    grad_pieces = list(weight_grads(here, token_blocks, grad_hot, act_parts, gated_parts))
    mix_part = mix_experts(here, gated_parts, pieces)
    *back_parts, grad_pieces[0], mix_part = tie(*back_parts, grad_pieces[0], mix_part)
    back_total = sum(part.astype(WIDE) for part in back_parts)
    mix_part = lax.psum_scatter(mix_part, "ctx", scatter_dimension=0, tiled=True)
    mix_sum = lax.psum(mix_part, "tp")
    for turn in range(1, ctx_count):
        grad_pieces[turn] = swap(grad_pieces[turn], "ctx", ctx_count, turn)
    back_sum = sum_over_tp(back_total, tp_count)
    back_sum, grad_pieces[1], grad_pieces[2], grad_pieces[4] = tie(
        back_sum, grad_pieces[1], grad_pieces[2], grad_pieces[4]
    )

    hidden_grad, attended_grad, ffn_gain_grad, logit_grads, mixed_grad = second_back(
        back_sum,
        hidden_one,
        grad_low,
        second_gain[None, :],
        router_rows,
        router_probs,
        out_all,
        units if by_units else 0,
        head_dim,
    )
    router_grad = jnp.dot(
        logit_grads[:, :experts].T, normed_two.astype(WIDE), precision=PRECISE
    )
    ffn_gain_grad = ffn_gain_grad[0]
    out_grad = dot(mixed, attended_grad, ((0,), (0,))).astype(LOW)

    normed_part, (weight_grad, owned), gain_grads = attention_back(mixed_grad, grad_pieces)
    normed_part, out_grad = tie(normed_part, out_grad)
    out_w_low = lax.psum_scatter(out_grad, "ctx", scatter_dimension=1, tiled=True)
    some = (0, 1, 2, 3, 4, 5) if ctx_count > 6 else tuple(range(ctx_count))
    rest = tuple(range(len(some), ctx_count))
    unpacked = list(
        unpack_experts(here, [grad_pieces[t] for t in some], some, ctx_count, [])
    )
    attn_gain_grad = gain_grads[0].reshape(ctx_count, width_here)
    head_gain_grad = jnp.concatenate(gain_grads[1:])
    head_gain_grad = jnp.broadcast_to(head_gain_grad, (ctx_count, 2 * head_dim))
    second_grads = jnp.concatenate([ffn_gain_grad[None, :], router_grad], 0)
    second_grads = second_grads.reshape(1 + experts, ctx_count, width_here).swapaxes(0, 1)
    second_grads = second_grads.reshape(ctx_count, -1)
    gain_parts = jnp.concatenate([attn_gain_grad, head_gain_grad, second_grads], 1)
    weight_grad, normed_part = tie(weight_grad, normed_part)
    proj_weight_grad, gain_parts = owned(weight_grad, gain_parts)
    gain_part = jnp.sum(gain_parts.astype(WIDE), 0)
    second_sums = gain_part[width_here + 2 * head_dim :].reshape(1 + experts, width_here)
    gain_part = gain_part[: width_here + 2 * head_dim]
    place = lax.axis_index("tp")
    normed_rows = rows_over_tp(normed_part, tp_count).astype(LOW)
    normed_rows, unpacked[0] = tie(normed_rows, unpacked[0])
    normed_rows = spread_over_tp(normed_rows, tp_count)
    gain_sum = sum(spread_over_tp(gain_part, tp_count))
    output, input_grad = finish(
        place, normed_rows, hidden_one, mix_sum, residual_in, hidden_grad, first_gain[None, :], seqs
    )
    input_grad, out_w_low, *grad_pieces[6:] = tie(input_grad, out_w_low, *grad_pieces[6:])
    router_out, ffn_gain_out = second_sums[1:].T, second_sums[0]
    if rest:
        unpacked = unpack_experts(here, [grad_pieces[t] for t in rest], rest, ctx_count, unpacked)
    gate_out, up_out, down_out = unpacked
    if by_units:
        proj_weight_grad = join_projections(proj_weight_grad, width_here, seqs, heads, head_dim)
    else:
        proj_weight_grad = proj_weight_grad.astype(WIDE).reshape(width_here, 3, columns)
        proj_weight_grad = jnp.swapaxes(proj_weight_grad, 0, 1)
    return (
        output,
        input_grad,
        gain_sum[:width_here],
        proj_weight_grad[0],
        proj_weight_grad[1],
        proj_weight_grad[2],
        gain_sum[width_here : width_here + head_dim],
        gain_sum[width_here + head_dim : width_here + 2 * head_dim],
        out_w_low.astype(WIDE),
        ffn_gain_out,
        router_out,
        gate_out,
        up_out,
        down_out,
    )


def solution(mesh):
    token = P("ctx", None, None)
    placed = (
        token,
        P("ctx"),
        P("ctx", "tp"),
        P("ctx", "tp"),
        P("ctx", "tp"),
        P(),
        P(),
        P("tp", "ctx"),
        P("ctx"),
        P("ctx", None),
        P(None, "ctx", "tp"),
        P(None, "ctx", "tp"),
        P(None, "tp", "ctx"),
        token,
        token,
    )
    given = (
        token,
        token,
        P("ctx"),
        P("ctx", "tp"),
        P("ctx", "tp"),
        P("ctx", "tp"),
        P(),
        P(),
        P("tp", "ctx"),
        P("ctx"),
        P("ctx", None),
        P(None, "ctx", "tp"),
        P(None, "ctx", "tp"),
        P(None, "tp", "ctx"),
    )
    return jax.shard_map(
        per_device, mesh=mesh, in_specs=placed, out_specs=given, check_vma=False
    )
```

```python
import functools
import math

import jax
import jax.numpy as jnp
from jax import lax
from jax.experimental import pallas as pl
from jax.experimental.pallas import tpu as pltpu
from jax.sharding import PartitionSpec as P

EPSILON = 1e-06
THETA = 50000.0
PRECISE = lax.Precision.HIGHEST
LOW = jnp.bfloat16
WIDE = jnp.float32
LANES = 128


def mul(equation, left, right):
    return jnp.einsum(equation, left, right, preferred_element_type=WIDE)


def dot(left, right, over):
    return lax.dot_general(left, right, (over, ((), ())), preferred_element_type=WIDE)


def inverse_rms(values):
    return lax.rsqrt(jnp.mean(values * values, -1, keepdims=True) + EPSILON)


def normalize(values, gain_values):
    return values * inverse_rms(values) * gain_values


def rotate(values, cosine, sine):
    half = values.shape[-1] // 2
    first, second = values[..., :half], values[..., half:]
    return jnp.concatenate([first * cosine - second * sine, second * cosine + first * sine], -1)


def tie(*values):
    return lax.optimization_barrier(values)


def trade(values, axis):
    return lax.all_to_all(values, axis, 0, 0, tiled=True)


def swap(values, axis, count, turn):
    return lax.ppermute(values, axis, [(i, i ^ turn) for i in range(count)])


def block_at(values, number, size, dim=0):
    return lax.dynamic_slice_in_dim(values, number * size, size, dim)


def rows_over_tp(values, count):
    rows = values.shape[0] // count
    place = lax.axis_index("tp")
    values = values.astype(LOW)
    total = block_at(values, place, rows).astype(WIDE)
    for turn in range(1, count):
        total += swap(block_at(values, place ^ turn, rows), "tp", count, turn).astype(WIDE)
    return total


def spread_over_tp(total, count):
    return [total] + [swap(total, "tp", count, turn) for turn in range(1, count)]


def sum_over_tp(values, count):
    total = rows_over_tp(values, count).astype(LOW)
    return lax.all_gather(total, "tp", axis=0, tiled=True)


def attend(queries, keys, values, scale):
    scores = mul("xqd,xkd->xqk", queries, keys) * scale
    weights = jnp.exp(scores - jnp.max(scores, -1, keepdims=True))
    probs = weights / jnp.sum(weights, -1, keepdims=True)
    mixed = mul("xqk,xkd->xqd", probs.astype(LOW), values).astype(LOW)
    return probs, mixed


def attend_back(probs, mixed_grad, queries, keys, values, scale):
    values_grad = mul("xqk,xqd->xkd", probs.astype(LOW), mixed_grad)
    prob_grad = mul("xqd,xkd->xqk", mixed_grad, values)
    row_delta = jnp.sum(probs * prob_grad, -1, keepdims=True)
    score_grad = (probs * (prob_grad - row_delta)).astype(LOW)
    queries_grad = mul("xqk,xkd->xqd", score_grad, keys) * scale
    keys_grad = mul("xqk,xqd->xkd", score_grad, queries) * scale
    return queries_grad, keys_grad, values_grad


def pack_kernel(own_experts, place, *refs):
    weights, (*pieces, held, in_sems, out_sems) = refs[:3], refs[3:]
    arriving, leaving = [], []
    for turn, piece in enumerate(pieces):
        start = (place[0] ^ turn) * own_experts
        for kind, weight in enumerate(weights):
            source = weight.at[pl.ds(start, own_experts)]
            target = held.at[turn, pl.ds(kind * own_experts, own_experts)]
            arriving.append(pltpu.make_async_copy(source, target, in_sems.at[3 * turn + kind]))
        leaving.append(pltpu.make_async_copy(held.at[turn], piece, out_sems.at[turn]))
    for copy in arriving:
        copy.start()
    for turn, copy in enumerate(leaving):
        for part in arriving[3 * turn : 3 * turn + 3]:
            part.wait()
        copy.start()
    for copy in leaving:
        copy.wait()


def pack_experts(here, weights, count):
    experts, deep, wide = weights[0].shape
    own_experts = experts // count
    shape = (3 * own_experts, deep, wide)
    anywhere = pl.BlockSpec(memory_space=pl.ANY)
    return pl.pallas_call(
        functools.partial(pack_kernel, own_experts),
        grid_spec=pltpu.PrefetchScalarGridSpec(
            num_scalar_prefetch=1,
            grid=(1,),
            in_specs=[anywhere] * 3,
            out_specs=[anywhere] * count,
            scratch_shapes=[
                pltpu.VMEM((count,) + shape, LOW),
                pltpu.SemaphoreType.DMA((3 * count,)),
                pltpu.SemaphoreType.DMA((count,)),
            ],
        ),
        out_shape=[jax.ShapeDtypeStruct(shape, LOW)] * count,
        compiler_params=pltpu.CompilerParams(vmem_limit_bytes=24 * 2**20),
        cost_estimate=pl.CostEstimate(
            flops=0, bytes_accessed=2 * 2 * 3 * experts * deep * wide, transcendentals=0
        ),
    )(here.reshape(1), *weights)


def unpack_kernel(own_experts, turns, place, *refs):
    count = len(turns)
    pieces, (*outs, held, wide, in_sems, out_sems) = refs[:count], refs[-7:]
    arriving = [
        pltpu.make_async_copy(piece, held.at[i], in_sems.at[i]) for i, piece in enumerate(pieces)
    ]
    leaving = []
    for i, turn in enumerate(turns):
        target = pl.ds((place[0] ^ turn) * own_experts, own_experts)
        for kind, out in enumerate(outs):
            part = pl.ds(kind * own_experts, own_experts)
            leaving.append(
                pltpu.make_async_copy(
                    wide.at[i % 2, part], out.at[target], out_sems.at[3 * i + kind]
                )
            )
    for copy in arriving:
        copy.start()
    for i in range(count):
        arriving[i].wait()
        if i >= 2:
            for copy in leaving[3 * i - 6 : 3 * i - 3]:
                copy.wait()
        wide[i % 2] = held[i].astype(WIDE)
        for copy in leaving[3 * i : 3 * i + 3]:
            copy.start()
    for copy in leaving[-6:] if count > 1 else leaving:
        copy.wait()


def unpack_experts(here, pieces, turns, count, kept):
    blocks, deep, wide = pieces[0].shape
    own_experts = blocks // 3
    anywhere = pl.BlockSpec(memory_space=pl.ANY)
    aliases = {1 + len(turns) + i: i for i in range(3)} if kept else {}
    return pl.pallas_call(
        functools.partial(unpack_kernel, own_experts, turns),
        grid_spec=pltpu.PrefetchScalarGridSpec(
            num_scalar_prefetch=1,
            grid=(1,),
            in_specs=[anywhere] * (len(turns) + len(kept)),
            out_specs=[anywhere] * 3,
            scratch_shapes=[
                pltpu.VMEM((len(turns), blocks, deep, wide), LOW),
                pltpu.VMEM((2, blocks, deep, wide), WIDE),
                pltpu.SemaphoreType.DMA((len(turns),)),
                pltpu.SemaphoreType.DMA((3 * len(turns),)),
            ],
        ),
        out_shape=[jax.ShapeDtypeStruct((count * own_experts, deep, wide), WIDE)] * 3,
        input_output_aliases=aliases,
        compiler_params=pltpu.CompilerParams(vmem_limit_bytes=24 * 2**20),
        cost_estimate=pl.CostEstimate(
            flops=0, bytes_accessed=6 * len(turns) * blocks * deep * wide, transcendentals=0
        ),
    )(here.reshape(1), *pieces, *kept)


def expert_kernel(own_experts, turns, place, *refs):
    count = len(turns)
    tokens, (grad_hot, router, *refs) = refs[:count], refs[count:]
    scratch = refs[-9:]
    rise, fall, token, grad, gated, act, back, in_sems, out_sems = scratch
    sources = len(refs) - 9 - 3 - count
    pieces, (gated_out, act_out, *backs, probs_out) = refs[:sources], refs[sources:-9]
    rows, width = tokens[0].shape
    slices, _, slice_rows, _ = grad_hot.shape
    width_here, hidden_here = pieces[0].shape[1:]
    own_hidden = own_experts * hidden_here
    here = place[0]
    started = []

    def start(source, target):
        copy = pltpu.make_async_copy(source, target, in_sems.at[len(started)])
        copy.start()
        started.append(copy)
        return copy

    def start_tokens(pair):
        return [
            start(tokens[i], token.at[pl.ds(i * rows, rows)]) for i in (2 * pair, 2 * pair + 1)
        ]

    def start_grads(pair):
        return [
            start(
                grad_hot.at[j, here ^ turns[i], :, pl.ds(0, width + LANES)],
                grad.at[pl.ds(i * rows + j * slice_rows, slice_rows)],
            )
            for i in (2 * pair, 2 * pair + 1)
            for j in range(slices)
        ]

    def start_weights(kinds):
        copies = []
        for source, piece in enumerate(pieces):
            deep = pl.ds(pl.multiple_of((here ^ source) * width_here, width_here), width_here)
            for own in range(own_experts):
                near = pl.ds(own * hidden_here, hidden_here)
                far = pl.ds(own_hidden + own * hidden_here, hidden_here)
                targets = (rise.at[deep, near], rise.at[deep, far], fall.at[near, deep])
                for kind in kinds:
                    block = piece.at[kind * own_experts + own]
                    copies.append(start(block, targets[kind]))
        return copies

    token_copies = [start_tokens(0)]
    rise_copies = start_weights((0, 1))
    grad_copies = [start_grads(0)]
    fall_copies = start_weights((2,))
    for pair in range(1, count // 2):
        token_copies.append(start_tokens(pair))
        grad_copies.append(start_grads(pair))
    left = []

    def leave(source, target):
        copy = pltpu.make_async_copy(source, target, out_sems.at[len(left)])
        copy.start()
        left.append(copy)

    lane = lax.broadcasted_iota(jnp.int32, (2 * rows, LANES), 1)
    experts = sources * own_experts
    step = min(512, width)
    for pair in range(count // 2):
        part = pl.ds(2 * pair * rows, 2 * rows)
        for copy in token_copies[pair]:
            copy.wait()
        logits = dot(token[part], router[...], ((1,), (1,)))
        logits = jnp.where(lane < experts, logits, -1e30)
        exp_logits = jnp.exp(logits - jnp.max(logits, -1, keepdims=True))
        probs = exp_logits / jnp.sum(exp_logits, -1, keepdims=True)
        if pair == 0:
            probs_out[...] = probs
            for copy in rise_copies:
                copy.wait()
        acts = []
        for own in range(own_experts):
            near = pl.ds(own * hidden_here, hidden_here)
            far = pl.ds(own_hidden + own * hidden_here, hidden_here)
            acts.append(
                (
                    dot(token[part], rise[:, near], ((1,), (0,))),
                    dot(token[part], rise[:, far], ((1,), (0,))),
                )
            )
        for copy in grad_copies[pair]:
            copy.wait()
        if pair == 0:
            for copy in fall_copies:
                copy.wait()
        hot = grad[part, width : width + LANES].astype(WIDE)
        routed = probs * hot
        placed = jnp.zeros((2 * rows, LANES), WIDE)
        for own, (act_gate, act_up) in enumerate(acts):
            near = pl.ds(own * hidden_here, hidden_here)
            far = pl.ds(own_hidden + own * hidden_here, hidden_here)
            mine = lane == here * own_experts + own
            gates = jnp.sum(jnp.where(mine, routed, 0.0), -1, keepdims=True)
            pulled = dot(grad[part, :width], fall[near, :], ((1,), (1,)))
            sigmoid_gate = jax.nn.sigmoid(act_gate)
            silu = act_gate * sigmoid_gate
            inner = (silu * act_up).astype(LOW).astype(WIDE)
            gate_grads = jnp.sum(inner * pulled, -1, keepdims=True)
            placed = jnp.where(mine, gate_grads * hot, placed)
            gated[part, near] = (inner * gates).astype(LOW)
            inner_grad = pulled * gates
            gate_side = inner_grad * act_up * sigmoid_gate * (1.0 + act_gate * (1.0 - sigmoid_gate))
            act[part, near] = gate_side.astype(LOW)
            act[part, far] = (inner_grad * silu).astype(LOW)
        for first in range(0, width, step):
            columns = pl.ds(first, step)
            back[part, columns] = dot(act[part], rise[columns, :], ((1,), (1,))).astype(LOW)
        back[part, width:] = placed.astype(LOW)
        for i in (2 * pair, 2 * pair + 1):
            leave(back.at[pl.ds(i * rows, rows)], backs[i])
        leave(gated.at[part], gated_out.at[part])
        leave(act.at[part], act_out.at[part])
    for copy in left:
        copy.wait()


def run_experts(turns, here, tokens, grad_hot, router, pieces):
    count = len(turns)
    rows, width = tokens[0].shape
    sources, own_experts = len(pieces), pieces[0].shape[0] // 3
    own_hidden = own_experts * pieces[0].shape[2]
    anywhere = pl.BlockSpec(memory_space=pl.ANY)
    router_spec = pl.BlockSpec((LANES, width), lambda i, p: (0, 0))
    probs_spec = pl.BlockSpec((2 * rows, LANES), lambda i, p: (0, 0))
    shapes = [
        jax.ShapeDtypeStruct((count * rows, own_hidden), LOW),
        jax.ShapeDtypeStruct((count * rows, 2 * own_hidden), LOW),
        *[jax.ShapeDtypeStruct((rows, width + LANES), LOW)] * count,
        jax.ShapeDtypeStruct((2 * rows, LANES), WIDE),
    ]
    copies_in = count * (1 + grad_hot.shape[0]) + 3 * own_experts * sources
    return pl.pallas_call(
        functools.partial(expert_kernel, own_experts, tuple(turns)),
        grid_spec=pltpu.PrefetchScalarGridSpec(
            num_scalar_prefetch=1,
            grid=(1,),
            in_specs=[anywhere] * (count + 1) + [router_spec] + [anywhere] * sources,
            out_specs=[anywhere] * (2 + count) + [probs_spec],
            scratch_shapes=[
                pltpu.VMEM((width, 2 * own_hidden), LOW),
                pltpu.VMEM((own_hidden, width), LOW),
                pltpu.VMEM((count * rows, width), LOW),
                pltpu.VMEM((count * rows, width + LANES), LOW),
                pltpu.VMEM((count * rows, own_hidden), LOW),
                pltpu.VMEM((count * rows, 2 * own_hidden), LOW),
                pltpu.VMEM((count * rows, width + LANES), LOW),
                pltpu.SemaphoreType.DMA((copies_in,)),
                pltpu.SemaphoreType.DMA((2 * count,)),
            ],
        ),
        out_shape=shapes,
        compiler_params=pltpu.CompilerParams(vmem_limit_bytes=40 * 2**20),
        cost_estimate=pl.CostEstimate(
            flops=2 * count * rows * width * own_hidden * 5,
            bytes_accessed=2 * (3 * own_hidden * width + count * rows * width * 4),
            transcendentals=0,
        ),
    )(here.reshape(1), *tokens, grad_hot, router, *pieces)


def mix_kernel(own_experts, sources, place, *refs):
    gated_near, gated_far, pieces = refs[0], refs[1], refs[2 : 2 + sources]
    out, fall, sems = refs[2 + sources :]
    width_here, hidden_here = pieces[0].shape[1:]
    rows = gated_near.shape[0] // 2
    step, here = pl.program_id(0), place[0]

    @pl.when(step == 0)
    def _():
        copies = []
        for source, piece in enumerate(pieces):
            start = pl.multiple_of((here ^ source) * width_here, width_here)
            for own in range(own_experts):
                target = fall.at[pl.ds(own * hidden_here, hidden_here), pl.ds(start, width_here)]
                sem = sems.at[own_experts * source + own]
                block = piece.at[2 * own_experts + own]
                copies.append(pltpu.make_async_copy(block, target, sem))
        for copy in copies:
            copy.start()
        for copy in copies:
            copy.wait()

    gated = jnp.where(step == 0, gated_near[...], gated_far[...])
    swapped = lax.rem(here, 2)
    first = pl.ds(pl.multiple_of(swapped * rows, rows), rows)
    second = pl.ds(pl.multiple_of((1 - swapped) * rows, rows), rows)
    mix = dot(gated, fall[...], ((1,), (0,))).astype(LOW)
    out[first] = mix[:rows]
    out[second] = mix[rows:]


def mix_experts(here, gated_parts, pieces):
    sources, own_experts = len(pieces), pieces[0].shape[0] // 3
    pair_rows, own_hidden = gated_parts[0].shape
    total = pair_rows * sources // 2
    width = sources * pieces[0].shape[1]
    return pl.pallas_call(
        functools.partial(mix_kernel, own_experts, sources),
        grid_spec=pltpu.PrefetchScalarGridSpec(
            num_scalar_prefetch=1,
            grid=(sources // 2,),
            in_specs=[
                pl.BlockSpec((pair_rows, own_hidden), lambda t, p: (0, 0)),
                pl.BlockSpec((pair_rows, own_hidden), lambda t, p: (jnp.maximum(t - 1, 0), 0)),
            ]
            + [pl.BlockSpec(memory_space=pl.ANY)] * sources,
            out_specs=pl.BlockSpec((pair_rows, width), lambda t, p: ((p[0] ^ (2 * t)) // 2, 0)),
            scratch_shapes=[
                pltpu.VMEM((own_hidden, width), LOW),
                pltpu.SemaphoreType.DMA((own_experts * sources,)),
            ],
        ),
        out_shape=jax.ShapeDtypeStruct((total, width), LOW),
        compiler_params=pltpu.CompilerParams(vmem_limit_bytes=56 * 2**20),
        cost_estimate=pl.CostEstimate(
            flops=0, bytes_accessed=own_hidden * width,
            transcendentals=0,
        ),
    )(here.reshape(1), *gated_parts, *pieces)


def project_kernel(first_column, mixed, blocks, out_all, attended, sems):
    count, rows, _ = blocks.shape
    columns, width = out_all.shape
    width_here = width // count
    copies = []
    for source in range(count):
        for i in range(columns // rows):
            block = blocks.at[source, :, pl.ds(first_column + i * width_here, width_here)]
            target = out_all.at[pl.ds(i * rows, rows), pl.ds(source * width_here, width_here)]
            sem = sems.at[source * (columns // rows) + i]
            copies.append(pltpu.make_async_copy(block, target, sem))
    for copy in copies:
        copy.start()
    for copy in copies:
        copy.wait()
    attended[...] = dot(mixed[...], out_all[...], ((1,), (0,))).astype(LOW)


def project(mixed, blocks, first_column, width):
    rows, columns = mixed.shape
    count = blocks.shape[0]
    return pl.pallas_call(
        functools.partial(project_kernel, first_column),
        in_specs=[pl.BlockSpec(memory_space=pltpu.VMEM), pl.BlockSpec(memory_space=pl.ANY)],
        out_specs=[pl.BlockSpec(memory_space=pltpu.VMEM)] * 2,
        scratch_shapes=[pltpu.SemaphoreType.DMA((count * (columns // rows),))],
        out_shape=[
            jax.ShapeDtypeStruct((columns, width), LOW),
            jax.ShapeDtypeStruct((rows, width), LOW),
        ],
        compiler_params=pltpu.CompilerParams(vmem_limit_bytes=32 * 2**20),
        cost_estimate=pl.CostEstimate(
            flops=2 * rows * columns * width,
            bytes_accessed=2 * 2 * columns * width,
            transcendentals=0,
        ),
    )(mixed, blocks)


def join_kernel(seqs, heads, head_dim, moved, *outs):
    for i, out in enumerate(outs):
        part = slice(i * head_dim, (i + 1) * head_dim)
        for head in range(heads):
            units = [2 * seqs * (head // 2) + 2 * seq + head % 2 for seq in range(seqs)]
            total = sum(moved[unit, : out.shape[0], part].astype(WIDE) for unit in units)
            out[:, head * head_dim : (head + 1) * head_dim] = total


def join_projections(moved, rows, seqs, heads, head_dim):
    shape = jax.ShapeDtypeStruct((rows, heads * head_dim), WIDE)
    return pl.pallas_call(
        functools.partial(join_kernel, seqs, heads, head_dim),
        out_shape=[shape] * 3,
        compiler_params=pltpu.CompilerParams(vmem_limit_bytes=32 * 2**20),
        cost_estimate=pl.CostEstimate(
            flops=0, bytes_accessed=2 * moved.size + 12 * rows * heads * head_dim, transcendentals=0
        ),
    )(moved)


def finish_kernel(count, place, *refs):
    normed, refs = refs[:count], refs[count:]
    hidden, mix, inputs, hidden_grad, gain, output, input_grad, grad_all = refs
    rows = normed[0].shape[0]
    for turn in range(count):
        part = pl.ds(pl.multiple_of((place[0] ^ turn) * rows, rows), rows)
        grad_all[part] = normed[turn][...]
    shard_len, seqs, _ = output.shape
    for seq in range(seqs):
        part = slice(seq * shard_len, (seq + 1) * shard_len)
        values = inputs[part]
        inverse = lax.rsqrt(jnp.mean(values * values, -1, keepdims=True) + EPSILON)
        unit = values * inverse
        scaled = grad_all[part].astype(WIDE) * gain[...]
        mean = jnp.mean(scaled * unit, -1, keepdims=True)
        input_grad[:, seq, :] = hidden_grad[part] + inverse * (scaled - unit * mean)
        output[:, seq, :] = (hidden[part] + mix[part].astype(WIDE)).astype(LOW)


def finish(place, normed, hidden, mix, inputs, hidden_grad, gain, seqs):
    count = len(normed)
    rows, width = inputs.shape
    shard_len = rows // seqs
    vmem = pl.BlockSpec(memory_space=pltpu.VMEM)
    smem = pl.BlockSpec(memory_space=pltpu.SMEM)
    return pl.pallas_call(
        functools.partial(finish_kernel, count),
        in_specs=[smem] + [vmem] * (count + 5),
        out_specs=[vmem] * 2,
        scratch_shapes=[pltpu.VMEM((rows, width), LOW)],
        out_shape=[
            jax.ShapeDtypeStruct((shard_len, seqs, width), LOW),
            jax.ShapeDtypeStruct((shard_len, seqs, width), WIDE),
        ],
        compiler_params=pltpu.CompilerParams(vmem_limit_bytes=32 * 2**20),
        cost_estimate=pl.CostEstimate(
            flops=10 * rows * width, bytes_accessed=16 * rows * width, transcendentals=0
        ),
    )(place.reshape(1), *normed, hidden, mix, inputs, hidden_grad, gain)


def second_back_kernel(units, *refs):
    back, hidden, cotangent, gain, router, probs_in, out_all = refs[:7]
    hidden_grad, low_grad, gain_grad, logit_grads, mixed_grad = refs[7:]
    rows, width = hidden.shape
    probs = probs_in[...]
    prob_grads = back[:, width:].astype(WIDE)
    logits = probs * (prob_grads - jnp.sum(probs * prob_grads, -1, keepdims=True))
    logit_grads[...] = logits
    high = logits.astype(LOW)
    rest = (logits - high.astype(WIDE)).astype(LOW)
    normed_grad = back[:, :width].astype(WIDE)
    normed_grad += dot(high, router[...], ((1,), (0,)))
    normed_grad += dot(rest, router[...], ((1,), (0,)))
    values = hidden[...]
    inverse = lax.rsqrt(jnp.mean(values * values, -1, keepdims=True) + EPSILON)
    unit = values * inverse
    gain_grad[...] = jnp.sum(normed_grad * unit, 0, keepdims=True)
    scaled = normed_grad * gain[...]
    mean = jnp.mean(scaled * unit, -1, keepdims=True)
    total = cotangent[...].astype(WIDE) + inverse * (scaled - unit * mean)
    hidden_grad[...] = total
    low_grad[...] = total.astype(LOW)
    mixed = dot(low_grad[...], out_all[...], ((1,), (1,))).astype(LOW)
    if not units:
        mixed_grad[...] = mixed
        return
    _, shard_len, head_dim = mixed_grad.shape
    for unit_number in range(units):
        head, seq = 2 * (unit_number // 4) + unit_number % 2, unit_number // 2 % 2
        part = mixed[seq * shard_len : (seq + 1) * shard_len]
        mixed_grad[unit_number] = part[:, head * head_dim : (head + 1) * head_dim]


def second_back(back, hidden, cotangent, gain, router, probs, out_all, units, head_dim):
    rows, width = hidden.shape
    columns = out_all.shape[0]
    mixed = (units, rows * columns // (units * head_dim), head_dim) if units else (rows, columns)
    vmem = pl.BlockSpec(memory_space=pltpu.VMEM)
    return pl.pallas_call(
        functools.partial(second_back_kernel, units),
        in_specs=[vmem] * 7,
        out_specs=[vmem] * 5,
        out_shape=[
            jax.ShapeDtypeStruct((rows, width), WIDE),
            jax.ShapeDtypeStruct((rows, width), LOW),
            jax.ShapeDtypeStruct((1, width), WIDE),
            jax.ShapeDtypeStruct((rows, LANES), WIDE),
            jax.ShapeDtypeStruct(mixed, LOW),
        ],
        compiler_params=pltpu.CompilerParams(vmem_limit_bytes=24 * 2**20),
        cost_estimate=pl.CostEstimate(
            flops=2 * rows * width * columns, bytes_accessed=4 * rows * width, transcendentals=0
        ),
    )(back, hidden, cotangent, gain, router, probs, out_all)


def pack_heads_kernel(head_dim, *refs):
    weights, (sent, held, in_sems, out_sems) = refs[:3], refs[3:]
    arriving = [pltpu.make_async_copy(w, held.at[i], in_sems.at[i]) for i, w in enumerate(weights)]
    for copy in arriving:
        copy.start()
    leaving = []
    for kind, copy in enumerate(arriving):
        copy.wait()
        for unit in range(sent.shape[0]):
            head = 2 * (unit // 4) + unit % 2
            source = held.at[kind, :, pl.ds(head * head_dim, head_dim)]
            target = sent.at[unit, :, pl.ds(kind * head_dim, head_dim)]
            leaving.append(pltpu.make_async_copy(source, target, out_sems.at[len(leaving)]))
            leaving[-1].start()
    for copy in leaving:
        copy.wait()


def pack_heads(weights, units, head_dim):
    rows, columns = weights[0].shape
    anywhere = pl.BlockSpec(memory_space=pl.ANY)
    return pl.pallas_call(
        functools.partial(pack_heads_kernel, head_dim),
        in_specs=[anywhere] * 3,
        out_specs=anywhere,
        scratch_shapes=[
            pltpu.VMEM((3, rows, columns), LOW),
            pltpu.SemaphoreType.DMA((3,)),
            pltpu.SemaphoreType.DMA((3 * units,)),
        ],
        out_shape=jax.ShapeDtypeStruct((units, rows, 3 * head_dim), LOW),
        compiler_params=pltpu.CompilerParams(vmem_limit_bytes=24 * 2**20),
        cost_estimate=pl.CostEstimate(flops=0, bytes_accessed=rows * columns, transcendentals=0),
    )(*weights)


def unit_norm_kernel(shard_len, width_here, gain_at, place, near, far, unit_in, normed, gain):
    core = lax.rem(place[0], 2)
    chips, _, width = near.shape
    row, lane = shard_len + gain_at // width, gain_at % width
    for other, part in enumerate((near, far)):
        for chip in range(chips):
            start = pl.multiple_of((2 * chip + (core ^ other)) * width_here, width_here)
            piece = part[chip, row : row + 1, lane : lane + width_here]
            gain[:, pl.ds(start, width_here)] = piece.astype(WIDE)
    for other, part in enumerate((near, far)):
        for chip in range(chips):
            rows = pl.ds((other * chips + chip) * shard_len, shard_len)
            low = part[chip, :shard_len]
            values = low.astype(WIDE)
            inverse = lax.rsqrt(jnp.mean(values * values, -1, keepdims=True) + EPSILON)
            unit_in[rows] = low
            normed[rows] = (values * inverse * gain[...]).astype(LOW)


def unit_norm(here, near, far, shard_len, width_here, gain_at):
    chips, _, width = near.shape
    vmem = pl.BlockSpec(memory_space=pltpu.VMEM)
    smem = pl.BlockSpec(memory_space=pltpu.SMEM)
    shape = jax.ShapeDtypeStruct((2 * chips * shard_len, width), LOW)
    return pl.pallas_call(
        functools.partial(unit_norm_kernel, shard_len, width_here, gain_at),
        in_specs=[smem, vmem, vmem],
        out_specs=[vmem] * 2,
        scratch_shapes=[pltpu.VMEM((1, width), WIDE)],
        out_shape=[shape] * 2,
        compiler_params=pltpu.CompilerParams(vmem_limit_bytes=32 * 2**20),
        cost_estimate=pl.CostEstimate(flops=0, bytes_accessed=0, transcendentals=0),
    )(here.reshape(1), near, far)


def weight_grad_kernel(own_experts, count, place, *refs):
    tokens, grads = refs[:count], refs[count : 2 * count]
    act_parts, gated_parts = refs[2 * count : 2 * count + 2], refs[2 * count + 2 : 2 * count + 4]
    pieces, (token, grad, act, gated) = refs[2 * count + 4 : -4], refs[-4:]
    rows = tokens[0].shape[0]
    hidden_here = pieces[0].shape[2]
    split = 2 * rows

    @pl.when(pl.program_id(0) == 0)
    def _():
        for part, source in ((slice(0, split), 0), (slice(split, None), 1)):
            act[part] = act_parts[source][...]
            gated[:, part] = gated_parts[source][...].T

    for turn in range(count):
        part = pl.ds(turn * rows, rows)
        token[part] = tokens[turn][...]
        grad[part] = grads[turn][...].reshape(rows, grad.shape[1])
    rise = dot(token[...], act[...], ((0,), (0,))).astype(LOW)
    fall = dot(gated[...], grad[...], ((1,), (0,))).astype(LOW)
    for turn, piece in enumerate(pieces):

        @pl.when(pl.program_id(0) == turn)
        def _():
            for i in range(2 * own_experts):
                piece[i] = rise[:, i * hidden_here : (i + 1) * hidden_here]
            for i in range(own_experts):
                piece[2 * own_experts + i] = fall[i * hidden_here : (i + 1) * hidden_here]


def weight_grads(here, tokens, grad_hot, act_parts, gated_parts):
    count = len(tokens)
    rows, width = tokens[0].shape
    width_here = width // count
    own_hidden = gated_parts[0].shape[1]
    own_experts = own_hidden // width_here
    hidden_here = own_hidden // own_experts
    total = count * rows
    slices, _, slice_rows, _ = grad_hot.shape

    def grad_spec(turn):
        shape = (slices, 1, slice_rows, width_here)
        return pl.BlockSpec(shape, lambda t, p: (0, p[0] ^ turn, 0, p[0] ^ t))

    def whole(shape):
        return pl.BlockSpec(shape, lambda t, p: (0,) * len(shape))

    shape = (3 * own_experts, width_here, hidden_here)
    return pl.pallas_call(
        functools.partial(weight_grad_kernel, own_experts, count),
        grid_spec=pltpu.PrefetchScalarGridSpec(
            num_scalar_prefetch=1,
            grid=(count,),
            in_specs=[pl.BlockSpec((rows, width_here), lambda t, p: (0, p[0] ^ t))] * count
            + [grad_spec(turn) for turn in range(count)]
            + [whole(part.shape) for part in (*act_parts, *gated_parts)],
            out_specs=[whole(shape)] * count,
            scratch_shapes=[
                pltpu.VMEM((total, width_here), LOW),
                pltpu.VMEM((total, width_here), LOW),
                pltpu.VMEM((total, 2 * own_hidden), LOW),
                pltpu.VMEM((own_hidden, total), LOW),
            ],
        ),
        out_shape=[jax.ShapeDtypeStruct(shape, LOW)] * count,
        compiler_params=pltpu.CompilerParams(vmem_limit_bytes=56 * 2**20),
        cost_estimate=pl.CostEstimate(
            flops=0, bytes_accessed=2 * own_hidden * width,
            transcendentals=0,
        ),
    )(here.reshape(1), *tokens, *([grad_hot] * count), *act_parts, *gated_parts)


def per_device(
    inputs,
    attn_gain,
    w_query,
    w_key,
    w_value,
    query_gain,
    key_gain,
    w_out,
    ffn_gain,
    w_router,
    w_gate,
    w_up,
    w_down,
    routes,
    cotangent,
):
    here = lax.axis_index("ctx")
    shard_len, seqs, width = inputs.shape
    width_here = attn_gain.shape[0]
    ctx_count = width // width_here
    head_dim = query_gain.shape[0]
    columns = w_query.shape[1]
    heads = columns // head_dim
    experts, _, hidden_here = w_gate.shape
    own_experts = experts // ctx_count
    tp_count = lax.axis_size("tp")
    rows = seqs * shard_len
    units = seqs * heads
    length = ctx_count * shard_len
    scale = 1.0 / math.sqrt(head_dim)

    def by_sequence(values):
        return jnp.swapaxes(values, 0, 1).reshape((rows,) + values.shape[2:])

    extra = jnp.concatenate([w_router.T, attn_gain[None, :], ffn_gain[None, :]], 0)
    extra = jnp.pad(extra, ((0, 32 - extra.shape[0]), (0, 0)))

    residual_in = by_sequence(inputs).astype(WIDE)
    grad_low = by_sequence(cotangent)
    frequency = THETA ** (-(jnp.arange(head_dim // 2, dtype=WIDE) * 2.0) / head_dim)
    query_scale, key_scale = query_gain.astype(WIDE), key_gain.astype(WIDE)

    def turned(positions):
        angles = positions.astype(WIDE)[:, None] * frequency
        cosine, sine = jnp.cos(angles), jnp.sin(angles)

        def prepare(values, gain_values):
            return rotate(normalize(values, gain_values), cosine, sine)

        return prepare

    core = here % 2

    def own_core_first(blocks):
        pairs = jnp.swapaxes(blocks.reshape((ctx_count // 2, 2) + blocks.shape[1:]), 0, 1)
        return jnp.where(core == 0, pairs, pairs[::-1])

    def by_ctx(pairs):
        pairs = jnp.where(core == 0, pairs, pairs[::-1])
        return jnp.swapaxes(pairs, 0, 1).reshape((ctx_count,) + pairs.shape[2:])

    def to_units(blocks):
        return own_core_first(trade(blocks, "ctx")).reshape(length, head_dim)

    def from_units(member):
        member = by_ctx(member.reshape(2, ctx_count // 2, shard_len, head_dim))
        moved = trade(member, "ctx").reshape(heads // 2, seqs, 2, shard_len, head_dim)
        return moved.transpose(1, 3, 0, 2, 4).reshape(rows, columns)

    def trade_same_core(values):
        groups = [list(range(i, ctx_count, 2)) for i in range(2)]
        return lax.all_to_all(values, "ctx", 0, 0, tiled=True, axis_index_groups=groups)

    def attention_by_units(sent_pieces):
        chips = ctx_count // 2
        sent = jnp.swapaxes(inputs, 0, 1)
        sent = jnp.broadcast_to(sent[None], (chips // seqs, seqs, shard_len, width))
        rider = extra.reshape(1, -1, width)
        rider_rows = rider.shape[1]
        rider = jnp.pad(rider, ((0, 0), (0, 8 - rider_rows), (0, 0)))
        rider = jnp.broadcast_to(rider, (chips, 8, width))
        sent = jnp.concatenate([sent.reshape(chips, shard_len, width), rider], 1)
        near = trade_same_core(sent)
        sent = pack_heads((w_query, w_key, w_value), units, head_dim)
        sent, near, *sent_pieces = tie(sent, near, *sent_pieces)
        far = swap(near, "ctx", ctx_count, 1)
        unit_weights = trade(sent, "ctx").reshape(width, 3 * head_dim)
        far, *sent_pieces = tie(far, *sent_pieces)
        unit_in, unit_normed = unit_norm(
            here, near, far, shard_len, width_here, experts * width_here
        )
        riders = jnp.stack([part[:, shard_len : shard_len + rider_rows] for part in (near, far)])
        extra_all = by_ctx(riders).reshape(ctx_count, 32, width_here)
        extra_all = jnp.swapaxes(extra_all, 0, 1).reshape(32, width)
        first_gain = extra_all[experts].astype(WIDE)
        projected = jnp.dot(unit_normed, unit_weights, preferred_element_type=WIDE)
        owners = jnp.arange(2)[:, None] ^ core
        owners = (2 * jnp.arange(chips)[None, :] + owners).reshape(ctx_count, 1)
        prepare = turned((owners * shard_len + jnp.arange(shard_len)).reshape(length))
        queries, query_pull = jax.vjp(prepare, projected[:, :head_dim], query_scale)
        keys, key_pull = jax.vjp(prepare, projected[:, head_dim : 2 * head_dim], key_scale)
        parts = [m.astype(LOW)[None] for m in (queries, keys, projected[:, 2 * head_dim :])]
        probs, unit_mixed = attend(*parts, scale)

        def back(mixed_grad, grad_pieces, gains_of):
            unit_grad = to_units(mixed_grad)[None]
            grads = attend_back(probs, unit_grad, *parts, scale)
            query_grad, query_gain_grad = query_pull(grads[0][0])
            key_grad, key_gain_grad = key_pull(grads[1][0])
            proj_grad = jnp.concatenate([query_grad, key_grad, grads[2][0]], 1).astype(LOW)
            part = dot(proj_grad, unit_weights, ((1,), (1,)))
            unit_input = unit_in.astype(WIDE)
            attn_gain_grad = jnp.sum(part * unit_input * inverse_rms(unit_input), 0)
            part = part.astype(LOW)
            part = part.reshape(2, chips, shard_len, width)
            moved = swap(part[1], "ctx", ctx_count, 1).astype(WIDE)
            part = (part[0].astype(WIDE) + moved).astype(LOW)
            weight_grad = dot(unit_normed, proj_grad, ((0,), (0,))).astype(LOW)
            gains = gains_of(attn_gain_grad, query_gain_grad, key_gain_grad)
            deep = 3 * head_dim
            rider_rows = -(-gains.shape[1] // (16 * deep)) * 16
            rider = jnp.pad(gains.astype(LOW), ((0, 0), (0, rider_rows * deep - gains.shape[1])))
            rider = rider.reshape(ctx_count, rider_rows, deep)
            sent = jnp.concatenate([weight_grad.reshape(ctx_count, width_here, deep), rider], 1)
            part = trade_same_core(part)
            part, sent, grad_pieces[3], grad_pieces[5] = tie(
                part, sent, grad_pieces[3], grad_pieces[5]
            )
            moved = trade(sent, "ctx")
            gains = moved[:, width_here:].reshape(ctx_count, -1)[:, : gains.shape[1]]
            part = part.reshape(chips // seqs, seqs, shard_len, width).astype(WIDE)
            part = jnp.sum(part, 0)
            return part.reshape(rows, width), moved, gains

        return unit_mixed[0], from_units, back, extra_all, sent_pieces

    def attention_by_tokens(sent_pieces):
        extra_all = jnp.swapaxes(lax.all_gather(extra, "ctx", axis=0), 0, 1).reshape(32, width)
        first_gain = extra_all[experts].astype(WIDE)
        packed = jnp.concatenate([w_query, w_key, w_value], 1)
        packed = lax.all_gather(packed, "ctx", axis=0, tiled=True)
        normed = normalize(residual_in, first_gain).astype(LOW)
        projected = jnp.dot(normed, packed, preferred_element_type=WIDE)
        positions = here * shard_len + jnp.arange(shard_len, dtype=jnp.int32)

        def heads_first(member):
            member = member.reshape(seqs, shard_len, heads, head_dim)
            return member.transpose(0, 2, 1, 3).reshape(units, shard_len, head_dim)

        def tokens_first(member):
            member = member.reshape(seqs, heads, shard_len, head_dim)
            return member.transpose(0, 2, 1, 3).reshape(rows, columns)

        prepare = turned(positions)
        cuts = [heads_first(projected[:, i * columns : (i + 1) * columns]) for i in range(3)]
        queries, query_pull = jax.vjp(prepare, cuts[0], query_scale)
        keys, key_pull = jax.vjp(prepare, cuts[1], key_scale)
        queries = queries.astype(LOW)
        pairs = jnp.concatenate([keys, cuts[2]], -1).astype(LOW)
        pairs = lax.all_gather(pairs, "ctx", axis=1, tiled=True)
        parts = [queries, pairs[..., :head_dim], pairs[..., head_dim:]]
        probs, mixed = attend(*parts, scale)

        def back(mixed_grad, grad_pieces, gains_of):
            grads = attend_back(probs, heads_first(mixed_grad), *parts, scale)
            moved = jnp.concatenate(grads[1:], -1).astype(LOW)
            moved = lax.psum_scatter(moved, "ctx", scatter_dimension=1, tiled=True).astype(WIDE)
            query_grad, query_gain_grad = query_pull(grads[0])
            key_grad, key_gain_grad = key_pull(moved[..., :head_dim])
            proj_grad = [tokens_first(g) for g in (query_grad, key_grad, moved[..., head_dim:])]
            proj_grad = jnp.concatenate(proj_grad, 1).astype(LOW)
            part = dot(proj_grad, packed, ((1,), (1,)))
            weight_grad = dot(normed, proj_grad, ((0,), (0,))).astype(LOW)
            attn_gain_grad = jnp.sum(part * residual_in * inverse_rms(residual_in), 0)
            gains = gains_of(attn_gain_grad, query_gain_grad, key_gain_grad)
            moved = lax.psum_scatter(weight_grad, "ctx", scatter_dimension=0, tiled=True)
            return part, moved, trade(gains.astype(LOW), "ctx")

        return mixed, tokens_first, back, extra_all, sent_pieces

    by_units = (ctx_count, seqs, heads) == (8, 2, 4)
    expert_ids = jnp.arange(LANES, dtype=jnp.int32)
    hot = jnp.sum((by_sequence(routes)[:, :, None] == expert_ids).astype(WIDE), 1).astype(LOW)
    grad_hot = jnp.concatenate([grad_low, hot], 1)
    sent = pack_experts(here, (w_gate, w_up, w_down), ctx_count)
    local_mixed, to_tokens, attention_back, extra_all, (*sent, grad_hot) = (
        attention_by_units([*sent, grad_hot])
        if by_units
        else attention_by_tokens([*sent, grad_hot])
    )
    first_gain = extra_all[experts].astype(WIDE)
    second_gain = extra_all[experts + 1].astype(WIDE)
    router_rows = jnp.pad(extra_all[:experts], ((0, LANES - experts), (0, 0)))
    stack = columns // rows
    out_cut = jnp.swapaxes(w_out.reshape(stack, rows, width_here), 0, 1)
    out_cut = out_cut.reshape(rows, stack * width_here)
    out_blocks = lax.all_gather(out_cut, "ctx", axis=0)
    grad_hot = lax.all_gather(grad_hot, "ctx", axis=0)[None]

    pieces = list(sent)
    for turn in (1, 2, 4):
        pieces[turn] = swap(sent[turn], "ctx", ctx_count, turn)
    mixed = to_tokens(local_mixed)
    mixed, *pieces = tie(mixed, *pieces)
    for turn in (3, *range(5, ctx_count)):
        pieces[turn] = swap(pieces[turn], "ctx", ctx_count, turn)

    out_all, attended = project(mixed, out_blocks, 0, width)
    attended = sum_over_tp(attended, tp_count)
    attended, pieces[3], *pieces[5:] = tie(attended, pieces[3], *pieces[5:])
    hidden_one = residual_in + attended.astype(WIDE)
    normed_two = normalize(hidden_one, second_gain).astype(LOW)

    token_blocks = [normed_two, swap(normed_two, "ctx", ctx_count, 1)]
    token_blocks += [None] * (ctx_count - 2)
    for turn in range(2, ctx_count, 2):
        token_blocks[turn] = swap(normed_two, "ctx", ctx_count, turn)
    back_parts, gated_parts, act_parts = [], [], []
    for turns in (range(2), range(2, ctx_count)):
        blocks = [token_blocks[turn] for turn in turns]
        gated, act_grad, *backs, probs = run_experts(
            turns, here, blocks, grad_hot, router_rows, pieces
        )
        gated_parts.append(gated)
        act_parts.append(act_grad)
        if turns[0] == 0:
            probs, *token_blocks[2::2] = tie(probs, *token_blocks[2::2])
            for turn in range(2, ctx_count, 2):
                token_blocks[turn + 1] = swap(token_blocks[turn], "ctx", ctx_count, 1)
            router_probs = probs[:rows]
        for i in range(0, len(turns), 2):
            moved = swap(backs[i + 1], "ctx", ctx_count, 1)
            back_sum = backs[i].astype(WIDE) + moved.astype(WIDE)
            if turns[i] == 0:
                back_parts.append(back_sum)
                continue
            back_parts.append(back_sum.astype(LOW))
    *back_parts, act_parts[1], gated_parts[1] = tie(*back_parts, act_parts[1], gated_parts[1])
    for i in range(1, len(back_parts)):
        back_parts[i] = swap(back_parts[i], "ctx", ctx_count, 2 * i)
    grad_pieces = list(weight_grads(here, token_blocks, grad_hot, act_parts, gated_parts))
    mix_part = mix_experts(here, gated_parts, pieces)
    *back_parts, grad_pieces[0] = tie(*back_parts, grad_pieces[0])
    back_total = sum(part.astype(WIDE) for part in back_parts)
    mix_part = lax.psum_scatter(mix_part, "ctx", scatter_dimension=0, tiled=True)
    mix_sum = lax.psum(mix_part, "tp")
    for turn in range(1, ctx_count):
        grad_pieces[turn] = swap(grad_pieces[turn], "ctx", ctx_count, turn)
    back_sum = sum_over_tp(back_total, tp_count)
    back_sum, grad_pieces[1], grad_pieces[2], grad_pieces[4] = tie(
        back_sum, grad_pieces[1], grad_pieces[2], grad_pieces[4]
    )

    hidden_grad, attended_grad, ffn_gain_grad, logit_grads, mixed_grad = second_back(
        back_sum,
        hidden_one,
        grad_low,
        second_gain[None, :],
        router_rows,
        router_probs,
        out_all,
        units if by_units else 0,
        head_dim,
    )
    router_grad = jnp.dot(
        logit_grads[:, :experts].T, normed_two.astype(WIDE), precision=PRECISE
    )
    ffn_gain_grad = ffn_gain_grad[0]
    out_grad = dot(mixed, attended_grad, ((0,), (0,))).astype(LOW)

    second_grads = jnp.concatenate([ffn_gain_grad[None, :], router_grad], 0)
    second_grads = second_grads.reshape(1 + experts, ctx_count, width_here).swapaxes(0, 1)
    second_grads = second_grads.reshape(ctx_count, -1)

    def gains_of(attn_gain_grad, query_gain_grad, key_gain_grad):
        head_gain_grad = jnp.concatenate([query_gain_grad, key_gain_grad])
        head_gain_grad = jnp.broadcast_to(head_gain_grad, (ctx_count, 2 * head_dim))
        attn_gain_grad = attn_gain_grad.reshape(ctx_count, width_here)
        return jnp.concatenate([attn_gain_grad, head_gain_grad, second_grads], 1)

    normed_part, proj_weight_grad, gain_parts = attention_back(mixed_grad, grad_pieces, gains_of)
    normed_part, out_grad = tie(normed_part, out_grad)
    out_w_low = lax.psum_scatter(out_grad, "ctx", scatter_dimension=1, tiled=True)
    some = (0, 1, 2, 3, 4, 5) if ctx_count > 6 else tuple(range(ctx_count))
    rest = tuple(range(len(some), ctx_count))
    unpacked = list(
        unpack_experts(here, [grad_pieces[t] for t in some], some, ctx_count, [])
    )
    gain_part = jnp.sum(gain_parts.astype(WIDE), 0)
    second_sums = gain_part[width_here + 2 * head_dim :].reshape(1 + experts, width_here)
    gain_part = gain_part[: width_here + 2 * head_dim]
    place = lax.axis_index("tp")
    normed_rows = rows_over_tp(normed_part, tp_count).astype(LOW)
    normed_rows, unpacked[0] = tie(normed_rows, unpacked[0])
    normed_rows = spread_over_tp(normed_rows, tp_count)
    gain_sum = sum(spread_over_tp(gain_part, tp_count))
    output, input_grad = finish(
        place, normed_rows, hidden_one, mix_sum, residual_in, hidden_grad, first_gain[None, :], seqs
    )
    input_grad, out_w_low, *grad_pieces[6:] = tie(input_grad, out_w_low, *grad_pieces[6:])
    router_out, ffn_gain_out = second_sums[1:].T, second_sums[0]
    if rest:
        unpacked = unpack_experts(here, [grad_pieces[t] for t in rest], rest, ctx_count, unpacked)
    gate_out, up_out, down_out = unpacked
    if by_units:
        proj_weight_grad = join_projections(proj_weight_grad, width_here, seqs, heads, head_dim)
    else:
        proj_weight_grad = proj_weight_grad.astype(WIDE).reshape(width_here, 3, columns)
        proj_weight_grad = jnp.swapaxes(proj_weight_grad, 0, 1)
    return (
        output,
        input_grad,
        gain_sum[:width_here],
        proj_weight_grad[0],
        proj_weight_grad[1],
        proj_weight_grad[2],
        gain_sum[width_here : width_here + head_dim],
        gain_sum[width_here + head_dim : width_here + 2 * head_dim],
        out_w_low.astype(WIDE),
        ffn_gain_out,
        router_out,
        gate_out,
        up_out,
        down_out,
    )


def solution(mesh):
    token = P("ctx", None, None)
    placed = (
        token,
        P("ctx"),
        P("ctx", "tp"),
        P("ctx", "tp"),
        P("ctx", "tp"),
        P(),
        P(),
        P("tp", "ctx"),
        P("ctx"),
        P("ctx", None),
        P(None, "ctx", "tp"),
        P(None, "ctx", "tp"),
        P(None, "tp", "ctx"),
        token,
        token,
    )
    given = (
        token,
        token,
        P("ctx"),
        P("ctx", "tp"),
        P("ctx", "tp"),
        P("ctx", "tp"),
        P(),
        P(),
        P("tp", "ctx"),
        P("ctx"),
        P("ctx", None),
        P(None, "ctx", "tp"),
        P(None, "ctx", "tp"),
        P(None, "tp", "ctx"),
    )
    return jax.shard_map(
        per_device, mesh=mesh, in_specs=placed, out_specs=given, check_vma=False
    )
```

```python
import functools
import math

import jax
import jax.numpy as jnp
from jax import lax
from jax.experimental import pallas as pl
from jax.experimental.pallas import tpu as pltpu
from jax.sharding import PartitionSpec as P

EPSILON = 1e-06
THETA = 50000.0
PRECISE = lax.Precision.HIGHEST
LOW = jnp.bfloat16
WIDE = jnp.float32
LANES = 128


def mul(equation, left, right):
    return jnp.einsum(equation, left, right, preferred_element_type=WIDE)


def dot(left, right, over):
    return lax.dot_general(left, right, (over, ((), ())), preferred_element_type=WIDE)


def inverse_rms(values):
    return lax.rsqrt(jnp.mean(values * values, -1, keepdims=True) + EPSILON)


def normalize(values, gain_values):
    return values * inverse_rms(values) * gain_values


def rotate(values, cosine, sine):
    half = values.shape[-1] // 2
    first, second = values[..., :half], values[..., half:]
    return jnp.concatenate([first * cosine - second * sine, second * cosine + first * sine], -1)


def tie(*values):
    return lax.optimization_barrier(values)


def trade(values, axis):
    return lax.all_to_all(values, axis, 0, 0, tiled=True)


def swap(values, axis, count, turn):
    return lax.ppermute(values, axis, [(i, i ^ turn) for i in range(count)])


def block_at(values, number, size, dim=0):
    return lax.dynamic_slice_in_dim(values, number * size, size, dim)


def rows_over_tp(values, count):
    rows = values.shape[0] // count
    place = lax.axis_index("tp")
    values = values.astype(LOW)
    total = block_at(values, place, rows).astype(WIDE)
    for turn in range(1, count):
        total += swap(block_at(values, place ^ turn, rows), "tp", count, turn).astype(WIDE)
    return total


def spread_over_tp(total, count):
    return [total] + [swap(total, "tp", count, turn) for turn in range(1, count)]


def sum_over_tp(values, count):
    total = rows_over_tp(values, count).astype(LOW)
    return lax.all_gather(total, "tp", axis=0, tiled=True)


def attend(queries, keys, values, scale):
    scores = mul("xqd,xkd->xqk", queries, keys) * scale
    weights = jnp.exp(scores - jnp.max(scores, -1, keepdims=True))
    probs = weights / jnp.sum(weights, -1, keepdims=True)
    mixed = mul("xqk,xkd->xqd", probs.astype(LOW), values).astype(LOW)
    return probs, mixed


def attend_back(probs, mixed_grad, queries, keys, values, scale):
    values_grad = mul("xqk,xqd->xkd", probs.astype(LOW), mixed_grad)
    prob_grad = mul("xqd,xkd->xqk", mixed_grad, values)
    row_delta = jnp.sum(probs * prob_grad, -1, keepdims=True)
    score_grad = (probs * (prob_grad - row_delta)).astype(LOW)
    queries_grad = mul("xqk,xkd->xqd", score_grad, keys) * scale
    keys_grad = mul("xqk,xqd->xkd", score_grad, queries) * scale
    return queries_grad, keys_grad, values_grad


def pack_kernel(own_experts, place, *refs):
    weights, (*pieces, held, in_sems, out_sems) = refs[:3], refs[3:]
    arriving, leaving = [], []
    for turn, piece in enumerate(pieces):
        start = (place[0] ^ turn) * own_experts
        for kind, weight in enumerate(weights):
            source = weight.at[pl.ds(start, own_experts)]
            target = held.at[turn, pl.ds(kind * own_experts, own_experts)]
            arriving.append(pltpu.make_async_copy(source, target, in_sems.at[3 * turn + kind]))
        leaving.append(pltpu.make_async_copy(held.at[turn], piece, out_sems.at[turn]))
    for copy in arriving:
        copy.start()
    for turn, copy in enumerate(leaving):
        for part in arriving[3 * turn : 3 * turn + 3]:
            part.wait()
        copy.start()
    for copy in leaving:
        copy.wait()


def pack_experts(here, weights, count):
    experts, deep, wide = weights[0].shape
    own_experts = experts // count
    shape = (3 * own_experts, deep, wide)
    anywhere = pl.BlockSpec(memory_space=pl.ANY)
    return pl.pallas_call(
        functools.partial(pack_kernel, own_experts),
        grid_spec=pltpu.PrefetchScalarGridSpec(
            num_scalar_prefetch=1,
            grid=(1,),
            in_specs=[anywhere] * 3,
            out_specs=[anywhere] * count,
            scratch_shapes=[
                pltpu.VMEM((count,) + shape, LOW),
                pltpu.SemaphoreType.DMA((3 * count,)),
                pltpu.SemaphoreType.DMA((count,)),
            ],
        ),
        out_shape=[jax.ShapeDtypeStruct(shape, LOW)] * count,
        compiler_params=pltpu.CompilerParams(vmem_limit_bytes=24 * 2**20),
        cost_estimate=pl.CostEstimate(
            flops=0, bytes_accessed=2 * 2 * 3 * experts * deep * wide, transcendentals=0
        ),
    )(here.reshape(1), *weights)


def unpack_kernel(own_experts, turns, place, *refs):
    count = len(turns)
    pieces, (*outs, held, wide, in_sems, out_sems) = refs[:count], refs[-7:]
    arriving = [
        pltpu.make_async_copy(piece, held.at[i], in_sems.at[i]) for i, piece in enumerate(pieces)
    ]
    leaving = []
    for i, turn in enumerate(turns):
        target = pl.ds((place[0] ^ turn) * own_experts, own_experts)
        for kind, out in enumerate(outs):
            part = pl.ds(kind * own_experts, own_experts)
            leaving.append(
                pltpu.make_async_copy(
                    wide.at[i % 2, part], out.at[target], out_sems.at[3 * i + kind]
                )
            )
    for copy in arriving:
        copy.start()
    for i in range(count):
        arriving[i].wait()
        if i >= 2:
            for copy in leaving[3 * i - 6 : 3 * i - 3]:
                copy.wait()
        wide[i % 2] = held[i].astype(WIDE)
        for copy in leaving[3 * i : 3 * i + 3]:
            copy.start()
    for copy in leaving[-6:] if count > 1 else leaving:
        copy.wait()


def unpack_experts(here, pieces, turns, count, kept):
    blocks, deep, wide = pieces[0].shape
    own_experts = blocks // 3
    anywhere = pl.BlockSpec(memory_space=pl.ANY)
    aliases = {1 + len(turns) + i: i for i in range(3)} if kept else {}
    return pl.pallas_call(
        functools.partial(unpack_kernel, own_experts, turns),
        grid_spec=pltpu.PrefetchScalarGridSpec(
            num_scalar_prefetch=1,
            grid=(1,),
            in_specs=[anywhere] * (len(turns) + len(kept)),
            out_specs=[anywhere] * 3,
            scratch_shapes=[
                pltpu.VMEM((len(turns), blocks, deep, wide), LOW),
                pltpu.VMEM((2, blocks, deep, wide), WIDE),
                pltpu.SemaphoreType.DMA((len(turns),)),
                pltpu.SemaphoreType.DMA((3 * len(turns),)),
            ],
        ),
        out_shape=[jax.ShapeDtypeStruct((count * own_experts, deep, wide), WIDE)] * 3,
        input_output_aliases=aliases,
        compiler_params=pltpu.CompilerParams(vmem_limit_bytes=24 * 2**20),
        cost_estimate=pl.CostEstimate(
            flops=0, bytes_accessed=6 * len(turns) * blocks * deep * wide, transcendentals=0
        ),
    )(here.reshape(1), *pieces, *kept)


def expert_kernel(own_experts, turns, place, *refs):
    count = len(turns)
    tokens, (grad_hot, router, *refs) = refs[:count], refs[count:]
    scratch = refs[-9:]
    rise, fall, token, grad, gated, act, back, in_sems, out_sems = scratch
    sources = len(refs) - 9 - 3 - count
    pieces, (gated_out, act_out, *backs, probs_out) = refs[:sources], refs[sources:-9]
    rows, width = tokens[0].shape
    slices, _, slice_rows, _ = grad_hot.shape
    width_here, hidden_here = pieces[0].shape[1:]
    own_hidden = own_experts * hidden_here
    here = place[0]
    started = []

    def start(source, target):
        copy = pltpu.make_async_copy(source, target, in_sems.at[len(started)])
        copy.start()
        started.append(copy)
        return copy

    def start_tokens(pair):
        return [
            start(tokens[i], token.at[pl.ds(i * rows, rows)]) for i in (2 * pair, 2 * pair + 1)
        ]

    def start_grads(pair):
        return [
            start(
                grad_hot.at[j, here ^ turns[i], :, pl.ds(0, width + LANES)],
                grad.at[pl.ds(i * rows + j * slice_rows, slice_rows)],
            )
            for i in (2 * pair, 2 * pair + 1)
            for j in range(slices)
        ]

    def start_weights(kinds):
        copies = []
        for source, piece in enumerate(pieces):
            deep = pl.ds(pl.multiple_of((here ^ source) * width_here, width_here), width_here)
            for own in range(own_experts):
                near = pl.ds(own * hidden_here, hidden_here)
                far = pl.ds(own_hidden + own * hidden_here, hidden_here)
                targets = (rise.at[deep, near], rise.at[deep, far], fall.at[near, deep])
                for kind in kinds:
                    block = piece.at[kind * own_experts + own]
                    copies.append(start(block, targets[kind]))
        return copies

    token_copies = [start_tokens(0)]
    rise_copies = start_weights((0, 1))
    grad_copies = [start_grads(0)]
    fall_copies = start_weights((2,))
    for pair in range(1, count // 2):
        token_copies.append(start_tokens(pair))
        grad_copies.append(start_grads(pair))
    left = []

    def leave(source, target):
        copy = pltpu.make_async_copy(source, target, out_sems.at[len(left)])
        copy.start()
        left.append(copy)

    lane = lax.broadcasted_iota(jnp.int32, (2 * rows, LANES), 1)
    experts = sources * own_experts
    step = min(512, width)
    for pair in range(count // 2):
        part = pl.ds(2 * pair * rows, 2 * rows)
        for copy in token_copies[pair]:
            copy.wait()
        logits = dot(token[part], router[...], ((1,), (1,)))
        logits = jnp.where(lane < experts, logits, -1e30)
        exp_logits = jnp.exp(logits - jnp.max(logits, -1, keepdims=True))
        probs = exp_logits / jnp.sum(exp_logits, -1, keepdims=True)
        if pair == 0:
            probs_out[...] = probs
            for copy in rise_copies:
                copy.wait()
        acts = []
        for own in range(own_experts):
            near = pl.ds(own * hidden_here, hidden_here)
            far = pl.ds(own_hidden + own * hidden_here, hidden_here)
            acts.append(
                (
                    dot(token[part], rise[:, near], ((1,), (0,))),
                    dot(token[part], rise[:, far], ((1,), (0,))),
                )
            )
        for copy in grad_copies[pair]:
            copy.wait()
        if pair == 0:
            for copy in fall_copies:
                copy.wait()
        hot = grad[part, width : width + LANES].astype(WIDE)
        routed = probs * hot
        placed = jnp.zeros((2 * rows, LANES), WIDE)
        for own, (act_gate, act_up) in enumerate(acts):
            near = pl.ds(own * hidden_here, hidden_here)
            far = pl.ds(own_hidden + own * hidden_here, hidden_here)
            mine = lane == here * own_experts + own
            gates = jnp.sum(jnp.where(mine, routed, 0.0), -1, keepdims=True)
            pulled = dot(grad[part, :width], fall[near, :], ((1,), (1,)))
            sigmoid_gate = jax.nn.sigmoid(act_gate)
            silu = act_gate * sigmoid_gate
            inner = (silu * act_up).astype(LOW).astype(WIDE)
            gate_grads = jnp.sum(inner * pulled, -1, keepdims=True)
            placed = jnp.where(mine, gate_grads * hot, placed)
            gated[part, near] = (inner * gates).astype(LOW)
            inner_grad = pulled * gates
            gate_side = inner_grad * act_up * sigmoid_gate * (1.0 + act_gate * (1.0 - sigmoid_gate))
            act[part, near] = gate_side.astype(LOW)
            act[part, far] = (inner_grad * silu).astype(LOW)
        for first in range(0, width, step):
            columns = pl.ds(first, step)
            back[part, columns] = dot(act[part], rise[columns, :], ((1,), (1,))).astype(LOW)
        back[part, width:] = placed.astype(LOW)
        for i in (2 * pair, 2 * pair + 1):
            leave(back.at[pl.ds(i * rows, rows)], backs[i])
        leave(gated.at[part], gated_out.at[part])
        leave(act.at[part], act_out.at[part])
    for copy in left:
        copy.wait()


def run_experts(turns, here, tokens, grad_hot, router, pieces):
    count = len(turns)
    rows, width = tokens[0].shape
    sources, own_experts = len(pieces), pieces[0].shape[0] // 3
    own_hidden = own_experts * pieces[0].shape[2]
    anywhere = pl.BlockSpec(memory_space=pl.ANY)
    router_spec = pl.BlockSpec((LANES, width), lambda i, p: (0, 0))
    probs_spec = pl.BlockSpec((2 * rows, LANES), lambda i, p: (0, 0))
    shapes = [
        jax.ShapeDtypeStruct((count * rows, own_hidden), LOW),
        jax.ShapeDtypeStruct((count * rows, 2 * own_hidden), LOW),
        *[jax.ShapeDtypeStruct((rows, width + LANES), LOW)] * count,
        jax.ShapeDtypeStruct((2 * rows, LANES), WIDE),
    ]
    copies_in = count * (1 + grad_hot.shape[0]) + 3 * own_experts * sources
    return pl.pallas_call(
        functools.partial(expert_kernel, own_experts, tuple(turns)),
        grid_spec=pltpu.PrefetchScalarGridSpec(
            num_scalar_prefetch=1,
            grid=(1,),
            in_specs=[anywhere] * (count + 1) + [router_spec] + [anywhere] * sources,
            out_specs=[anywhere] * (2 + count) + [probs_spec],
            scratch_shapes=[
                pltpu.VMEM((width, 2 * own_hidden), LOW),
                pltpu.VMEM((own_hidden, width), LOW),
                pltpu.VMEM((count * rows, width), LOW),
                pltpu.VMEM((count * rows, width + LANES), LOW),
                pltpu.VMEM((count * rows, own_hidden), LOW),
                pltpu.VMEM((count * rows, 2 * own_hidden), LOW),
                pltpu.VMEM((count * rows, width + LANES), LOW),
                pltpu.SemaphoreType.DMA((copies_in,)),
                pltpu.SemaphoreType.DMA((2 * count,)),
            ],
        ),
        out_shape=shapes,
        compiler_params=pltpu.CompilerParams(vmem_limit_bytes=40 * 2**20),
        cost_estimate=pl.CostEstimate(
            flops=2 * count * rows * width * own_hidden * 5,
            bytes_accessed=2 * (3 * own_hidden * width + count * rows * width * 4),
            transcendentals=0,
        ),
    )(here.reshape(1), *tokens, grad_hot, router, *pieces)


def mix_kernel(own_experts, sources, place, *refs):
    gated_near, gated_far, pieces = refs[0], refs[1], refs[2 : 2 + sources]
    out, fall, sems = refs[2 + sources :]
    width_here, hidden_here = pieces[0].shape[1:]
    rows = gated_near.shape[0] // 2
    step, here = pl.program_id(0), place[0]

    @pl.when(step == 0)
    def _():
        copies = []
        for source, piece in enumerate(pieces):
            start = pl.multiple_of((here ^ source) * width_here, width_here)
            for own in range(own_experts):
                target = fall.at[pl.ds(own * hidden_here, hidden_here), pl.ds(start, width_here)]
                sem = sems.at[own_experts * source + own]
                block = piece.at[2 * own_experts + own]
                copies.append(pltpu.make_async_copy(block, target, sem))
        for copy in copies:
            copy.start()
        for copy in copies:
            copy.wait()

    gated = jnp.where(step == 0, gated_near[...], gated_far[...])
    swapped = lax.rem(here, 2)
    first = pl.ds(pl.multiple_of(swapped * rows, rows), rows)
    second = pl.ds(pl.multiple_of((1 - swapped) * rows, rows), rows)
    mix = dot(gated, fall[...], ((1,), (0,))).astype(LOW)
    out[first] = mix[:rows]
    out[second] = mix[rows:]


def mix_experts(here, gated_parts, pieces):
    sources, own_experts = len(pieces), pieces[0].shape[0] // 3
    pair_rows, own_hidden = gated_parts[0].shape
    total = pair_rows * sources // 2
    width = sources * pieces[0].shape[1]
    return pl.pallas_call(
        functools.partial(mix_kernel, own_experts, sources),
        grid_spec=pltpu.PrefetchScalarGridSpec(
            num_scalar_prefetch=1,
            grid=(sources // 2,),
            in_specs=[
                pl.BlockSpec((pair_rows, own_hidden), lambda t, p: (0, 0)),
                pl.BlockSpec((pair_rows, own_hidden), lambda t, p: (jnp.maximum(t - 1, 0), 0)),
            ]
            + [pl.BlockSpec(memory_space=pl.ANY)] * sources,
            out_specs=pl.BlockSpec((pair_rows, width), lambda t, p: ((p[0] ^ (2 * t)) // 2, 0)),
            scratch_shapes=[
                pltpu.VMEM((own_hidden, width), LOW),
                pltpu.SemaphoreType.DMA((own_experts * sources,)),
            ],
        ),
        out_shape=jax.ShapeDtypeStruct((total, width), LOW),
        compiler_params=pltpu.CompilerParams(vmem_limit_bytes=56 * 2**20),
        cost_estimate=pl.CostEstimate(
            flops=0, bytes_accessed=own_hidden * width,
            transcendentals=0,
        ),
    )(here.reshape(1), *gated_parts, *pieces)


def project_kernel(first_column, mixed, blocks, out_all, attended, sems):
    count, rows, _ = blocks.shape
    columns, width = out_all.shape
    width_here = width // count
    copies = []
    for source in range(count):
        for i in range(columns // rows):
            block = blocks.at[source, :, pl.ds(first_column + i * width_here, width_here)]
            target = out_all.at[pl.ds(i * rows, rows), pl.ds(source * width_here, width_here)]
            sem = sems.at[source * (columns // rows) + i]
            copies.append(pltpu.make_async_copy(block, target, sem))
    for copy in copies:
        copy.start()
    for copy in copies:
        copy.wait()
    attended[...] = dot(mixed[...], out_all[...], ((1,), (0,))).astype(LOW)


def project(mixed, blocks, first_column, width):
    rows, columns = mixed.shape
    count = blocks.shape[0]
    return pl.pallas_call(
        functools.partial(project_kernel, first_column),
        in_specs=[pl.BlockSpec(memory_space=pltpu.VMEM), pl.BlockSpec(memory_space=pl.ANY)],
        out_specs=[pl.BlockSpec(memory_space=pltpu.VMEM)] * 2,
        scratch_shapes=[pltpu.SemaphoreType.DMA((count * (columns // rows),))],
        out_shape=[
            jax.ShapeDtypeStruct((columns, width), LOW),
            jax.ShapeDtypeStruct((rows, width), LOW),
        ],
        compiler_params=pltpu.CompilerParams(vmem_limit_bytes=32 * 2**20),
        cost_estimate=pl.CostEstimate(
            flops=2 * rows * columns * width,
            bytes_accessed=2 * 2 * columns * width,
            transcendentals=0,
        ),
    )(mixed, blocks)


def join_kernel(seqs, heads, head_dim, moved, *outs):
    for i, out in enumerate(outs):
        part = slice(i * head_dim, (i + 1) * head_dim)
        for head in range(heads):
            units = [2 * seqs * (head // 2) + 2 * seq + head % 2 for seq in range(seqs)]
            total = sum(moved[unit, : out.shape[0], part].astype(WIDE) for unit in units)
            out[:, head * head_dim : (head + 1) * head_dim] = total


def join_projections(moved, rows, seqs, heads, head_dim):
    shape = jax.ShapeDtypeStruct((rows, heads * head_dim), WIDE)
    return pl.pallas_call(
        functools.partial(join_kernel, seqs, heads, head_dim),
        out_shape=[shape] * 3,
        compiler_params=pltpu.CompilerParams(vmem_limit_bytes=32 * 2**20),
        cost_estimate=pl.CostEstimate(
            flops=0, bytes_accessed=2 * moved.size + 12 * rows * heads * head_dim, transcendentals=0
        ),
    )(moved)


def finish_kernel(count, place, *refs):
    normed, refs = refs[:count], refs[count:]
    hidden, mix, inputs, hidden_grad, gain, output, input_grad, grad_all = refs
    rows = normed[0].shape[0]
    for turn in range(count):
        part = pl.ds(pl.multiple_of((place[0] ^ turn) * rows, rows), rows)
        grad_all[part] = normed[turn][...]
    shard_len, seqs, _ = output.shape
    for seq in range(seqs):
        part = slice(seq * shard_len, (seq + 1) * shard_len)
        values = inputs[part]
        inverse = lax.rsqrt(jnp.mean(values * values, -1, keepdims=True) + EPSILON)
        unit = values * inverse
        scaled = grad_all[part].astype(WIDE) * gain[...]
        mean = jnp.mean(scaled * unit, -1, keepdims=True)
        input_grad[:, seq, :] = hidden_grad[part] + inverse * (scaled - unit * mean)
        output[:, seq, :] = (hidden[part] + mix[part].astype(WIDE)).astype(LOW)


def finish(place, normed, hidden, mix, inputs, hidden_grad, gain, seqs):
    count = len(normed)
    rows, width = inputs.shape
    shard_len = rows // seqs
    vmem = pl.BlockSpec(memory_space=pltpu.VMEM)
    smem = pl.BlockSpec(memory_space=pltpu.SMEM)
    return pl.pallas_call(
        functools.partial(finish_kernel, count),
        in_specs=[smem] + [vmem] * (count + 5),
        out_specs=[vmem] * 2,
        scratch_shapes=[pltpu.VMEM((rows, width), LOW)],
        out_shape=[
            jax.ShapeDtypeStruct((shard_len, seqs, width), LOW),
            jax.ShapeDtypeStruct((shard_len, seqs, width), WIDE),
        ],
        compiler_params=pltpu.CompilerParams(vmem_limit_bytes=32 * 2**20),
        cost_estimate=pl.CostEstimate(
            flops=10 * rows * width, bytes_accessed=16 * rows * width, transcendentals=0
        ),
    )(place.reshape(1), *normed, hidden, mix, inputs, hidden_grad, gain)


def second_back_kernel(units, *refs):
    back, hidden, cotangent, gain, router, probs_in, out_all = refs[:7]
    hidden_grad, low_grad, gain_grad, logit_grads, mixed_grad = refs[7:]
    rows, width = hidden.shape
    probs = probs_in[...]
    prob_grads = back[:, width:].astype(WIDE)
    logits = probs * (prob_grads - jnp.sum(probs * prob_grads, -1, keepdims=True))
    logit_grads[...] = logits
    high = logits.astype(LOW)
    rest = (logits - high.astype(WIDE)).astype(LOW)
    normed_grad = back[:, :width].astype(WIDE)
    normed_grad += dot(high, router[...], ((1,), (0,)))
    normed_grad += dot(rest, router[...], ((1,), (0,)))
    values = hidden[...]
    inverse = lax.rsqrt(jnp.mean(values * values, -1, keepdims=True) + EPSILON)
    unit = values * inverse
    gain_grad[...] = jnp.sum(normed_grad * unit, 0, keepdims=True)
    scaled = normed_grad * gain[...]
    mean = jnp.mean(scaled * unit, -1, keepdims=True)
    total = cotangent[...].astype(WIDE) + inverse * (scaled - unit * mean)
    hidden_grad[...] = total
    low_grad[...] = total.astype(LOW)
    mixed = dot(low_grad[...], out_all[...], ((1,), (1,))).astype(LOW)
    if not units:
        mixed_grad[...] = mixed
        return
    _, shard_len, head_dim = mixed_grad.shape
    for unit_number in range(units):
        head, seq = 2 * (unit_number // 4) + unit_number % 2, unit_number // 2 % 2
        part = mixed[seq * shard_len : (seq + 1) * shard_len]
        mixed_grad[unit_number] = part[:, head * head_dim : (head + 1) * head_dim]


def second_back(back, hidden, cotangent, gain, router, probs, out_all, units, head_dim):
    rows, width = hidden.shape
    columns = out_all.shape[0]
    mixed = (units, rows * columns // (units * head_dim), head_dim) if units else (rows, columns)
    vmem = pl.BlockSpec(memory_space=pltpu.VMEM)
    return pl.pallas_call(
        functools.partial(second_back_kernel, units),
        in_specs=[vmem] * 7,
        out_specs=[vmem] * 5,
        out_shape=[
            jax.ShapeDtypeStruct((rows, width), WIDE),
            jax.ShapeDtypeStruct((rows, width), LOW),
            jax.ShapeDtypeStruct((1, width), WIDE),
            jax.ShapeDtypeStruct((rows, LANES), WIDE),
            jax.ShapeDtypeStruct(mixed, LOW),
        ],
        compiler_params=pltpu.CompilerParams(vmem_limit_bytes=24 * 2**20),
        cost_estimate=pl.CostEstimate(
            flops=2 * rows * width * columns, bytes_accessed=4 * rows * width, transcendentals=0
        ),
    )(back, hidden, cotangent, gain, router, probs, out_all)


def pack_heads_kernel(head_dim, *refs):
    weights, (sent, held, in_sems, out_sems) = refs[:3], refs[3:]
    arriving = [pltpu.make_async_copy(w, held.at[i], in_sems.at[i]) for i, w in enumerate(weights)]
    for copy in arriving:
        copy.start()
    leaving = []
    for kind, copy in enumerate(arriving):
        copy.wait()
        for unit in range(sent.shape[0]):
            head = 2 * (unit // 4) + unit % 2
            source = held.at[kind, :, pl.ds(head * head_dim, head_dim)]
            target = sent.at[unit, :, pl.ds(kind * head_dim, head_dim)]
            leaving.append(pltpu.make_async_copy(source, target, out_sems.at[len(leaving)]))
            leaving[-1].start()
    for copy in leaving:
        copy.wait()


def pack_heads(weights, units, head_dim):
    rows, columns = weights[0].shape
    anywhere = pl.BlockSpec(memory_space=pl.ANY)
    return pl.pallas_call(
        functools.partial(pack_heads_kernel, head_dim),
        in_specs=[anywhere] * 3,
        out_specs=anywhere,
        scratch_shapes=[
            pltpu.VMEM((3, rows, columns), LOW),
            pltpu.SemaphoreType.DMA((3,)),
            pltpu.SemaphoreType.DMA((3 * units,)),
        ],
        out_shape=jax.ShapeDtypeStruct((units, rows, 3 * head_dim), LOW),
        compiler_params=pltpu.CompilerParams(vmem_limit_bytes=24 * 2**20),
        cost_estimate=pl.CostEstimate(flops=0, bytes_accessed=rows * columns, transcendentals=0),
    )(*weights)


def unit_norm_kernel(shard_len, width_here, gain_at, place, near, far, unit_in, normed, gain):
    core = lax.rem(place[0], 2)
    chips, _, width = near.shape
    row, lane = shard_len + gain_at // width, gain_at % width
    for other, part in enumerate((near, far)):
        for chip in range(chips):
            start = pl.multiple_of((2 * chip + (core ^ other)) * width_here, width_here)
            piece = part[chip, row : row + 1, lane : lane + width_here]
            gain[:, pl.ds(start, width_here)] = piece.astype(WIDE)
    for other, part in enumerate((near, far)):
        for chip in range(chips):
            rows = pl.ds((other * chips + chip) * shard_len, shard_len)
            low = part[chip, :shard_len]
            values = low.astype(WIDE)
            inverse = lax.rsqrt(jnp.mean(values * values, -1, keepdims=True) + EPSILON)
            unit_in[rows] = low
            normed[rows] = (values * inverse * gain[...]).astype(LOW)


def unit_norm(here, near, far, shard_len, width_here, gain_at):
    chips, _, width = near.shape
    vmem = pl.BlockSpec(memory_space=pltpu.VMEM)
    smem = pl.BlockSpec(memory_space=pltpu.SMEM)
    shape = jax.ShapeDtypeStruct((2 * chips * shard_len, width), LOW)
    return pl.pallas_call(
        functools.partial(unit_norm_kernel, shard_len, width_here, gain_at),
        in_specs=[smem, vmem, vmem],
        out_specs=[vmem] * 2,
        scratch_shapes=[pltpu.VMEM((1, width), WIDE)],
        out_shape=[shape] * 2,
        compiler_params=pltpu.CompilerParams(vmem_limit_bytes=32 * 2**20),
        cost_estimate=pl.CostEstimate(flops=0, bytes_accessed=0, transcendentals=0),
    )(here.reshape(1), near, far)


def weight_grad_kernel(own_experts, count, place, *refs):
    tokens, grads = refs[:count], refs[count : 2 * count]
    act_parts, gated_parts = refs[2 * count : 2 * count + 2], refs[2 * count + 2 : 2 * count + 4]
    pieces, (token, grad, act, gated) = refs[2 * count + 4 : -4], refs[-4:]
    rows = tokens[0].shape[0]
    hidden_here = pieces[0].shape[2]
    split = 2 * rows

    @pl.when(pl.program_id(0) == 0)
    def _():
        for part, source in ((slice(0, split), 0), (slice(split, None), 1)):
            act[part] = act_parts[source][...]
            gated[:, part] = gated_parts[source][...].T

    for turn in range(count):
        part = pl.ds(turn * rows, rows)
        token[part] = tokens[turn][...]
        grad[part] = grads[turn][...].reshape(rows, grad.shape[1])
    rise = dot(token[...], act[...], ((0,), (0,))).astype(LOW)
    fall = dot(gated[...], grad[...], ((1,), (0,))).astype(LOW)
    for turn, piece in enumerate(pieces):

        @pl.when(pl.program_id(0) == turn)
        def _():
            for i in range(2 * own_experts):
                piece[i] = rise[:, i * hidden_here : (i + 1) * hidden_here]
            for i in range(own_experts):
                piece[2 * own_experts + i] = fall[i * hidden_here : (i + 1) * hidden_here]


def weight_grads(here, tokens, grad_hot, act_parts, gated_parts):
    count = len(tokens)
    rows, width = tokens[0].shape
    width_here = width // count
    own_hidden = gated_parts[0].shape[1]
    own_experts = own_hidden // width_here
    hidden_here = own_hidden // own_experts
    total = count * rows
    slices, _, slice_rows, _ = grad_hot.shape

    def grad_spec(turn):
        shape = (slices, 1, slice_rows, width_here)
        return pl.BlockSpec(shape, lambda t, p: (0, p[0] ^ turn, 0, p[0] ^ t))

    def whole(shape):
        return pl.BlockSpec(shape, lambda t, p: (0,) * len(shape))

    shape = (3 * own_experts, width_here, hidden_here)
    return pl.pallas_call(
        functools.partial(weight_grad_kernel, own_experts, count),
        grid_spec=pltpu.PrefetchScalarGridSpec(
            num_scalar_prefetch=1,
            grid=(count,),
            in_specs=[pl.BlockSpec((rows, width_here), lambda t, p: (0, p[0] ^ t))] * count
            + [grad_spec(turn) for turn in range(count)]
            + [whole(part.shape) for part in (*act_parts, *gated_parts)],
            out_specs=[whole(shape)] * count,
            scratch_shapes=[
                pltpu.VMEM((total, width_here), LOW),
                pltpu.VMEM((total, width_here), LOW),
                pltpu.VMEM((total, 2 * own_hidden), LOW),
                pltpu.VMEM((own_hidden, total), LOW),
            ],
        ),
        out_shape=[jax.ShapeDtypeStruct(shape, LOW)] * count,
        compiler_params=pltpu.CompilerParams(vmem_limit_bytes=56 * 2**20),
        cost_estimate=pl.CostEstimate(
            flops=0, bytes_accessed=2 * own_hidden * width,
            transcendentals=0,
        ),
    )(here.reshape(1), *tokens, *([grad_hot] * count), *act_parts, *gated_parts)


def per_device(
    inputs,
    attn_gain,
    w_query,
    w_key,
    w_value,
    query_gain,
    key_gain,
    w_out,
    ffn_gain,
    w_router,
    w_gate,
    w_up,
    w_down,
    routes,
    cotangent,
):
    here = lax.axis_index("ctx")
    shard_len, seqs, width = inputs.shape
    width_here = attn_gain.shape[0]
    ctx_count = width // width_here
    head_dim = query_gain.shape[0]
    columns = w_query.shape[1]
    heads = columns // head_dim
    experts, _, hidden_here = w_gate.shape
    own_experts = experts // ctx_count
    tp_count = lax.axis_size("tp")
    rows = seqs * shard_len
    units = seqs * heads
    length = ctx_count * shard_len
    scale = 1.0 / math.sqrt(head_dim)

    def by_sequence(values):
        return jnp.swapaxes(values, 0, 1).reshape((rows,) + values.shape[2:])

    extra = jnp.concatenate([w_router.T, attn_gain[None, :], ffn_gain[None, :]], 0)
    extra = jnp.pad(extra, ((0, 32 - extra.shape[0]), (0, 0)))

    residual_in = by_sequence(inputs).astype(WIDE)
    grad_low = by_sequence(cotangent)
    frequency = THETA ** (-(jnp.arange(head_dim // 2, dtype=WIDE) * 2.0) / head_dim)
    query_scale, key_scale = query_gain.astype(WIDE), key_gain.astype(WIDE)

    def turned(positions):
        angles = positions.astype(WIDE)[:, None] * frequency
        cosine, sine = jnp.cos(angles), jnp.sin(angles)

        def prepare(values, gain_values):
            return rotate(normalize(values, gain_values), cosine, sine)

        return prepare

    core = here % 2

    def own_core_first(blocks):
        pairs = jnp.swapaxes(blocks.reshape((ctx_count // 2, 2) + blocks.shape[1:]), 0, 1)
        return jnp.where(core == 0, pairs, pairs[::-1])

    def by_ctx(pairs):
        pairs = jnp.where(core == 0, pairs, pairs[::-1])
        return jnp.swapaxes(pairs, 0, 1).reshape((ctx_count,) + pairs.shape[2:])

    def to_units(blocks):
        return own_core_first(trade(blocks, "ctx")).reshape(length, head_dim)

    def from_units(member):
        member = by_ctx(member.reshape(2, ctx_count // 2, shard_len, head_dim))
        moved = trade(member, "ctx").reshape(heads // 2, seqs, 2, shard_len, head_dim)
        return moved.transpose(1, 3, 0, 2, 4).reshape(rows, columns)

    def trade_same_core(values):
        groups = [list(range(i, ctx_count, 2)) for i in range(2)]
        return lax.all_to_all(values, "ctx", 0, 0, tiled=True, axis_index_groups=groups)

    def attention_by_units(sent_pieces):
        chips = ctx_count // 2
        sent = jnp.swapaxes(inputs, 0, 1)
        sent = jnp.broadcast_to(sent[None], (chips // seqs, seqs, shard_len, width))
        rider = extra.reshape(1, -1, width)
        rider_rows = rider.shape[1]
        rider = jnp.pad(rider, ((0, 0), (0, 8 - rider_rows), (0, 0)))
        rider = jnp.broadcast_to(rider, (chips, 8, width))
        sent = jnp.concatenate([sent.reshape(chips, shard_len, width), rider], 1)
        near = trade_same_core(sent)
        sent = pack_heads((w_query, w_key, w_value), units, head_dim)
        sent, near, *sent_pieces = tie(sent, near, *sent_pieces)
        far = swap(near, "ctx", ctx_count, 1)
        unit_weights = trade(sent, "ctx").reshape(width, 3 * head_dim)
        far, *sent_pieces = tie(far, *sent_pieces)
        unit_in, unit_normed = unit_norm(
            here, near, far, shard_len, width_here, experts * width_here
        )
        riders = jnp.stack([part[:, shard_len : shard_len + rider_rows] for part in (near, far)])
        extra_all = by_ctx(riders).reshape(ctx_count, 32, width_here)
        extra_all = jnp.swapaxes(extra_all, 0, 1).reshape(32, width)
        first_gain = extra_all[experts].astype(WIDE)
        projected = jnp.dot(unit_normed, unit_weights, preferred_element_type=WIDE)
        owners = jnp.arange(2)[:, None] ^ core
        owners = (2 * jnp.arange(chips)[None, :] + owners).reshape(ctx_count, 1)
        prepare = turned((owners * shard_len + jnp.arange(shard_len)).reshape(length))
        queries, query_pull = jax.vjp(prepare, projected[:, :head_dim], query_scale)
        keys, key_pull = jax.vjp(prepare, projected[:, head_dim : 2 * head_dim], key_scale)
        parts = [m.astype(LOW)[None] for m in (queries, keys, projected[:, 2 * head_dim :])]
        probs, unit_mixed = attend(*parts, scale)

        def back(mixed_grad, grad_pieces, gains_of):
            unit_grad = to_units(mixed_grad)[None]
            grads = attend_back(probs, unit_grad, *parts, scale)
            query_grad, query_gain_grad = query_pull(grads[0][0])
            key_grad, key_gain_grad = key_pull(grads[1][0])
            proj_grad = jnp.concatenate([query_grad, key_grad, grads[2][0]], 1).astype(LOW)
            part = dot(proj_grad, unit_weights, ((1,), (1,)))
            unit_input = unit_in.astype(WIDE)
            attn_gain_grad = jnp.sum(part * unit_input * inverse_rms(unit_input), 0)
            part = part.astype(LOW)
            part = part.reshape(2, chips, shard_len, width)
            moved = swap(part[1], "ctx", ctx_count, 1).astype(WIDE)
            part = (part[0].astype(WIDE) + moved).astype(LOW)
            weight_grad = dot(unit_normed, proj_grad, ((0,), (0,))).astype(LOW)
            gains = gains_of(attn_gain_grad, query_gain_grad, key_gain_grad)
            deep = 3 * head_dim
            rider_rows = -(-gains.shape[1] // (16 * deep)) * 16
            rider = jnp.pad(gains.astype(LOW), ((0, 0), (0, rider_rows * deep - gains.shape[1])))
            rider = rider.reshape(ctx_count, rider_rows, deep)
            sent = jnp.concatenate([weight_grad.reshape(ctx_count, width_here, deep), rider], 1)
            part = trade_same_core(part)
            part, sent, grad_pieces[3], grad_pieces[5] = tie(
                part, sent, grad_pieces[3], grad_pieces[5]
            )
            moved = trade(sent, "ctx")
            gains = moved[:, width_here:].reshape(ctx_count, -1)[:, : gains.shape[1]]
            part = part.reshape(chips // seqs, seqs, shard_len, width).astype(WIDE)
            part = jnp.sum(part, 0)
            return part.reshape(rows, width), moved, gains

        return unit_mixed[0], from_units, back, extra_all, sent_pieces

    def attention_by_tokens(sent_pieces):
        extra_all = jnp.swapaxes(lax.all_gather(extra, "ctx", axis=0), 0, 1).reshape(32, width)
        first_gain = extra_all[experts].astype(WIDE)
        packed = jnp.concatenate([w_query, w_key, w_value], 1)
        packed = lax.all_gather(packed, "ctx", axis=0, tiled=True)
        normed = normalize(residual_in, first_gain).astype(LOW)
        projected = jnp.dot(normed, packed, preferred_element_type=WIDE)
        positions = here * shard_len + jnp.arange(shard_len, dtype=jnp.int32)

        def heads_first(member):
            member = member.reshape(seqs, shard_len, heads, head_dim)
            return member.transpose(0, 2, 1, 3).reshape(units, shard_len, head_dim)

        def tokens_first(member):
            member = member.reshape(seqs, heads, shard_len, head_dim)
            return member.transpose(0, 2, 1, 3).reshape(rows, columns)

        prepare = turned(positions)
        cuts = [heads_first(projected[:, i * columns : (i + 1) * columns]) for i in range(3)]
        queries, query_pull = jax.vjp(prepare, cuts[0], query_scale)
        keys, key_pull = jax.vjp(prepare, cuts[1], key_scale)
        queries = queries.astype(LOW)
        pairs = jnp.concatenate([keys, cuts[2]], -1).astype(LOW)
        pairs = lax.all_gather(pairs, "ctx", axis=1, tiled=True)
        parts = [queries, pairs[..., :head_dim], pairs[..., head_dim:]]
        probs, mixed = attend(*parts, scale)

        def back(mixed_grad, grad_pieces, gains_of):
            grads = attend_back(probs, heads_first(mixed_grad), *parts, scale)
            moved = jnp.concatenate(grads[1:], -1).astype(LOW)
            moved = lax.psum_scatter(moved, "ctx", scatter_dimension=1, tiled=True).astype(WIDE)
            query_grad, query_gain_grad = query_pull(grads[0])
            key_grad, key_gain_grad = key_pull(moved[..., :head_dim])
            proj_grad = [tokens_first(g) for g in (query_grad, key_grad, moved[..., head_dim:])]
            proj_grad = jnp.concatenate(proj_grad, 1).astype(LOW)
            part = dot(proj_grad, packed, ((1,), (1,)))
            weight_grad = dot(normed, proj_grad, ((0,), (0,))).astype(LOW)
            attn_gain_grad = jnp.sum(part * residual_in * inverse_rms(residual_in), 0)
            gains = gains_of(attn_gain_grad, query_gain_grad, key_gain_grad)
            moved = lax.psum_scatter(weight_grad, "ctx", scatter_dimension=0, tiled=True)
            return part, moved, trade(gains.astype(LOW), "ctx")

        return mixed, tokens_first, back, extra_all, sent_pieces

    by_units = (ctx_count, seqs, heads) == (8, 2, 4)
    expert_ids = jnp.arange(LANES, dtype=jnp.int32)
    hot = jnp.sum((by_sequence(routes)[:, :, None] == expert_ids).astype(WIDE), 1).astype(LOW)
    grad_hot = jnp.concatenate([grad_low, hot], 1)
    sent = pack_experts(here, (w_gate, w_up, w_down), ctx_count)
    local_mixed, to_tokens, attention_back, extra_all, (*sent, grad_hot) = (
        attention_by_units([*sent, grad_hot])
        if by_units
        else attention_by_tokens([*sent, grad_hot])
    )
    first_gain = extra_all[experts].astype(WIDE)
    second_gain = extra_all[experts + 1].astype(WIDE)
    router_rows = jnp.pad(extra_all[:experts], ((0, LANES - experts), (0, 0)))
    stack = columns // rows
    out_cut = jnp.swapaxes(w_out.reshape(stack, rows, width_here), 0, 1)
    out_cut = out_cut.reshape(rows, stack * width_here)
    out_blocks = lax.all_gather(out_cut, "ctx", axis=0)
    grad_hot = lax.all_gather(grad_hot, "ctx", axis=0)[None]

    pieces = list(sent)
    for turn in (1, 2, 4):
        pieces[turn] = swap(sent[turn], "ctx", ctx_count, turn)
    mixed = to_tokens(local_mixed)
    mixed, *pieces = tie(mixed, *pieces)
    for turn in (3, *range(5, ctx_count)):
        pieces[turn] = swap(pieces[turn], "ctx", ctx_count, turn)

    out_all, attended = project(mixed, out_blocks, 0, width)
    attended = sum_over_tp(attended, tp_count)
    attended, pieces[3], *pieces[5:] = tie(attended, pieces[3], *pieces[5:])
    hidden_one = residual_in + attended.astype(WIDE)
    normed_two = normalize(hidden_one, second_gain).astype(LOW)

    token_blocks = [normed_two, swap(normed_two, "ctx", ctx_count, 1)]
    token_blocks += [None] * (ctx_count - 2)
    for turn in range(2, ctx_count, 2):
        token_blocks[turn] = swap(normed_two, "ctx", ctx_count, turn)
    back_parts, gated_parts, act_parts = [], [], []
    for turns in (range(2), range(2, ctx_count)):
        blocks = [token_blocks[turn] for turn in turns]
        gated, act_grad, *backs, probs = run_experts(
            turns, here, blocks, grad_hot, router_rows, pieces
        )
        gated_parts.append(gated)
        act_parts.append(act_grad)
        if turns[0] == 0:
            probs, *token_blocks[2::2] = tie(probs, *token_blocks[2::2])
            for turn in range(2, ctx_count, 2):
                token_blocks[turn + 1] = swap(token_blocks[turn], "ctx", ctx_count, 1)
            router_probs = probs[:rows]
        for i in range(0, len(turns), 2):
            moved = swap(backs[i + 1], "ctx", ctx_count, 1)
            back_sum = backs[i].astype(WIDE) + moved.astype(WIDE)
            if turns[i] == 0:
                back_parts.append(back_sum)
                continue
            back_parts.append(back_sum.astype(LOW))
    *back_parts, act_parts[1], gated_parts[1] = tie(*back_parts, act_parts[1], gated_parts[1])
    for i in range(1, len(back_parts)):
        back_parts[i] = swap(back_parts[i], "ctx", ctx_count, 2 * i)
    grad_pieces = list(weight_grads(here, token_blocks, grad_hot, act_parts, gated_parts))
    mix_part = mix_experts(here, gated_parts, pieces)
    *back_parts, grad_pieces[0] = tie(*back_parts, grad_pieces[0])
    back_total = sum(part.astype(WIDE) for part in back_parts)
    mix_part = lax.psum_scatter(mix_part, "ctx", scatter_dimension=0, tiled=True)
    mix_sum = lax.psum(mix_part, "tp")
    for turn in range(1, ctx_count):
        grad_pieces[turn] = swap(grad_pieces[turn], "ctx", ctx_count, turn)
    back_sum = sum_over_tp(back_total, tp_count)
    back_sum, grad_pieces[1], grad_pieces[2], grad_pieces[4] = tie(
        back_sum, grad_pieces[1], grad_pieces[2], grad_pieces[4]
    )

    hidden_grad, attended_grad, ffn_gain_grad, logit_grads, mixed_grad = second_back(
        back_sum,
        hidden_one,
        grad_low,
        second_gain[None, :],
        router_rows,
        router_probs,
        out_all,
        units if by_units else 0,
        head_dim,
    )
    router_grad = jnp.dot(
        logit_grads[:, :experts].T, normed_two.astype(WIDE), precision=PRECISE
    )
    ffn_gain_grad = ffn_gain_grad[0]
    out_grad = dot(mixed, attended_grad, ((0,), (0,))).astype(LOW)

    second_grads = jnp.concatenate([ffn_gain_grad[None, :], router_grad], 0)
    second_grads = second_grads.reshape(1 + experts, ctx_count, width_here).swapaxes(0, 1)
    second_grads = second_grads.reshape(ctx_count, -1)

    def gains_of(attn_gain_grad, query_gain_grad, key_gain_grad):
        head_gain_grad = jnp.concatenate([query_gain_grad, key_gain_grad])
        head_gain_grad = jnp.broadcast_to(head_gain_grad, (ctx_count, 2 * head_dim))
        attn_gain_grad = attn_gain_grad.reshape(ctx_count, width_here)
        return jnp.concatenate([attn_gain_grad, head_gain_grad, second_grads], 1)

    normed_part, proj_weight_grad, gain_parts = attention_back(mixed_grad, grad_pieces, gains_of)
    normed_part, out_grad = tie(normed_part, out_grad)
    out_w_low = lax.psum_scatter(out_grad, "ctx", scatter_dimension=1, tiled=True)
    some = (0, 1, 2, 3, 4, 5) if ctx_count > 6 else tuple(range(ctx_count))
    rest = tuple(range(len(some), ctx_count))
    unpacked = list(
        unpack_experts(here, [grad_pieces[t] for t in some], some, ctx_count, [])
    )
    gain_part = jnp.sum(gain_parts.astype(WIDE), 0)
    second_sums = gain_part[width_here + 2 * head_dim :].reshape(1 + experts, width_here)
    gain_part = gain_part[: width_here + 2 * head_dim]
    place = lax.axis_index("tp")
    normed_rows = rows_over_tp(normed_part, tp_count).astype(LOW)
    normed_rows, unpacked[0] = tie(normed_rows, unpacked[0])
    normed_rows = spread_over_tp(normed_rows, tp_count)
    gain_sum = sum(spread_over_tp(gain_part, tp_count))
    output, input_grad = finish(
        place, normed_rows, hidden_one, mix_sum, residual_in, hidden_grad, first_gain[None, :], seqs
    )
    input_grad, *grad_pieces[6:] = tie(input_grad, *grad_pieces[6:])
    router_out, ffn_gain_out = second_sums[1:].T, second_sums[0]
    if rest:
        unpacked = unpack_experts(here, [grad_pieces[t] for t in rest], rest, ctx_count, unpacked)
    gate_out, up_out, down_out = unpacked
    gate_out, out_w_low = tie(gate_out, out_w_low)
    if by_units:
        proj_weight_grad = join_projections(proj_weight_grad, width_here, seqs, heads, head_dim)
    else:
        proj_weight_grad = proj_weight_grad.astype(WIDE).reshape(width_here, 3, columns)
        proj_weight_grad = jnp.swapaxes(proj_weight_grad, 0, 1)
    return (
        output,
        input_grad,
        gain_sum[:width_here],
        proj_weight_grad[0],
        proj_weight_grad[1],
        proj_weight_grad[2],
        gain_sum[width_here : width_here + head_dim],
        gain_sum[width_here + head_dim : width_here + 2 * head_dim],
        out_w_low.astype(WIDE),
        ffn_gain_out,
        router_out,
        gate_out,
        up_out,
        down_out,
    )


def solution(mesh):
    token = P("ctx", None, None)
    placed = (
        token,
        P("ctx"),
        P("ctx", "tp"),
        P("ctx", "tp"),
        P("ctx", "tp"),
        P(),
        P(),
        P("tp", "ctx"),
        P("ctx"),
        P("ctx", None),
        P(None, "ctx", "tp"),
        P(None, "ctx", "tp"),
        P(None, "tp", "ctx"),
        token,
        token,
    )
    given = (
        token,
        token,
        P("ctx"),
        P("ctx", "tp"),
        P("ctx", "tp"),
        P("ctx", "tp"),
        P(),
        P(),
        P("tp", "ctx"),
        P("ctx"),
        P("ctx", None),
        P(None, "ctx", "tp"),
        P(None, "ctx", "tp"),
        P(None, "tp", "ctx"),
    )
    return jax.shard_map(
        per_device, mesh=mesh, in_specs=placed, out_specs=given, check_vma=False
    )
```
